32 devices in a mesh: batch: 2 (over core), ctx: 16 (over z, y, x).
Axes of the slice: x: 2, y: 2, z: 4, core: 2. Of those that a mesh axis runs over, the one named last changes fastest.
Arguments:
- inputs: bfloat16 [2, 2048, 512], P('batch', 'ctx'), may hold values from -6 to 6
- segments: int32 [2, 2048], P('batch'), may hold values from 0 to 4, as said below
- mixer_gain: bfloat16 [512], P(('batch', 'ctx')), may hold values from 0.5 to 1.5
- mixer_shift: bfloat16 [512], P(('batch', 'ctx')), may hold values from -2 to 2
- joint_weight: bfloat16 [512, 1536], P(('batch', 'ctx')), may hold values from -0.25 to 0.25
- offset_weight: bfloat16 [512, 512], P(('batch', 'ctx')), may hold values from -0.25 to 0.25
- content_bias: bfloat16 [512], P(('batch', 'ctx')), may hold values from -4 to 4
- offset_bias: bfloat16 [512], P(('batch', 'ctx')), may hold values from -4 to 4
- merge_weight: bfloat16 [512, 512], P(('batch', 'ctx')), may hold values from -3 to 3
- feed_gain: bfloat16 [512], P(('batch', 'ctx')), may hold values from 0.5 to 1.5
- feed_shift: bfloat16 [512], P(('batch', 'ctx')), may hold values from -2 to 2
- expand_weight: bfloat16 [512, 2048], P(('batch', 'ctx')), may hold values from -0.25 to 0.25
- expand_bias: bfloat16 [2048], P(('batch', 'ctx')), may hold values from -3 to 3
- reduce_weight: bfloat16 [2048, 512], P(('batch', 'ctx')), may hold values from -0.125 to 0.125
- reduce_bias: bfloat16 [512], P(('batch', 'ctx')), may hold values from -2 to 2
- cotangent: bfloat16 [2, 2048, 512], P('batch', 'ctx'), may hold values from -6 to 6
Outputs:
- result: bfloat16 [2, 2048, 512], P('batch', 'ctx')
- gradient: float32 [2, 2048, 512], P('batch', 'ctx')
- gain_mixer: float32 [512], P(('batch', 'ctx'))
- shift_mixer: float32 [512], P(('batch', 'ctx'))
- joint_grad: float32 [512, 1536], P(('batch', 'ctx'))
- offset_grad: float32 [512, 512], P(('batch', 'ctx'))
- content_grad: float32 [512], P(('batch', 'ctx'))
- bias_offset: float32 [512], P(('batch', 'ctx'))
- merge_grad: float32 [512, 512], P(('batch', 'ctx'))
- gain_feed: float32 [512], P(('batch', 'ctx'))
- shift_feed: float32 [512], P(('batch', 'ctx'))
- expand_grad: float32 [512, 2048], P(('batch', 'ctx'))
- bias_expand: float32 [2048], P(('batch', 'ctx'))
- reduce_grad: float32 [2048, 512], P(('batch', 'ctx'))
- bias_reduce: float32 [512], P(('batch', 'ctx'))
The draws below stay inside these ranges and needn't reach their ends.
Inputs may be any that keep to these rules, and one draw needn't show every extreme that they name: `segments`: in each row the numbers never fall, start at 0 and rise by one at each document bound; document 2 begins within the first 128 positions and ends within the last 128.
All inputs are finite; a program needn't handle non-finite values.
Results may differ from the reference program's by a relative error of at most 0.024.
Values may be sent and summed in bfloat16 or wider, within the bound.
A program may use at most 256 MiB of HBM per device.

```python
import math
import jax
import jax.numpy as jnp
from jax import lax

D = 512
HEADS = 8
HEAD = 64
FF = 2048
TOK_DEV = 128
SEQS = 2
SEQ_LEN = 2048


def draw_segments(key, part):
    rows = []
    for number in range(SEQS):
        inner = jax.random.fold_in(key, 41 + number)
        first_key, second_key, third_key, fourth_key = jax.random.split(inner, 4)
        begin = jax.random.randint(first_key, (), 2, TOK_DEV)
        early = jax.random.randint(second_key, (), 1, begin)
        tail = jax.random.randint(third_key, (), 2, TOK_DEV)
        finish = SEQ_LEN - tail
        late = finish + jax.random.randint(fourth_key, (), 1, tail)
        place = jnp.arange(SEQ_LEN, dtype=jnp.int32)
        ident = (place >= early).astype(jnp.int32) + (place >= begin).astype(jnp.int32) + (place >= finish).astype(jnp.int32) + (place >= late).astype(jnp.int32)
        rows.append(ident)
    return jnp.stack(rows).astype(jnp.int32)


def steps_of(own_key, dims, cuts, least, largest):
    level = 1.0
    for axis_at, blocks in cuts:
        heights = jax.random.uniform(jax.random.fold_in(jax.random.fold_in(own_key, 6), axis_at), (blocks,), jnp.float32, least / len(cuts), largest / len(cuts))
        level = level * jnp.repeat(jnp.exp(heights), dims[axis_at] // blocks).reshape((-1,) + (1,) * (len(dims) - 1 - axis_at))
    return level


def noise(rng, extent, scale, limit, cuts=(), kind=jnp.bfloat16):
    factor_of = steps_of(rng, extent, cuts, -0.22, 0.18) if cuts else 1.0
    result = jax.random.normal(rng, extent, jnp.float32) * scale * factor_of
    return jnp.minimum(jnp.maximum(result, -limit), limit).astype(kind)


def setup_inputs(seed: int = 0) -> dict:
    splits = jax.random.split(jax.random.key(seed), 17)
    inputs = noise(splits[0], (SEQS, SEQ_LEN, D), 1.0, 6.0, ((0, 2), (1, 16)))
    segments = draw_segments(jax.random.fold_in(splits[16], 71), 0)
    mixer_gain = jnp.clip(1.0 + 0.1 * jax.random.normal(splits[2], (D,), jnp.float32), 0.5, 1.5).astype(jnp.bfloat16)
    mixer_shift = noise(splits[3], (D,), 0.3, 2.0, ((0, 32),))
    joint_weight = noise(splits[4], (D, 3 * D), D ** -0.5, 0.25, ((0, 32),))
    offset_weight = noise(splits[5], (D, D), D ** -0.5, 0.25, ((0, 32),))
    content_bias = noise(splits[6], (D,), 1.0, 4.0, ((0, 32),))
    offset_bias = noise(splits[7], (D,), 1.0, 4.0, ((0, 32),))
    merge_weight = noise(splits[8], (D, D), 4 ** -0.5, 3.0, ((0, 32),))
    feed_gain = jnp.clip(1.0 + 0.1 * jax.random.normal(splits[9], (D,), jnp.float32), 0.5, 1.5).astype(jnp.bfloat16)
    feed_shift = noise(splits[10], (D,), 0.3, 2.0, ((0, 32),))
    expand_weight = noise(splits[11], (D, FF), D ** -0.5, 0.25, ((0, 32),))
    expand_bias = noise(splits[12], (FF,), 0.5, 3.0, ((0, 32),))
    reduce_weight = noise(splits[13], (FF, D), FF ** -0.5, 0.125, ((0, 32),))
    reduce_bias = noise(splits[14], (D,), 0.3, 2.0, ((0, 32),))
    cotangent = noise(splits[15], (SEQS, SEQ_LEN, D), 1.0, 6.0, ((0, 2), (1, 16)))
    return dict(inputs=inputs, segments=segments, mixer_gain=mixer_gain, mixer_shift=mixer_shift, joint_weight=joint_weight, offset_weight=offset_weight, content_bias=content_bias, offset_bias=offset_bias, merge_weight=merge_weight, feed_gain=feed_gain, feed_shift=feed_shift, expand_weight=expand_weight, expand_bias=expand_bias, reduce_weight=reduce_weight, reduce_bias=reduce_bias, cotangent=cotangent)


@jax.custom_vjp
def low(v):
    return lax.optimization_barrier(v.astype(jnp.bfloat16)).astype(jnp.float32)

@jax.custom_vjp
def low_back(v):
    return v

def low_keep(v):
    return (low(v), None)

def low_pass(kept, grad):
    return (grad,)

def back_keep(v):
    return (v, None)

def back_low(kept, grad):
    return (low(grad),)
low.defvjp(low_keep, low_pass)
low_back.defvjp(back_keep, back_low)
masked_score = -1e+30

def exact_dot(left, right):
    return jnp.dot(left, right, precision=lax.Precision.HIGHEST)

def layer_norm(values, gain, shift):
    center = values - lax.optimization_barrier(jnp.mean(values, axis=-1, keepdims=True))
    spread = lax.optimization_barrier(jnp.mean(center * center, axis=-1, keepdims=True))
    return center * lax.rsqrt(spread + 1e-05) * gain + shift

def sinusoid(first, count, width):
    half = width // 2
    freq = jnp.power(10000.0, -2.0 * jnp.arange(half, dtype=jnp.float32) / width)
    place = (first + jnp.arange(count, dtype=jnp.int32)).astype(jnp.float32)
    angle = place[:, None] * freq[None, :]
    return jnp.concatenate([jnp.sin(angle), jnp.cos(angle)], axis=1)

def attend_sequence(query_content_term, query_position_term, keys, values, seg_row, relative_offsets):
    block = 4 * TOK_DEV
    scale = 1.0 / math.sqrt(HEAD)
    key_pos = jnp.arange(SEQ_LEN, dtype=jnp.int32)

    def one_block(first):
        rows_content = lax.dynamic_slice_in_dim(query_content_term, first, block, 0)
        position_rows = lax.dynamic_slice_in_dim(query_position_term, first, block, 0)
        content = jnp.einsum('ahd,bhd->hab', rows_content, keys, precision=lax.Precision.HIGHEST)
        relative_scores = jnp.einsum('scx,icx->csi', position_rows, relative_offsets, precision=lax.Precision.HIGHEST)
        query_pos = first + jnp.arange(block, dtype=jnp.int32)
        distance = query_pos[:, None] - key_pos[None, :]
        index = jnp.clip(distance, 0, SEQ_LEN - 1).astype(jnp.int32)
        relative = jnp.take_along_axis(relative_scores, jnp.broadcast_to(index[None], relative_scores.shape), axis=2)
        scores = low_back(scale * (content + relative))
        query_seg = lax.dynamic_slice_in_dim(seg_row, first, block, 0)
        allowed = (distance >= 0) & (query_seg[:, None] == seg_row[None, :])
        masked = jnp.where(allowed[None], scores, masked_score)
        peak = lax.optimization_barrier(jnp.max(masked, axis=-1, keepdims=True))
        weights = jnp.where(allowed[None], jnp.exp(masked - peak), 0.0)
        probs = low(weights / lax.optimization_barrier(jnp.sum(weights, axis=-1, keepdims=True)))
        return jnp.einsum('hab,bhd->ahd', probs, values, precision=lax.Precision.HIGHEST)
    starts = (jnp.arange(SEQ_LEN // block, dtype=jnp.int32) * block).astype(jnp.int32)
    blocks = lax.map(jax.checkpoint(one_block), starts)
    return blocks.reshape(SEQ_LEN, HEADS, HEAD)

def reference(inputs, segments, mixer_gain, mixer_shift, joint_weight, offset_weight, content_bias, offset_bias, merge_weight, feed_gain, feed_shift, expand_weight, expand_bias, reduce_weight, reduce_bias, cotangent):
    params = tuple((item.astype(jnp.float32) for item in (mixer_gain, mixer_shift, joint_weight, offset_weight, content_bias, offset_bias, merge_weight, feed_gain, feed_shift, expand_weight, expand_bias, reduce_weight, reduce_bias)))

    def forward(source, weights):
        gain_one, shift_one, joint_matrix, offset_matrix, bias_content, bias_position, merge_matrix, gain_two, shift_two, expand_matrix, expand_vector, reduce_matrix, reduce_vector = weights
        tokens = source.reshape(SEQS * SEQ_LEN, D)
        normed = low(layer_norm(tokens, gain_one, shift_one))
        joint = low_back(exact_dot(normed, joint_matrix))
        query = joint[:, :D]
        keys = low(joint[:, D:2 * D])
        values = low(joint[:, 2 * D:])
        query_content_term = low(query + bias_content)
        query_position_term = low(query + bias_position)
        table = low(sinusoid(0, SEQ_LEN, D))
        relative_offsets = low(exact_dot(table, offset_matrix)).reshape(SEQ_LEN, HEADS, HEAD)
        shape_four = (SEQS, SEQ_LEN, HEADS, HEAD)

        def per_sequence(item):
            return attend_sequence(item[0], item[1], item[2], item[3], item[4], relative_offsets)
        mixed = lax.map(per_sequence, (query_content_term.reshape(shape_four), query_position_term.reshape(shape_four), keys.reshape(shape_four), values.reshape(shape_four), segments))
        attended = low(low_back(mixed.reshape(SEQS * SEQ_LEN, D)))
        branch = low_back(exact_dot(attended, merge_matrix))
        middle = tokens + branch
        second = low(layer_norm(middle, gain_two, shift_two))
        hidden = low_back(exact_dot(second, expand_matrix) + expand_vector)
        active = low(jax.nn.gelu(hidden, approximate=True))
        output = middle + exact_dot(active, reduce_matrix) + reduce_vector
        return output.reshape(SEQS, SEQ_LEN, D)
    output, pullback = jax.vjp(forward, inputs.astype(jnp.float32), params)
    grad_input, grads = pullback(cotangent.astype(jnp.float32))
    return (output.astype(jnp.bfloat16), grad_input, grads[0], grads[1], grads[2], grads[3], grads[4], grads[5], grads[6], grads[7], grads[8], grads[9], grads[10], grads[11], grads[12])
```

```python
import functools
import math

import jax
import jax.numpy as jnp
import ml_dtypes
import numpy as np
from jax import lax
from jax.experimental import pallas as pl
from jax.experimental.pallas import tpu as pltpu
from jax.sharding import PartitionSpec as P

HEADS = 8
HEAD = 64


masked_score = -1e30


def shifted(array, axis, by):
    peers = lax.axis_size(axis)
    pairs = [(i, i + by) for i in range(peers) if 0 <= i + by < peers]
    return lax.ppermute(array, axis, pairs)


def shifted_2(value, axis, steps):
    count = lax.axis_size(axis)
    pairs = [(source, (source + steps) % count) for source in range(count)]
    return lax.ppermute(value, axis, pairs)


def layer_norm(values, gain, shift):
    center = values - jnp.mean(values, axis=-1, keepdims=True)
    spread = jnp.mean(center * center, axis=-1, keepdims=True)
    return center * lax.rsqrt(spread + 1e-05) * gain + shift


def sinusoid(first, count, width):
    half = width // 2
    freq = jnp.power(10000.0, -2.0 * jnp.arange(half, dtype=jnp.float32) / width)
    place = (first + jnp.arange(count, dtype=jnp.int32)).astype(jnp.float32)
    angle = place[:, None] * freq[None, :]
    return jnp.concatenate([jnp.sin(angle), jnp.cos(angle)], axis=1)


def contract_rows(left, right):
    return lax.dot_general(
        left, right, (((0,), (0,)), ((), ())), preferred_element_type=jnp.float32
    )


def contract_cols(left, right):
    return lax.dot_general(
        left, right, (((1,), (1,)), ((), ())), preferred_element_type=jnp.float32
    )


def split_contract(table, grad_rows):
    upper = grad_rows.astype(jnp.bfloat16)
    lower = (grad_rows - upper.astype(jnp.float32)).astype(jnp.bfloat16)
    return contract_rows(table, upper) + contract_rows(table, lower)


def fold_blocks(step, carry, pieces, limit):
    count = pieces[0].shape[0]
    size = min(count, limit)
    number = count // size
    stacked = tuple((item.reshape((number, size) + item.shape[1:]) for item in pieces))

    def inner(state, item):
        offset, parts = item
        return (step(state, parts, offset * size), None)

    folded, _ = lax.scan(inner, carry, (jnp.arange(number, dtype=jnp.int32), stacked))
    return folded


def realign(relative_scores, count):
    heads, rows, width = relative_scores.shape
    flat = relative_scores.reshape(heads, rows * width)
    band = flat[:, rows - 1 : rows - 1 + rows * (width - 1)]
    return band.reshape(heads, rows, width - 1)[:, :, :count]


def pair_terms(
    query_content_term, query_position_term, keys, query_first, key_first, seg_row, offsets_pad
):
    rows, heads, size = query_content_term.shape
    count = keys.shape[0]
    length = offsets_pad.shape[0] // 2
    anchor = query_first - key_first - count + length
    attention_span = lax.dynamic_slice_in_dim(offsets_pad, anchor, rows + count, 0)[::-1].reshape(
        rows + count, heads, size
    )
    content = jnp.einsum(
        "ahd,bhd->hab", query_content_term, keys, preferred_element_type=jnp.float32
    )
    relative_scores = jnp.einsum(
        "scx,icx->csi", query_position_term, attention_span, preferred_element_type=jnp.float32
    )
    scores = (content + realign(relative_scores, count)) * (1.0 / math.sqrt(size))
    query_seg = lax.dynamic_slice_in_dim(seg_row, query_first, rows, 0)
    key_seg = lax.dynamic_slice_in_dim(seg_row, key_first, count, 0)
    query_pos = query_first + jnp.arange(rows, dtype=jnp.int32)
    key_pos = key_first + jnp.arange(count, dtype=jnp.int32)
    allowed = (key_pos[None, :] <= query_pos[:, None]) & (key_seg[None, :] == query_seg[:, None])
    return (scores, allowed, attention_span, anchor)


def pair_grads(
    query_content_term,
    query_position_term,
    keys,
    values,
    query_first,
    key_first,
    seg_row,
    offsets_pad,
    logsum,
    spread,
    grad_attended,
):
    rows, heads, size = query_content_term.shape
    count = keys.shape[0]
    scale = 1.0 / math.sqrt(size)
    scores, allowed, attention_span, anchor = pair_terms(
        query_content_term, query_position_term, keys, query_first, key_first, seg_row, offsets_pad
    )
    probs = jnp.where(allowed[None], jnp.exp(scores - logsum[..., None]), 0.0)
    grad_values = jnp.einsum(
        "hab,ahd->bhd",
        probs.astype(jnp.bfloat16),
        grad_attended,
        preferred_element_type=jnp.float32,
    )
    grad_probs = jnp.einsum(
        "ahd,bhd->hab", grad_attended, values, preferred_element_type=jnp.float32
    )
    grad_scores = (probs * (grad_probs - spread[..., None])).astype(jnp.bfloat16)
    grad_content = scale * jnp.einsum(
        "hab,bhd->ahd", grad_scores, keys, preferred_element_type=jnp.float32
    )
    grad_keys = scale * jnp.einsum(
        "hab,ahd->bhd", grad_scores, query_content_term, preferred_element_type=jnp.float32
    )
    blank = jnp.zeros((heads, rows, rows + count), jnp.float32)
    _, realign_back = jax.vjp(lambda relative_scores: realign(relative_scores, count), blank)
    gradient_relative_scores = realign_back(grad_scores.astype(jnp.float32))[0].astype(jnp.bfloat16)
    grad_offset = scale * jnp.einsum(
        "nsk,kno->sno", gradient_relative_scores, attention_span, preferred_element_type=jnp.float32
    )
    grad_window = scale * jnp.einsum(
        "cqu,qcn->ucn",
        gradient_relative_scores,
        query_position_term,
        preferred_element_type=jnp.float32,
    )
    grad_window = grad_window.reshape(rows + count, heads * size)[::-1]
    return (grad_content, grad_offset, grad_keys, grad_values, grad_window, anchor)


def add_window(grad_rows, grad_window, anchor):
    current = lax.dynamic_slice_in_dim(grad_rows, anchor, grad_window.shape[0], 0)
    return lax.dynamic_update_slice_in_dim(grad_rows, current + grad_window, anchor, 0)


def local(
    inputs,
    segments,
    mixer_gain,
    mixer_shift,
    joint_weight,
    offset_weight,
    content_bias,
    offset_bias,
    merge_weight,
    feed_gain,
    feed_shift,
    expand_weight,
    expand_bias,
    reduce_weight,
    reduce_bias,
    cotangent,
):
    (
        first_gain,
        first_shift,
        joint_matrix,
        offset_matrix,
        bias_content,
        bias_position,
        merge_matrix,
    ) = (
        lax.all_gather(mixer_gain, ("batch", "ctx"), axis=0, tiled=True),
        lax.all_gather(mixer_shift, ("batch", "ctx"), axis=0, tiled=True),
        lax.all_gather(joint_weight, ("batch", "ctx"), axis=0, tiled=True),
        lax.all_gather(offset_weight, ("batch", "ctx"), axis=0, tiled=True),
        lax.all_gather(content_bias, ("batch", "ctx"), axis=0, tiled=True),
        lax.all_gather(offset_bias, ("batch", "ctx"), axis=0, tiled=True),
        lax.all_gather(merge_weight, ("batch", "ctx"), axis=0, tiled=True),
    )
    tokens = inputs[0].astype(jnp.float32)
    rows, width = tokens.shape
    seg_row = segments[0]
    length = seg_row.shape[0]
    place = lax.axis_index("ctx")
    cycle = lax.axis_size("ctx")
    block_first = place * rows
    heads_shape = (rows, HEADS, HEAD)
    gain_one = first_gain.astype(jnp.float32)
    shift_one = first_shift.astype(jnp.float32)
    normed = layer_norm(tokens, gain_one, shift_one)
    normed_low = normed.astype(jnp.bfloat16)
    joint = jnp.dot(normed_low, joint_matrix, preferred_element_type=jnp.float32)
    query = joint[:, :width]
    keys = joint[:, width : 2 * width].astype(jnp.bfloat16).reshape(heads_shape)
    values = joint[:, 2 * width :].astype(jnp.bfloat16).reshape(heads_shape)
    query_content_term = (
        (query + bias_content.astype(jnp.float32)).astype(jnp.bfloat16).reshape(heads_shape)
    )
    query_position_term = (
        (query + bias_position.astype(jnp.float32)).astype(jnp.bfloat16).reshape(heads_shape)
    )
    everyone = lax.axis_size(("batch", "ctx"))
    share = length // everyone
    table = sinusoid(lax.axis_index(("batch", "ctx")) * share, share, width).astype(jnp.bfloat16)
    offsets_local = jnp.dot(table, offset_matrix, preferred_element_type=jnp.float32).astype(
        jnp.bfloat16
    )
    offsets_all = lax.all_gather(offsets_local, ("batch", "ctx"), axis=0, tiled=True)
    offsets_pad = jnp.concatenate([jnp.zeros_like(offsets_all), offsets_all], axis=0)

    def stats_block(carry, pieces, start):
        peak, total = carry
        scores, allowed, attention_span, anchor = pair_terms(
            query_content_term,
            query_position_term,
            pieces[0],
            block_first,
            start,
            seg_row,
            offsets_pad,
        )
        masked = jnp.where(allowed[None], scores, masked_score)
        new_peak = jnp.maximum(peak, jnp.max(masked, axis=-1))
        added = jnp.sum(
            jnp.where(allowed[None], jnp.exp(masked - new_peak[..., None]), 0.0), axis=-1
        )
        return (new_peak, total * jnp.exp(peak - new_peak) + added)

    peak_start = jnp.full((HEADS, rows), masked_score, jnp.float32)
    total_start = jnp.zeros((HEADS, rows), jnp.float32)
    peak, total = fold_blocks(
        stats_block,
        (peak_start, total_start),
        (lax.all_gather(keys, "ctx", axis=0, tiled=True),),
        rows,
    )
    logsum = peak + jnp.log(total)

    def output_block(carry, pieces, start):
        scores, allowed, attention_span, anchor = pair_terms(
            query_content_term,
            query_position_term,
            pieces[0],
            block_first,
            start,
            seg_row,
            offsets_pad,
        )
        probs = jnp.where(allowed[None], jnp.exp(scores - logsum[..., None]), 0.0).astype(
            jnp.bfloat16
        )
        return carry + jnp.einsum(
            "hab,bhd->ahd", probs, pieces[1], preferred_element_type=jnp.float32
        )

    mixed = fold_blocks(
        output_block,
        jnp.zeros(heads_shape, jnp.float32),
        (
            lax.all_gather(keys, "ctx", axis=0, tiled=True),
            lax.all_gather(values, "ctx", axis=0, tiled=True),
        ),
        rows,
    )
    attended_low = mixed.reshape(rows, width).astype(jnp.bfloat16)
    middle = tokens + jnp.dot(attended_low, merge_matrix, preferred_element_type=jnp.float32)
    second_gain, second_shift, expand_matrix, expand_vector, reduce_matrix, reduce_vector = (
        lax.all_gather(feed_gain, ("batch", "ctx"), axis=0, tiled=True),
        lax.all_gather(feed_shift, ("batch", "ctx"), axis=0, tiled=True),
        lax.all_gather(expand_weight, ("batch", "ctx"), axis=0, tiled=True),
        lax.all_gather(expand_bias, ("batch", "ctx"), axis=0, tiled=True),
        lax.all_gather(reduce_weight, ("batch", "ctx"), axis=0, tiled=True),
        lax.all_gather(reduce_bias, ("batch", "ctx"), axis=0, tiled=True),
    )
    gain_two = second_gain.astype(jnp.float32)
    shift_two = second_shift.astype(jnp.float32)
    second_low = layer_norm(middle, gain_two, shift_two).astype(jnp.bfloat16)
    hidden = jnp.dot(
        second_low, expand_matrix, preferred_element_type=jnp.float32
    ) + expand_vector.astype(jnp.float32)
    active_low = jax.nn.gelu(hidden, approximate=True).astype(jnp.bfloat16)
    output = (
        middle
        + jnp.dot(active_low, reduce_matrix, preferred_element_type=jnp.float32)
        + reduce_vector.astype(jnp.float32)
    )
    result = output.astype(jnp.bfloat16)[None]
    grad_out = cotangent[0]
    grad_outf = grad_out.astype(jnp.float32)
    grad_reduce_bias = jnp.sum(grad_outf, axis=0)
    grad_reduce = contract_rows(active_low, grad_out)
    grad_active = contract_cols(grad_out, reduce_matrix)
    _, gelu_back = jax.vjp(lambda value: jax.nn.gelu(value, approximate=True), hidden)
    grad_hidden = gelu_back(grad_active)[0].astype(jnp.bfloat16)
    grad_expand_bias = jnp.sum(grad_hidden.astype(jnp.float32), axis=0)
    grad_expand = contract_rows(second_low, grad_hidden)
    grad_second = contract_cols(grad_hidden, expand_matrix)
    _, second_back = jax.vjp(layer_norm, middle, gain_two, shift_two)
    grad_mid, grad_gain_two, grad_shift_two = second_back(grad_second)
    grad_middle = grad_outf + grad_mid
    feed_sums = (
        lax.psum_scatter(grad_gain_two, ("batch", "ctx"), scatter_dimension=0, tiled=True),
        lax.psum_scatter(grad_shift_two, ("batch", "ctx"), scatter_dimension=0, tiled=True),
        lax.psum_scatter(grad_expand, ("batch", "ctx"), scatter_dimension=0, tiled=True),
        lax.psum_scatter(grad_expand_bias, ("batch", "ctx"), scatter_dimension=0, tiled=True),
        lax.psum_scatter(grad_reduce, ("batch", "ctx"), scatter_dimension=0, tiled=True),
        lax.psum_scatter(grad_reduce_bias, ("batch", "ctx"), scatter_dimension=0, tiled=True),
    )
    middle_low = grad_middle.astype(jnp.bfloat16)
    grad_merge = contract_rows(attended_low, middle_low)
    grad_attended = (
        contract_cols(middle_low, merge_matrix).astype(jnp.bfloat16).reshape(heads_shape)
    )
    spread = jnp.einsum("ahd,ahd->ha", grad_attended.astype(jnp.float32), mixed)
    zero_heads = jnp.zeros(heads_shape, jnp.float32)
    zero_rows = jnp.zeros((2 * length, width), jnp.float32)

    def cycle_step(turn, carry):
        visiting, carried, grad_content, grad_offset, grad_rows = carry
        owner = (place - turn) % cycle
        terms = pair_grads(
            query_content_term,
            query_position_term,
            visiting[0],
            visiting[1],
            block_first,
            owner * rows,
            seg_row,
            offsets_pad,
            logsum,
            spread,
            grad_attended,
        )
        carried = carried + jnp.stack([terms[2], terms[3]])
        grad_rows = add_window(grad_rows, terms[4], terms[5])
        visiting = shifted(visiting, "ctx", 1)
        carried = shifted_2(carried.astype(jnp.bfloat16), "ctx", 1).astype(carried.dtype)
        return (visiting, carried, grad_content + terms[0], grad_offset + terms[1], grad_rows)

    start_state = (
        jnp.stack([keys, values]),
        jnp.zeros((2,) + heads_shape, jnp.float32),
        zero_heads,
        zero_heads,
        zero_rows,
    )
    _, carried, grad_content, grad_offset, grad_rows = lax.fori_loop(
        0, cycle, cycle_step, start_state
    )
    grad_keys = carried[0]
    grad_values = carried[1]
    grad_content_bias = jnp.sum(grad_content, axis=0).reshape(width)
    gradient_position_bias = jnp.sum(grad_offset, axis=0).reshape(width)
    grad_joint = jnp.concatenate(
        [
            (grad_content + grad_offset).reshape(rows, width),
            grad_keys.reshape(rows, width),
            grad_values.reshape(rows, width),
        ],
        axis=1,
    ).astype(jnp.bfloat16)
    grad_joint_matrix = contract_rows(normed_low, grad_joint)
    grad_normed = contract_cols(grad_joint, joint_matrix)
    _, first_back = jax.vjp(layer_norm, tokens, gain_one, shift_one)
    grad_tokens, grad_gain_one, grad_shift_one = first_back(grad_normed)
    gradient = (grad_middle + grad_tokens)[None]
    full_table = sinusoid(0, length, width).astype(jnp.bfloat16)
    grad_offset_matrix = split_contract(full_table, grad_rows[length:])
    mixer_sums = (
        lax.psum_scatter(grad_gain_one, ("batch", "ctx"), scatter_dimension=0, tiled=True),
        lax.psum_scatter(grad_shift_one, ("batch", "ctx"), scatter_dimension=0, tiled=True),
        lax.psum_scatter(grad_joint_matrix, ("batch", "ctx"), scatter_dimension=0, tiled=True),
        lax.psum_scatter(grad_offset_matrix, ("batch", "ctx"), scatter_dimension=0, tiled=True),
        lax.psum_scatter(grad_content_bias, ("batch", "ctx"), scatter_dimension=0, tiled=True),
        lax.psum_scatter(gradient_position_bias, ("batch", "ctx"), scatter_dimension=0, tiled=True),
        lax.psum_scatter(grad_merge, ("batch", "ctx"), scatter_dimension=0, tiled=True),
    )
    return (
        result,
        gradient,
        mixer_sums[0],
        mixer_sums[1],
        mixer_sums[2],
        mixer_sums[3],
        mixer_sums[4],
        mixer_sums[5],
        mixer_sums[6],
        feed_sums[0],
        feed_sums[1],
        feed_sums[2],
        feed_sums[3],
        feed_sums[4],
        feed_sums[5],
    )


F32, BF16 = jnp.float32, jnp.bfloat16
MESH = pl.DeviceIdType.MESH
NEG = -1e30
ZS, YS, SS = 4, 2, 2


def dot(a, b, dims=((1,), (0,)), precision=None):
    return lax.dot_general(a, b, (dims, ((), ())), preferred_element_type=F32, precision=precision)


def dot_nt(a, b):
    return dot(a, b, ((1,), (1,)))


def dot_tn(a, b):
    return dot(a, b, ((0,), (0,)))


def iota(shape, axis):
    return lax.broadcasted_iota(jnp.int32, shape, axis)


def wide(tiles):
    return jnp.concatenate(tiles, axis=1)


def tall(tiles):
    return jnp.concatenate(tiles, axis=0)


def fold(x):
    half = x.shape[0] // 2
    return wide([x[:half], x[half:]])


def unfold(x):
    return tall([x[:, :HEAD], x[:, HEAD:]])


def normalize(x):
    center = x - jnp.mean(x, axis=-1, keepdims=True)
    inverse = lax.rsqrt(jnp.mean(center * center, axis=-1, keepdims=True) + 1e-05)
    return center * inverse, inverse


def norm_back(e, n, inverse):
    return inverse * (e - jnp.mean(e, axis=-1, keepdims=True) - n * jnp.mean(e * n, axis=-1, keepdims=True))


def colsum(x):
    return jnp.sum(x, axis=0, keepdims=True)


class Wires:
    def __init__(self, sends, recvs):
        self.sends, self.recvs, self.sent, self.received, self.pending = sends, recvs, 0, 0, []

    def slots(self, count):
        first = self.received
        self.received += count
        return first

    def copy(self, src, dst, slot, to, when=None):
        made = pltpu.make_async_remote_copy(
            src_ref=src,
            dst_ref=dst,
            send_sem=self.sends.at[self.sent],
            recv_sem=self.recvs.at[slot],
            device_id=to,
            device_id_type=MESH,
        )
        self.sent += 1
        self.pending.append((made, when))
        if when is None:
            made.start()
        else:
            pl.when(when)(made.start)

    def arrived(self, dst, slot, to):
        pltpu.make_async_remote_copy(
            src_ref=dst,
            dst_ref=dst,
            send_sem=self.sends.at[0],
            recv_sem=self.recvs.at[slot],
            device_id=to,
            device_id_type=MESH,
        ).wait_recv()

    def finish(self):
        for made, when in self.pending:
            if when is None:
                made.wait_send()
            else:
                pl.when(when)(made.wait_send)


def layer_kernel(
    n,
    x_ref,
    seg_ref,
    vec_ref,
    jw_ref,
    ow_ref,
    mw_ref,
    ew_ref,
    rw_ref,
    g_ref,
    table_ref,
    result_ref,
    gradient_ref,
    jg_ref,
    og_ref,
    mg_ref,
    eg_ref,
    rg_ref,
    vg_ref,
    TAB,
    TOK,
    NRM,
    W1S,
    W1,
    JW,
    MW,
    EW,
    RW,
    KV,
    QC,
    QO,
    OFF,
    SCR,
    PST,
    ATF,
    LIN,
    ATS,
    ATR,
    ACT,
    GH,
    GAS,
    GAR,
    DKVT,
    DROWT,
    DKVS,
    DKVR,
    DKVF,
    DQF,
    RKV,
    RDQ,
    MG,
    EG,
    RG,
    CM,
    CE,
    CR,
    AM2,
    BM2,
    AE2,
    BE2,
    AR2,
    BR2,
    AM3,
    BM3,
    AE3,
    BE3,
    AR3,
    BR3,
    ZM,
    ZE,
    ZR,
    JGA,
    JGM,
    JR1,
    JF,
    JR2,
    table_sem,
    sends,
    recvs,
):
    T = x_ref.shape[1]
    D = x_ref.shape[2]
    FF = ew_ref.shape[1]
    r = jw_ref.shape[0]
    b = lax.axis_index("batch")
    c = lax.axis_index("ctx")
    h, s = c // SS, c % SS
    z, y = h // YS, h % YS
    shard = b * n + c

    def dev(b_, h_, s_):
        return {"batch": b_, "ctx": h_ * SS + s_}

    core = dev(1 - b, h, s)
    side = dev(b, h, 1 - s)
    flip_y = dev(b, h ^ 1, s)
    heads = [(q, h ^ q) for q in range(1, HEADS)]
    group = [(1 - b, s), (b, 1 - s), (1 - b, 1 - s)]
    wires = Wires(sends, recvs)

    barrier = pltpu.get_barrier_semaphore()
    for _, peer in heads:
        pl.semaphore_signal(barrier, inc=1, device_id=dev(b, peer, s), device_id_type=MESH)
    for b_, s_ in group:
        pl.semaphore_signal(barrier, inc=1, device_id=dev(b_, h, s_), device_id_type=MESH)

    table_copy = pltpu.make_async_copy(table_ref, TAB, table_sem)
    table_copy.start()

    vec = vec_ref[...].astype(F32)
    by_16 = pltpu.roll(vec, (shard % 8) * 16, 1)
    by_64 = pltpu.roll(vec, (shard % 2) * 64, 1)
    vec = jnp.where(iota(vec.shape, 0) == 7, by_64, by_16).astype(BF16)
    jw, ow = jw_ref[...], ow_ref[...]
    for k in range(HEADS):
        at = k * HEAD
        W1S[k] = wide(
            [
                jw[:, D + at : D + at + HEAD],
                jw[:, 2 * D + at : 2 * D + at + HEAD],
                jw[:, at : at + HEAD],
                ow[:, at : at + HEAD],
                vec,
            ]
        )
    TOK[h] = x_ref[0]
    W1[b, h, s] = W1S[h]
    pl.semaphore_wait(barrier, len(heads) + len(group))

    tok_slot = wires.slots(HEADS)
    for dz in range(1, ZS):
        wires.copy(x_ref.at[0], TOK.at[h], tok_slot + h, dev(b, h ^ (2 * dz), s))
    w1_slot = wires.slots(HEADS)
    for _, peer in heads:
        wires.copy(W1S.at[peer], W1.at[b, h, s], w1_slot + h, dev(b, peer, s))
    wires.copy(x_ref.at[0], TOK.at[h], tok_slot + h, flip_y)

    def gather(W, ref, cols):
        rows = ref.shape[0]
        half = cols // 2
        lo, hi = pl.ds(0, half), pl.ds(half, half)
        slot = wires.slots(4 + 2 + 2 + 1)

        def start():
            W[b, z, y, s] = ref[...]
            for dz in range(1, ZS):
                wires.copy(ref, W.at[b, z, y, s], slot + z, dev(b, h ^ (2 * dz), s))

        def second():
            for dz in range(1, ZS):
                wires.arrived(W.at[b, z ^ dz, y, s], slot + (z ^ dz), side)
            wires.copy(W.at[b, :, y, s, :, lo], W.at[b, :, y, s, :, lo], slot + 4, flip_y)
            wires.copy(W.at[b, :, y, s, :, hi], W.at[b, :, y, s, :, hi], slot + 5, side)

        def third():
            wires.arrived(W.at[b, :, 1 - y, s, :, lo], slot + 4, flip_y)
            wires.copy(W.at[b, :, :, s, :, lo], W.at[b, :, :, s, :, lo], slot + 6, side)
            wires.arrived(W.at[b, :, y, 1 - s, :, hi], slot + 5, side)
            wires.copy(W.at[b, :, y, :, :, hi], W.at[b, :, y, :, :, hi], slot + 7, flip_y)

        def fourth():
            wires.arrived(W.at[b, :, :, 1 - s, :, lo], slot + 6, side)
            wires.arrived(W.at[b, :, 1 - y, :, :, hi], slot + 7, flip_y)
            wires.copy(W.at[b], W.at[b], slot + 8, core)

        def fifth():
            wires.arrived(W.at[1 - b], slot + 8, core)

        return start, second, third, fourth, fifth

    gm, gr = gather(MW, mw_ref, D), gather(RW, rw_ref, D)
    ge, gj = gather(EW, ew_ref, FF), gather(JW, jw_ref, 3 * D)

    for _, peer in heads:
        wires.arrived(W1.at[b, peer, s], w1_slot + peer, side)
    w1_group = wires.slots(4)
    for b_, s_ in group:
        wires.copy(W1.at[b, :, s], W1.at[b, :, s], w1_group + b * 2 + s, dev(b_, h, s_))
    gm[0]()
    gr[0]()
    ge[0]()
    gj[0]()
    for b_, s_ in group:
        wires.arrived(W1.at[b_, :, s_], w1_group + b_ * 2 + s_, core)

    vecs = W1[:, :, :, :, 256:384].reshape(2 * n, r, 128).astype(F32)
    rows = wide([jnp.sum(vecs[8 * t : 8 * t + 8], axis=0) for t in range(D // 128)])
    gain_one, shift_one, bias_c, bias_o = rows[0:1], rows[1:2], rows[2:3], rows[3:4]
    gain_two, shift_two, reduce_bias = rows[4:5], rows[5:6], rows[6:7]
    expand_bias = wide([vecs[2 * t] + vecs[2 * t + 1] for t in range(FF // 128)])[7:8]
    lane = iota((1, 128), 1)
    low_lane = lane < HEAD

    def own_head(row):
        pairs = jnp.zeros((1, 128), F32)
        for t in range(HEADS // 2):
            pairs = pairs + jnp.where(h // 2 == t, row[:, 128 * t : 128 * t + 128], 0.0)
        turned = pltpu.roll(pairs, HEAD, 1)
        return jnp.where(h % 2 == 0, pairs, turned)

    bias_c, bias_o = own_head(bias_c), own_head(bias_o)

    own_w = W1[:, :, :, :, 0:256].reshape(D, 256)
    kv_slot = wires.slots(HEADS)

    def project(k):
        normed, _ = normalize(TOK[k].astype(F32))
        normed = (normed * gain_one + shift_one).astype(BF16)
        NRM[k] = normed
        out = dot(normed, own_w)
        KV[k * SS + s] = out[:, :128].astype(BF16)
        wires.copy(KV.at[k * SS + s], KV.at[k * SS + s], kv_slot + k, side)
        query = out[:, 128:]
        QC[k] = jnp.where(low_lane, (query + bias_c).astype(BF16).astype(F32) * 0.125, 0.0).astype(BF16)
        second = (query + bias_o).astype(BF16).astype(F32) * 0.125
        QO[k] = pltpu.roll(jnp.where(low_lane, second, 0.0), HEAD, 1).astype(BF16)

    for dz in range(ZS):
        near, far = h ^ (2 * dz), h ^ (2 * dz + 1)
        if dz > 0:
            wires.arrived(TOK.at[near], tok_slot + near, side)
            wires.copy(TOK.at[near], TOK.at[near], tok_slot + near, flip_y)
    table_copy.wait()
    tiles = TAB.shape[0] // T
    off_w = own_w[:, 128:]

    def offset_tile(t, carry):
        start = pl.multiple_of(t * T, T)
        OFF[t] = dot(TAB[pl.ds(start, T), :], off_w).astype(BF16)
        return carry

    lax.fori_loop(0, tiles, offset_tile, 0)
    for t in range(4):
        OFF[tiles + t] = jnp.zeros((T, 128), BF16)
    project(h)
    for dz in range(1, ZS):
        project(h ^ (2 * dz))
    gm[1]()
    for dz in range(ZS):
        far = h ^ (2 * dz + 1)
        wires.arrived(TOK.at[far], tok_slot + far, side)
        project(far)
    gr[1]()
    ge[1]()

    tril = iota((T, T), 1) <= iota((T, T), 0)
    diff = iota((T, T), 1) - iota((T, T), 0)
    eye = iota((T, T), 1) == iota((T, T), 0)
    flip = jnp.where(iota((T, T), 0) + iota((T, T), 1) == T - 1, 1.0, 0.0).astype(BF16)
    att_slot = wires.slots(HEADS)

    def forward(k):
        block = k * SS + s
        base = n - 1 - block
        trips = (k * SS + SS + 3) // 4
        qc, qo = QC[k], QO[k]
        seg_row = seg_ref[0:1, pl.ds(pl.multiple_of(block * T, T), T)].astype(F32)
        seg_q = jnp.sum(jnp.where(eye, seg_row, 0.0), axis=1, keepdims=True)
        peak = jnp.full((T, T), NEG, F32)
        for ch in range(trips):
            first = ch * 4
            kv = KV[first : first + 4].reshape(4 * T, 128)
            content = dot_nt(qc, kv)
            window = OFF[pl.ds(base + first, 5)].reshape(5 * T, 128)
            rel = dot_nt(qo, window)
            turned = [pltpu.roll(rel[:, t * T : (t + 1) * T], 1, 1, stride=1, stride_axis=0) for t in range(5)]
            for t in range(4):
                seg_k = seg_ref[0:1, (first + t) * T : (first + t + 1) * T].astype(F32)
                ok = (diff <= (block - first - t) * T) & (seg_k == seg_q)
                score = content[:, t * T : (t + 1) * T] + jnp.where(tril, turned[t], turned[t + 1])
                score = jnp.where(ok, score, NEG)
                SCR[first + t] = score
                peak = jnp.maximum(peak, score)
        peak = jnp.max(peak, axis=1, keepdims=True)
        total, out = jnp.zeros((T, T), F32), jnp.zeros((T, 128), F32)
        for ch in range(trips):
            first = ch * 4
            kv = KV[first : first + 4].reshape(4 * T, 128)
            low = []
            for t in range(4):
                p = jnp.exp(SCR[first + t] - peak)
                total = total + p
                low.append(p.astype(BF16))
            low = wide(low)
            out = out + dot(low, kv)
            turned = dot(flip, low).astype(BF16)
            for t in range(4):
                PST[k, first + t] = turned[:, t * T : (t + 1) * T]
        inverse = 1.0 / jnp.sum(total, axis=1, keepdims=True)
        att = out[:, HEAD:] * inverse
        ATF[k] = att
        LIN[k] = jnp.broadcast_to(inverse, (T, T))
        ATS[k] = fold(att).astype(BF16)
        wires.copy(ATS.at[k], ATR.at[h], att_slot + h, dev(b, k, s), when=h != k)

    schedule = {
        0: [gm[2]],
        1: [gj[1]],
        2: [gr[2]],
        3: [gm[3]],
        4: [ge[2]],
        5: [gr[3]],
        6: [gj[2]],
        7: [ge[3]],
    }
    for k in range(HEADS):
        if k % 2 == 0:
            for m in (k, k + 1):
                wires.arrived(KV.at[m * SS + 1 - s], kv_slot + m, side)
        forward(k)
        for step in schedule[k]:
            step()
    ATR[h] = ATS[h]
    gm[4]()
    gr[4]()
    ge[4]()
    gj[3]()
    for _, peer in heads:
        wires.arrived(ATR.at[peer], att_slot + peer, side)

    def by_heads(R):
        return wide([unfold(R[k].astype(F32)) for k in range(HEADS)]).astype(BF16)

    att_low = by_heads(ATR)
    x = x_ref[0].astype(F32)
    middle = x + dot(att_low, MW[...].reshape(D, D))
    n_two, inverse_two = normalize(middle)
    second_low = (n_two * gain_two + shift_two).astype(BF16)
    g_low = g_ref[0]
    g = g_low.astype(F32)
    output = middle + reduce_bias
    grad_second = jnp.zeros((T, D), F32)
    bias_expand = []
    step = min(512, FF)
    root, cube = math.sqrt(2.0 / math.pi), 0.044715
    per = 2 * n * step // FF
    for f in range(FF // step):
        cols = slice(f * step, f * step + step)
        e_w = EW[:, :, :, :, :, cols].reshape(D, step)
        r_w = RW[...].reshape(FF, D)[cols]
        v = dot(second_low, e_w) + expand_bias[:, cols]
        tanh = jnp.tanh(root * (v + cube * v * v * v))
        active = (0.5 * v * (1.0 + tanh)).astype(BF16)
        ACT[:, cols] = active
        output = output + dot(active, r_w)
        slope = 0.5 * (1.0 + tanh) + 0.5 * v * (1.0 - tanh * tanh) * (root * (1.0 + 3.0 * cube * v * v))
        grad_hidden = (dot_nt(g_low, r_w) * slope).astype(BF16)
        GH[:, cols] = grad_hidden
        bias_expand.append(colsum(grad_hidden.astype(F32)))
        grad_second = grad_second + dot_nt(grad_hidden, e_w)
    result_ref[0] = output.astype(BF16)
    grad_middle = g + norm_back(grad_second * gain_two, n_two, inverse_two)
    middle_low = grad_middle.astype(BF16)
    gradient_ref[0] = grad_middle
    grad_att = dot_nt(middle_low, MW[...].reshape(D, D))
    ga_slot = wires.slots(HEADS)
    for k in range(HEADS):
        GAS[k] = fold(grad_att[:, k * HEAD : (k + 1) * HEAD]).astype(BF16)
    for _, peer in heads:
        wires.copy(GAS.at[peer], GAR.at[h], ga_slot + h, dev(b, peer, s))
    GAR[h] = GAS[h]
    vec_feed = [colsum(grad_second * n_two), colsum(grad_second), colsum(g)]
    bias_expand = wide(bias_expand)

    def scatter(W, C, A2, B2, A3, B3, ZR_, out_ref):
        rows, cols = W.shape[4], W.shape[5]
        half = cols // 2
        lo, hi = pl.ds(0, half), pl.ds(half, half)
        slot = wires.slots(1 + 2 + 2 + 4)

        def first():
            wires.copy(W.at[1 - b], C, slot, core)

        def second():
            wires.arrived(C, slot, core)

            def add(i, carry):
                i0, i1 = i // YS, i % YS
                for i2 in range(SS):
                    W[b, i0, i1, i2] = (W[b, i0, i1, i2].astype(F32) + C[i0, i1, i2].astype(F32)).astype(BF16)
                return carry

            lax.fori_loop(0, ZS * YS, add, 0)
            wires.copy(W.at[b, :, :, 1 - s, :, lo], A2, slot + 1, side)
            wires.copy(W.at[b, :, 1 - y, :, :, hi], B2, slot + 2, flip_y)

        def third():
            wires.arrived(A2, slot + 1, side)

            def add_a(i, carry):
                for j in range(YS):
                    W[b, i, j, s, :, lo] = (W[b, i, j, s, :, lo].astype(F32) + A2[i, j].astype(F32)).astype(BF16)
                return carry

            lax.fori_loop(0, ZS, add_a, 0)
            wires.copy(W.at[b, :, 1 - y, s, :, lo], A3, slot + 3, flip_y)
            wires.arrived(B2, slot + 2, flip_y)

            def add_b(i, carry):
                for j in range(SS):
                    W[b, i, y, j, :, hi] = (W[b, i, y, j, :, hi].astype(F32) + B2[i, j].astype(F32)).astype(BF16)
                return carry

            lax.fori_loop(0, ZS, add_b, 0)
            wires.copy(W.at[b, :, y, 1 - s, :, hi], B3, slot + 4, side)

        def fourth():
            wires.arrived(A3, slot + 3, flip_y)
            wires.arrived(B3, slot + 4, side)
            for i in range(ZS):
                W[b, i, y, s, :, lo] = (W[b, i, y, s, :, lo].astype(F32) + A3[i].astype(F32)).astype(BF16)
                W[b, i, y, s, :, hi] = (W[b, i, y, s, :, hi].astype(F32) + B3[i].astype(F32)).astype(BF16)
            for dz in range(1, ZS):
                wires.copy(W.at[b, z ^ dz, y, s], ZR_.at[z], slot + 5 + z, dev(b, h ^ (2 * dz), s))

        def fifth():
            total = W[b, z, y, s].astype(F32)
            for dz in range(1, ZS):
                wires.arrived(ZR_.at[z ^ dz], slot + 5 + (z ^ dz), side)
                total = total + ZR_[z ^ dz].astype(F32)
            out_ref[...] = total

        return first, second, third, fourth, fifth

    sr = scatter(RG, CR, AR2, BR2, AR3, BR3, ZR, rg_ref)
    se = scatter(EG, CE, AE2, BE2, AE3, BE3, ZE, eg_ref)
    sm = scatter(MG, CM, AM2, BM2, AM3, BM3, ZM, mg_ref)
    for f in range(FF // step):
        cols = slice(f * step, f * step + step)
        out = dot_tn(ACT[:, cols], g_low).astype(BF16)
        per_b = FF // 2
        first = f * step
        b_ = first // per_b
        z_ = (first % per_b) * ZS // per_b
        zs = max(1, step * ZS // per_b)
        RG[b_, z_ : z_ + zs] = out.reshape(zs, YS, SS, FF // (2 * n), D)
    sr[0]()
    for f in range(FF // step):
        cols = slice(f * step, f * step + step)
        EG[:, :, :, :, :, cols] = dot_tn(second_low, GH[:, cols]).astype(BF16).reshape(2, ZS, YS, SS, r, step)
    se[0]()
    MG[...] = dot_tn(att_low, middle_low).astype(BF16).reshape(2, ZS, YS, SS, r, D)
    sm[0]()
    for _, peer in heads:
        wires.arrived(GAR.at[peer], ga_slot + peer, side)

    cut = iota((T, T), 1) >= iota((T, T), 0)
    low_rows = iota((T, T), 0) < HEAD
    dkv_slot = wires.slots(HEADS)
    rkv_slot = wires.slots(HEADS)
    rdq_slot = wires.slots(HEADS)

    def zero(t, carry):
        DKVT[t] = jnp.zeros((128, T), F32)
        return carry

    lax.fori_loop(0, n, zero, 0)

    def zero_rows(t, carry):
        DROWT[t] = jnp.zeros((HEAD, T), F32)
        return carry

    lax.fori_loop(0, n + 4, zero_rows, 0)
    JGA[...] = jnp.zeros((D, 256), F32)
    sums = {"c": jnp.zeros((1, 128), F32), "o": jnp.zeros((1, 128), F32), "kv": jnp.zeros((1, 128), F32), "q": jnp.zeros((1, 128), F32)}

    def backward(k):
        block = k * SS + s
        base = n - 1 - block
        trips = (k * SS + SS + 3) // 4
        ga = unfold(GAR[k].astype(F32))
        inverse = LIN[k][:, :1]
        spread = jnp.sum(ga * ATF[k], axis=1, keepdims=True) * inverse
        spread = dot(flip.astype(F32), jnp.broadcast_to(spread, (T, T)), precision=lax.Precision.HIGHEST)
        scaled = (ga * inverse).astype(BF16)
        both = dot(flip, wide([QC[k][:, :HEAD], scaled]))
        ga_pad = jnp.where(low_lane, 0.0, both).astype(BF16)
        both_t = both.T
        left = wide([jnp.where(low_rows, both_t, 0.0), jnp.where(low_rows, 0.0, both_t)]).astype(BF16)
        qo_t = dot(flip, QO[k]).T[HEAD:].astype(BF16)
        dq, dqo = jnp.zeros((T, 128), F32), jnp.zeros((T, 128), F32)
        for ch in range(trips):
            first = ch * 4
            kv = KV[first : first + 4].reshape(4 * T, 128)
            gp = dot_nt(ga_pad, kv)
            low, turned, probs = [], [], []
            for t in range(4):
                p = PST[k, first + t]
                ds = p.astype(F32) * (gp[:, t * T : (t + 1) * T] - spread)
                probs.append(p)
                low.append(ds.astype(BF16))
                turned.append(pltpu.roll(ds, 0, 1, stride=1, stride_axis=0))
            low, probs = wide(low), wide(probs)
            dq = dq + dot(low, kv)
            add = dot(left, tall([low, probs]))
            for t in range(4):
                DKVT[first + t] += add[:, t * T : (t + 1) * T]
            dr = [jnp.where(cut, turned[0], 0.0)]
            for t in range(1, 4):
                dr.append(jnp.where(cut, turned[t], turned[t - 1]))
            dr.append(jnp.where(cut, 0.0, turned[3]))
            dr = wide(dr).astype(BF16)
            window = OFF[pl.ds(base + first, 5)].reshape(5 * T, 128)
            dqo = dqo + dot(dr, window)
            back = dot(qo_t, dr)
            for t in range(5):
                DROWT[base + first + t] += back[:, t * T : (t + 1) * T]
        dqo = pltpu.roll(dqo, HEAD, 1)
        sums["c"] = sums["c"] + colsum(dq) * 0.125
        sums["o"] = sums["o"] + colsum(dqo) * 0.125
        dq = ((dq + dqo) * 0.125).astype(BF16)
        dq = dot(flip, dq)
        DQF[k] = fold(dq[:, :HEAD]).astype(BF16)
        wires.copy(DQF.at[k], RDQ.at[h], rdq_slot + h, dev(b, k, s), when=h != k)
        DKVS[k] = DKVT[k * SS + 1 - s].T.astype(BF16)
        wires.copy(DKVS.at[k], DKVR.at[k], dkv_slot + k, side)
        return dq

    def settle(k, dq):
        wires.arrived(DKVR.at[k], dkv_slot + k, side)
        dkv = (DKVT[k * SS + s].T + DKVR[k].astype(F32)).astype(BF16)
        DKVF[k] = dkv
        wires.copy(DKVF.at[k], RKV.at[h], rkv_slot + h, dev(b, k, s), when=h != k)
        sums["kv"] = sums["kv"] + colsum(dkv.astype(F32))
        sums["q"] = sums["q"] + jnp.where(low_lane, colsum(dq), 0.0)
        low = wide([dkv, jnp.where(low_lane, dq, 0.0).astype(BF16)])
        JGA[...] += dot_tn(NRM[k], low)

    pump = {
        7: [sr[1]],
        6: [se[1]],
        5: [sm[1], sr[2]],
        4: [se[2]],
        3: [sm[2], sr[3]],
        2: [se[3], gj[4]],
        1: [sm[3]],
        0: [],
    }
    waiting = None
    for k in reversed(range(HEADS)):
        dq = backward(k)
        if waiting is not None:
            settle(*waiting)
        waiting = (k, dq)
        for step_ in pump[k]:
            step_()

    rows_t = wide([DROWT[t] for t in range(tiles)])
    upper = rows_t.astype(BF16)
    lower = (rows_t - upper.astype(F32)).astype(BF16)
    og_t = dot(tall([upper, lower]), TAB[...])
    og = (og_t[:HEAD] + og_t[HEAD:]).T
    settle(*waiting)
    RKV[h] = DKVF[h]
    RDQ[h] = DQF[h]
    og = pltpu.roll(wide([og, jnp.zeros((D, HEAD), F32)]), HEAD, 1)
    grads = JGA[...]
    w_f = own_w.astype(F32)
    col_w = jnp.where(iota((D, 256), 1) < 192, w_f, 0.0)
    ones = jnp.ones((8, 256), F32)
    totals = jnp.broadcast_to(wide([sums["kv"], sums["q"]]), (8, 256))
    highest = lax.Precision.HIGHEST
    shift_mixer = dot(totals, col_w, ((1,), (1,)), highest)[0:1]
    gain_mixer = dot(ones, col_w * grads, ((1,), (1,)), highest)[0:1]
    gain_mixer = (gain_mixer - shift_one * shift_mixer) / gain_one

    def place_head(row):
        row = jnp.where(low_lane, row, 0.0)
        row = row + pltpu.roll(row, HEAD, 1)
        row = wide([row] * (D // 128))
        return jnp.where(iota((1, D), 1) // HEAD == h, row, 0.0)

    partial = tall(
        [gain_mixer, shift_mixer, place_head(sums["c"]), place_head(sums["o"])]
        + vec_feed
        + [jnp.zeros((9, D), F32)]
    )
    row_index = iota((r, 128), 0)
    last = wide([grads[:, :128], grads[:, 128:] + og]).astype(BF16).reshape(2, HEADS, SS, r, 256)
    for b_ in range(2):
        for k in range(HEADS):
            for s_ in range(SS):
                d_ = (b_ * HEADS + k) * SS + s_
                tile = partial[:, d_ // 8 * 128 : d_ // 8 * 128 + 128]
                if d_ % 8:
                    tile = pltpu.roll(tile, 128 - d_ % 8 * 16, 1)
                bias = bias_expand[:, d_ // 2 * 128 : d_ // 2 * 128 + 128]
                if d_ % 2:
                    bias = pltpu.roll(bias, 64, 1)
                tile = jnp.where(row_index == 7, bias, tile)
                JGM[b_, k, s_] = wide([last[b_, k, s_], tile.astype(BF16)])
    jr_slot = wires.slots(4)
    for b_, s_ in group:
        wires.copy(JGM.at[b_, :, s_], JR1.at[b * 2 + s], jr_slot + b * 2 + s, dev(b_, h, s_))

    for _, peer in heads:
        wires.arrived(RKV.at[peer], rkv_slot + peer, side)
        wires.arrived(RDQ.at[peer], rdq_slot + peer, side)
    pieces_k, pieces_v = [], []
    for k in range(0, HEADS, 2):
        a_, b_ = RKV[k].astype(F32), RKV[k + 1].astype(F32)
        pieces_k.append(jnp.where(low_lane, a_, pltpu.roll(b_, HEAD, 1)))
        pieces_v.append(jnp.where(low_lane, pltpu.roll(a_, HEAD, 1), b_))
    grad_joint = wide([by_heads(RDQ), wide(pieces_k).astype(BF16), wide(pieces_v).astype(BF16)])
    joint_w = JW[...].reshape(D, 3 * D)
    grad_normed = dot_nt(grad_joint, joint_w)
    n_one, inverse_one = normalize(x)
    gradient_ref[0] += norm_back(grad_normed * gain_one, n_one, inverse_one)

    total = JGM[b, :, s].astype(F32)
    for b_, s_ in group:
        wires.arrived(JR1.at[b_ * 2 + s_], jr_slot + b_ * 2 + s_, core)
        total = total + JR1[b_ * 2 + s_].astype(F32)
    JF[...] = total.astype(BF16)
    jf_slot = wires.slots(HEADS)
    for _, peer in heads:
        wires.copy(JF.at[peer], JR2.at[h], jf_slot + h, dev(b, peer, s))
    JR2[h] = JF[h]
    sr[4]()
    se[4]()
    sm[4]()
    for _, peer in heads:
        wires.arrived(JR2.at[peer], jf_slot + peer, side)
    got = [JR2[k].astype(F32) for k in range(HEADS)]
    jg_ref[...] = wide([a[:, 128:192] for a in got] + [a[:, 0:64] for a in got] + [a[:, 64:128] for a in got])
    og_ref[...] = wide([a[:, 192:256] for a in got])
    vectors = got[0][:, 256:]
    for a in got[1:]:
        vectors = vectors + a[:, 256:]
    vg_ref[...] = vectors
    wires.finish()


def table_reversed(length, width):
    half = width // 2
    freq = 10000.0 ** (-2.0 * np.arange(half) / width)
    angle = np.arange(length - 1, -1, -1)[:, None] * freq[None, :]
    return np.concatenate([np.sin(angle), np.cos(angle)], axis=1).astype(np.float32).astype(ml_dtypes.bfloat16)


def fast(
    n,
    inputs,
    segments,
    mixer_gain,
    mixer_shift,
    joint_weight,
    offset_weight,
    content_bias,
    offset_bias,
    merge_weight,
    feed_gain,
    feed_shift,
    expand_weight,
    expand_bias,
    reduce_weight,
    reduce_bias,
    cotangent,
):
    T, D = inputs.shape[1:]
    r = joint_weight.shape[0]
    FF = expand_weight.shape[1]
    rr = reduce_weight.shape[0]
    length = segments.shape[1]
    small = [mixer_gain, mixer_shift, content_bias, offset_bias, feed_gain, feed_shift, reduce_bias]
    vec = jnp.stack([jnp.pad(v, (0, 128 - v.shape[0])) for v in small + [expand_bias]])
    vec = jnp.pad(vec, ((0, r - vec.shape[0]), (0, 0)))
    table = jnp.asarray(table_reversed(length, D))
    V = pltpu.VMEM
    grid4 = (ZS, YS, SS)

    def reduce_buffers(rows, cols):
        return (
            V((ZS, YS, rows, cols // 2), BF16),
            V((ZS, SS, rows, cols // 2), BF16),
        ), (V((ZS, rows, cols // 2), BF16), V((ZS, rows, cols // 2), BF16))

    m2, m3 = reduce_buffers(r, D)
    e2, e3 = reduce_buffers(r, FF)
    r2, r3 = reduce_buffers(rr, D)
    scratch = [
        V((length, D), BF16),
        V((HEADS, T, D), BF16),
        V((HEADS, T, D), BF16),
        V((HEADS, r, 384), BF16),
        V((2, HEADS, SS, r, 384), BF16),
        V((2,) + grid4 + (r, 3 * D), BF16),
        V((2,) + grid4 + (r, D), BF16),
        V((2,) + grid4 + (r, FF), BF16),
        V((2,) + grid4 + (rr, D), BF16),
        V((n, T, 128), BF16),
        V((HEADS, T, 128), BF16),
        V((HEADS, T, 128), BF16),
        V((n + 4, T, 128), BF16),
        V((n, T, T), F32),
        V((HEADS, n, T, T), BF16),
        V((HEADS, T, HEAD), F32),
        V((HEADS, T, T), F32),
        V((HEADS, T // 2, 128), BF16),
        V((HEADS, T // 2, 128), BF16),
        V((T, FF), BF16),
        V((T, FF), BF16),
        V((HEADS, T // 2, 128), BF16),
        V((HEADS, T // 2, 128), BF16),
        V((n, 128, T), F32),
        V((n + 4, HEAD, T), F32),
        V((HEADS, T, 128), BF16),
        V((HEADS, T, 128), BF16),
        V((HEADS, T, 128), BF16),
        V((HEADS, T // 2, 128), BF16),
        V((HEADS, T, 128), BF16),
        V((HEADS, T // 2, 128), BF16),
        V((2,) + grid4 + (r, D), BF16),
        V((2,) + grid4 + (r, FF), BF16),
        V((2,) + grid4 + (rr, D), BF16),
        V(grid4 + (r, D), BF16),
        V(grid4 + (r, FF), BF16),
        V(grid4 + (rr, D), BF16),
        m2[0],
        m2[1],
        e2[0],
        e2[1],
        r2[0],
        r2[1],
        m3[0],
        m3[1],
        e3[0],
        e3[1],
        r3[0],
        r3[1],
        V((ZS, r, D), BF16),
        V((ZS, r, FF), BF16),
        V((ZS, rr, D), BF16),
        V((D, 256), F32),
        V((2, HEADS, SS, r, 384), BF16),
        V((4, HEADS, r, 384), BF16),
        V((HEADS, r, 384), BF16),
        V((HEADS, r, 384), BF16),
        pltpu.SemaphoreType.DMA,
        pltpu.SemaphoreType.DMA((180,)),
        pltpu.SemaphoreType.DMA((180,)),
    ]
    vmem, hbm = pl.BlockSpec(memory_space=V), pl.BlockSpec(memory_space=pl.ANY)
    outs = pl.pallas_call(
        functools.partial(layer_kernel, n),
        out_shape=[
            jax.ShapeDtypeStruct((1, T, D), BF16),
            jax.ShapeDtypeStruct((1, T, D), F32),
            jax.ShapeDtypeStruct((r, 3 * D), F32),
            jax.ShapeDtypeStruct((r, D), F32),
            jax.ShapeDtypeStruct((r, D), F32),
            jax.ShapeDtypeStruct((r, FF), F32),
            jax.ShapeDtypeStruct((rr, D), F32),
            jax.ShapeDtypeStruct((r, 128), F32),
        ],
        in_specs=[vmem] * 9 + [hbm],
        out_specs=[vmem] * 8,
        scratch_shapes=scratch,
        compiler_params=pltpu.CompilerParams(
            collective_id=0, has_side_effects=True, vmem_limit_bytes=60 * 2**20
        ),
    )(
        inputs,
        segments,
        vec,
        joint_weight,
        offset_weight,
        merge_weight,
        expand_weight,
        reduce_weight,
        cotangent,
        table,
    )
    result, gradient, jg, og, mg, eg, rg, vg = outs
    few = mixer_gain.shape[0]
    return (
        result,
        gradient,
        vg[0, :few],
        vg[1, :few],
        jg,
        og,
        vg[2, :few],
        vg[3, :few],
        mg,
        vg[4, :few],
        vg[5, :few],
        eg,
        vg[7, : expand_bias.shape[0]],
        rg,
        vg[6, :few],
    )


def solution(mesh):
    in_specs = (
        P("batch", "ctx", None),
        P("batch", None),
        P(("batch", "ctx")),
        P(("batch", "ctx")),
        P(("batch", "ctx"), None),
        P(("batch", "ctx"), None),
        P(("batch", "ctx")),
        P(("batch", "ctx")),
        P(("batch", "ctx"), None),
        P(("batch", "ctx")),
        P(("batch", "ctx")),
        P(("batch", "ctx"), None),
        P(("batch", "ctx")),
        P(("batch", "ctx"), None),
        P(("batch", "ctx")),
        P("batch", "ctx", None),
    )
    out_specs = (
        P("batch", "ctx", None),
        P("batch", "ctx", None),
        P(("batch", "ctx")),
        P(("batch", "ctx")),
        P(("batch", "ctx"), None),
        P(("batch", "ctx"), None),
        P(("batch", "ctx")),
        P(("batch", "ctx")),
        P(("batch", "ctx"), None),
        P(("batch", "ctx")),
        P(("batch", "ctx")),
        P(("batch", "ctx"), None),
        P(("batch", "ctx")),
        P(("batch", "ctx"), None),
        P(("batch", "ctx")),
    )
    n, cores = mesh.shape["ctx"], mesh.shape["batch"]

    def layer(*args):
        suits = n == HEADS * SS and cores == 2 and args[0].shape[1] == 128 and args[4].shape[0] == 16
        return fast(n, *args) if suits else local(*args)

    return jax.shard_map(layer, mesh=mesh, in_specs=in_specs, out_specs=out_specs, check_vma=False)
```

```python
import functools
import math
from types import SimpleNamespace

import jax
import jax.numpy as jnp
import ml_dtypes
import numpy as np
from jax import lax
from jax.experimental import pallas as pl
from jax.experimental.pallas import tpu as pltpu
from jax.sharding import PartitionSpec as P

HEADS = 8
HEAD = 64


masked_score = -1e30


def shifted(array, axis, by):
    peers = lax.axis_size(axis)
    pairs = [(i, i + by) for i in range(peers) if 0 <= i + by < peers]
    return lax.ppermute(array, axis, pairs)


def shifted_2(value, axis, steps):
    count = lax.axis_size(axis)
    pairs = [(source, (source + steps) % count) for source in range(count)]
    return lax.ppermute(value, axis, pairs)


def layer_norm(values, gain, shift):
    center = values - jnp.mean(values, axis=-1, keepdims=True)
    spread = jnp.mean(center * center, axis=-1, keepdims=True)
    return center * lax.rsqrt(spread + 1e-05) * gain + shift


def sinusoid(first, count, width):
    half = width // 2
    freq = jnp.power(10000.0, -2.0 * jnp.arange(half, dtype=jnp.float32) / width)
    place = (first + jnp.arange(count, dtype=jnp.int32)).astype(jnp.float32)
    angle = place[:, None] * freq[None, :]
    return jnp.concatenate([jnp.sin(angle), jnp.cos(angle)], axis=1)


def contract_rows(left, right):
    return lax.dot_general(
        left, right, (((0,), (0,)), ((), ())), preferred_element_type=jnp.float32
    )


def contract_cols(left, right):
    return lax.dot_general(
        left, right, (((1,), (1,)), ((), ())), preferred_element_type=jnp.float32
    )


def split_contract(table, grad_rows):
    upper = grad_rows.astype(jnp.bfloat16)
    lower = (grad_rows - upper.astype(jnp.float32)).astype(jnp.bfloat16)
    return contract_rows(table, upper) + contract_rows(table, lower)


def fold_blocks(step, carry, pieces, limit):
    count = pieces[0].shape[0]
    size = min(count, limit)
    number = count // size
    stacked = tuple((item.reshape((number, size) + item.shape[1:]) for item in pieces))

    def inner(state, item):
        offset, parts = item
        return (step(state, parts, offset * size), None)

    folded, _ = lax.scan(inner, carry, (jnp.arange(number, dtype=jnp.int32), stacked))
    return folded


def realign(relative_scores, count):
    heads, rows, width = relative_scores.shape
    flat = relative_scores.reshape(heads, rows * width)
    band = flat[:, rows - 1 : rows - 1 + rows * (width - 1)]
    return band.reshape(heads, rows, width - 1)[:, :, :count]


def pair_terms(
    query_content_term, query_position_term, keys, query_first, key_first, seg_row, offsets_pad
):
    rows, heads, size = query_content_term.shape
    count = keys.shape[0]
    length = offsets_pad.shape[0] // 2
    anchor = query_first - key_first - count + length
    attention_span = lax.dynamic_slice_in_dim(offsets_pad, anchor, rows + count, 0)[::-1].reshape(
        rows + count, heads, size
    )
    content = jnp.einsum(
        "ahd,bhd->hab", query_content_term, keys, preferred_element_type=jnp.float32
    )
    relative_scores = jnp.einsum(
        "scx,icx->csi", query_position_term, attention_span, preferred_element_type=jnp.float32
    )
    scores = (content + realign(relative_scores, count)) * (1.0 / math.sqrt(size))
    query_seg = lax.dynamic_slice_in_dim(seg_row, query_first, rows, 0)
    key_seg = lax.dynamic_slice_in_dim(seg_row, key_first, count, 0)
    query_pos = query_first + jnp.arange(rows, dtype=jnp.int32)
    key_pos = key_first + jnp.arange(count, dtype=jnp.int32)
    allowed = (key_pos[None, :] <= query_pos[:, None]) & (key_seg[None, :] == query_seg[:, None])
    return (scores, allowed, attention_span, anchor)


def pair_grads(
    query_content_term,
    query_position_term,
    keys,
    values,
    query_first,
    key_first,
    seg_row,
    offsets_pad,
    logsum,
    spread,
    grad_attended,
):
    rows, heads, size = query_content_term.shape
    count = keys.shape[0]
    scale = 1.0 / math.sqrt(size)
    scores, allowed, attention_span, anchor = pair_terms(
        query_content_term, query_position_term, keys, query_first, key_first, seg_row, offsets_pad
    )
    probs = jnp.where(allowed[None], jnp.exp(scores - logsum[..., None]), 0.0)
    grad_values = jnp.einsum(
        "hab,ahd->bhd",
        probs.astype(jnp.bfloat16),
        grad_attended,
        preferred_element_type=jnp.float32,
    )
    grad_probs = jnp.einsum(
        "ahd,bhd->hab", grad_attended, values, preferred_element_type=jnp.float32
    )
    grad_scores = (probs * (grad_probs - spread[..., None])).astype(jnp.bfloat16)
    grad_content = scale * jnp.einsum(
        "hab,bhd->ahd", grad_scores, keys, preferred_element_type=jnp.float32
    )
    grad_keys = scale * jnp.einsum(
        "hab,ahd->bhd", grad_scores, query_content_term, preferred_element_type=jnp.float32
    )
    blank = jnp.zeros((heads, rows, rows + count), jnp.float32)
    _, realign_back = jax.vjp(lambda relative_scores: realign(relative_scores, count), blank)
    gradient_relative_scores = realign_back(grad_scores.astype(jnp.float32))[0].astype(jnp.bfloat16)
    grad_offset = scale * jnp.einsum(
        "nsk,kno->sno", gradient_relative_scores, attention_span, preferred_element_type=jnp.float32
    )
    grad_window = scale * jnp.einsum(
        "cqu,qcn->ucn",
        gradient_relative_scores,
        query_position_term,
        preferred_element_type=jnp.float32,
    )
    grad_window = grad_window.reshape(rows + count, heads * size)[::-1]
    return (grad_content, grad_offset, grad_keys, grad_values, grad_window, anchor)


def add_window(grad_rows, grad_window, anchor):
    current = lax.dynamic_slice_in_dim(grad_rows, anchor, grad_window.shape[0], 0)
    return lax.dynamic_update_slice_in_dim(grad_rows, current + grad_window, anchor, 0)


def local(
    inputs,
    segments,
    mixer_gain,
    mixer_shift,
    joint_weight,
    offset_weight,
    content_bias,
    offset_bias,
    merge_weight,
    feed_gain,
    feed_shift,
    expand_weight,
    expand_bias,
    reduce_weight,
    reduce_bias,
    cotangent,
):
    (
        first_gain,
        first_shift,
        joint_matrix,
        offset_matrix,
        bias_content,
        bias_position,
        merge_matrix,
    ) = (
        lax.all_gather(mixer_gain, ("batch", "ctx"), axis=0, tiled=True),
        lax.all_gather(mixer_shift, ("batch", "ctx"), axis=0, tiled=True),
        lax.all_gather(joint_weight, ("batch", "ctx"), axis=0, tiled=True),
        lax.all_gather(offset_weight, ("batch", "ctx"), axis=0, tiled=True),
        lax.all_gather(content_bias, ("batch", "ctx"), axis=0, tiled=True),
        lax.all_gather(offset_bias, ("batch", "ctx"), axis=0, tiled=True),
        lax.all_gather(merge_weight, ("batch", "ctx"), axis=0, tiled=True),
    )
    tokens = inputs[0].astype(jnp.float32)
    rows, width = tokens.shape
    seg_row = segments[0]
    length = seg_row.shape[0]
    place = lax.axis_index("ctx")
    cycle = lax.axis_size("ctx")
    block_first = place * rows
    heads_shape = (rows, HEADS, HEAD)
    gain_one = first_gain.astype(jnp.float32)
    shift_one = first_shift.astype(jnp.float32)
    normed = layer_norm(tokens, gain_one, shift_one)
    normed_low = normed.astype(jnp.bfloat16)
    joint = jnp.dot(normed_low, joint_matrix, preferred_element_type=jnp.float32)
    query = joint[:, :width]
    keys = joint[:, width : 2 * width].astype(jnp.bfloat16).reshape(heads_shape)
    values = joint[:, 2 * width :].astype(jnp.bfloat16).reshape(heads_shape)
    query_content_term = (
        (query + bias_content.astype(jnp.float32)).astype(jnp.bfloat16).reshape(heads_shape)
    )
    query_position_term = (
        (query + bias_position.astype(jnp.float32)).astype(jnp.bfloat16).reshape(heads_shape)
    )
    everyone = lax.axis_size(("batch", "ctx"))
    share = length // everyone
    table = sinusoid(lax.axis_index(("batch", "ctx")) * share, share, width).astype(jnp.bfloat16)
    offsets_local = jnp.dot(table, offset_matrix, preferred_element_type=jnp.float32).astype(
        jnp.bfloat16
    )
    offsets_all = lax.all_gather(offsets_local, ("batch", "ctx"), axis=0, tiled=True)
    offsets_pad = jnp.concatenate([jnp.zeros_like(offsets_all), offsets_all], axis=0)

    def stats_block(carry, pieces, start):
        peak, total = carry
        scores, allowed, attention_span, anchor = pair_terms(
            query_content_term,
            query_position_term,
            pieces[0],
            block_first,
            start,
            seg_row,
            offsets_pad,
        )
        masked = jnp.where(allowed[None], scores, masked_score)
        new_peak = jnp.maximum(peak, jnp.max(masked, axis=-1))
        added = jnp.sum(
            jnp.where(allowed[None], jnp.exp(masked - new_peak[..., None]), 0.0), axis=-1
        )
        return (new_peak, total * jnp.exp(peak - new_peak) + added)

    peak_start = jnp.full((HEADS, rows), masked_score, jnp.float32)
    total_start = jnp.zeros((HEADS, rows), jnp.float32)
    peak, total = fold_blocks(
        stats_block,
        (peak_start, total_start),
        (lax.all_gather(keys, "ctx", axis=0, tiled=True),),
        rows,
    )
    logsum = peak + jnp.log(total)

    def output_block(carry, pieces, start):
        scores, allowed, attention_span, anchor = pair_terms(
            query_content_term,
            query_position_term,
            pieces[0],
            block_first,
            start,
            seg_row,
            offsets_pad,
        )
        probs = jnp.where(allowed[None], jnp.exp(scores - logsum[..., None]), 0.0).astype(
            jnp.bfloat16
        )
        return carry + jnp.einsum(
            "hab,bhd->ahd", probs, pieces[1], preferred_element_type=jnp.float32
        )

    mixed = fold_blocks(
        output_block,
        jnp.zeros(heads_shape, jnp.float32),
        (
            lax.all_gather(keys, "ctx", axis=0, tiled=True),
            lax.all_gather(values, "ctx", axis=0, tiled=True),
        ),
        rows,
    )
    attended_low = mixed.reshape(rows, width).astype(jnp.bfloat16)
    middle = tokens + jnp.dot(attended_low, merge_matrix, preferred_element_type=jnp.float32)
    second_gain, second_shift, expand_matrix, expand_vector, reduce_matrix, reduce_vector = (
        lax.all_gather(feed_gain, ("batch", "ctx"), axis=0, tiled=True),
        lax.all_gather(feed_shift, ("batch", "ctx"), axis=0, tiled=True),
        lax.all_gather(expand_weight, ("batch", "ctx"), axis=0, tiled=True),
        lax.all_gather(expand_bias, ("batch", "ctx"), axis=0, tiled=True),
        lax.all_gather(reduce_weight, ("batch", "ctx"), axis=0, tiled=True),
        lax.all_gather(reduce_bias, ("batch", "ctx"), axis=0, tiled=True),
    )
    gain_two = second_gain.astype(jnp.float32)
    shift_two = second_shift.astype(jnp.float32)
    second_low = layer_norm(middle, gain_two, shift_two).astype(jnp.bfloat16)
    hidden = jnp.dot(
        second_low, expand_matrix, preferred_element_type=jnp.float32
    ) + expand_vector.astype(jnp.float32)
    active_low = jax.nn.gelu(hidden, approximate=True).astype(jnp.bfloat16)
    output = (
        middle
        + jnp.dot(active_low, reduce_matrix, preferred_element_type=jnp.float32)
        + reduce_vector.astype(jnp.float32)
    )
    result = output.astype(jnp.bfloat16)[None]
    grad_out = cotangent[0]
    grad_outf = grad_out.astype(jnp.float32)
    grad_reduce_bias = jnp.sum(grad_outf, axis=0)
    grad_reduce = contract_rows(active_low, grad_out)
    grad_active = contract_cols(grad_out, reduce_matrix)
    _, gelu_back = jax.vjp(lambda value: jax.nn.gelu(value, approximate=True), hidden)
    grad_hidden = gelu_back(grad_active)[0].astype(jnp.bfloat16)
    grad_expand_bias = jnp.sum(grad_hidden.astype(jnp.float32), axis=0)
    grad_expand = contract_rows(second_low, grad_hidden)
    grad_second = contract_cols(grad_hidden, expand_matrix)
    _, second_back = jax.vjp(layer_norm, middle, gain_two, shift_two)
    grad_mid, grad_gain_two, grad_shift_two = second_back(grad_second)
    grad_middle = grad_outf + grad_mid
    feed_sums = (
        lax.psum_scatter(grad_gain_two, ("batch", "ctx"), scatter_dimension=0, tiled=True),
        lax.psum_scatter(grad_shift_two, ("batch", "ctx"), scatter_dimension=0, tiled=True),
        lax.psum_scatter(grad_expand, ("batch", "ctx"), scatter_dimension=0, tiled=True),
        lax.psum_scatter(grad_expand_bias, ("batch", "ctx"), scatter_dimension=0, tiled=True),
        lax.psum_scatter(grad_reduce, ("batch", "ctx"), scatter_dimension=0, tiled=True),
        lax.psum_scatter(grad_reduce_bias, ("batch", "ctx"), scatter_dimension=0, tiled=True),
    )
    middle_low = grad_middle.astype(jnp.bfloat16)
    grad_merge = contract_rows(attended_low, middle_low)
    grad_attended = (
        contract_cols(middle_low, merge_matrix).astype(jnp.bfloat16).reshape(heads_shape)
    )
    spread = jnp.einsum("ahd,ahd->ha", grad_attended.astype(jnp.float32), mixed)
    zero_heads = jnp.zeros(heads_shape, jnp.float32)
    zero_rows = jnp.zeros((2 * length, width), jnp.float32)

    def cycle_step(turn, carry):
        visiting, carried, grad_content, grad_offset, grad_rows = carry
        owner = (place - turn) % cycle
        terms = pair_grads(
            query_content_term,
            query_position_term,
            visiting[0],
            visiting[1],
            block_first,
            owner * rows,
            seg_row,
            offsets_pad,
            logsum,
            spread,
            grad_attended,
        )
        carried = carried + jnp.stack([terms[2], terms[3]])
        grad_rows = add_window(grad_rows, terms[4], terms[5])
        visiting = shifted(visiting, "ctx", 1)
        carried = shifted_2(carried.astype(jnp.bfloat16), "ctx", 1).astype(carried.dtype)
        return (visiting, carried, grad_content + terms[0], grad_offset + terms[1], grad_rows)

    start_state = (
        jnp.stack([keys, values]),
        jnp.zeros((2,) + heads_shape, jnp.float32),
        zero_heads,
        zero_heads,
        zero_rows,
    )
    _, carried, grad_content, grad_offset, grad_rows = lax.fori_loop(
        0, cycle, cycle_step, start_state
    )
    grad_keys = carried[0]
    grad_values = carried[1]
    grad_content_bias = jnp.sum(grad_content, axis=0).reshape(width)
    gradient_position_bias = jnp.sum(grad_offset, axis=0).reshape(width)
    grad_joint = jnp.concatenate(
        [
            (grad_content + grad_offset).reshape(rows, width),
            grad_keys.reshape(rows, width),
            grad_values.reshape(rows, width),
        ],
        axis=1,
    ).astype(jnp.bfloat16)
    grad_joint_matrix = contract_rows(normed_low, grad_joint)
    grad_normed = contract_cols(grad_joint, joint_matrix)
    _, first_back = jax.vjp(layer_norm, tokens, gain_one, shift_one)
    grad_tokens, grad_gain_one, grad_shift_one = first_back(grad_normed)
    gradient = (grad_middle + grad_tokens)[None]
    full_table = sinusoid(0, length, width).astype(jnp.bfloat16)
    grad_offset_matrix = split_contract(full_table, grad_rows[length:])
    mixer_sums = (
        lax.psum_scatter(grad_gain_one, ("batch", "ctx"), scatter_dimension=0, tiled=True),
        lax.psum_scatter(grad_shift_one, ("batch", "ctx"), scatter_dimension=0, tiled=True),
        lax.psum_scatter(grad_joint_matrix, ("batch", "ctx"), scatter_dimension=0, tiled=True),
        lax.psum_scatter(grad_offset_matrix, ("batch", "ctx"), scatter_dimension=0, tiled=True),
        lax.psum_scatter(grad_content_bias, ("batch", "ctx"), scatter_dimension=0, tiled=True),
        lax.psum_scatter(gradient_position_bias, ("batch", "ctx"), scatter_dimension=0, tiled=True),
        lax.psum_scatter(grad_merge, ("batch", "ctx"), scatter_dimension=0, tiled=True),
    )
    return (
        result,
        gradient,
        mixer_sums[0],
        mixer_sums[1],
        mixer_sums[2],
        mixer_sums[3],
        mixer_sums[4],
        mixer_sums[5],
        mixer_sums[6],
        feed_sums[0],
        feed_sums[1],
        feed_sums[2],
        feed_sums[3],
        feed_sums[4],
        feed_sums[5],
    )


F32, BF16 = jnp.float32, jnp.bfloat16
MESH = pl.DeviceIdType.MESH
NEG = -1e30
ZS, YS, SS = 4, 2, 2


def dot(a, b, dims=((1,), (0,)), precision=None):
    return lax.dot_general(a, b, (dims, ((), ())), preferred_element_type=F32, precision=precision)


def dot_nt(a, b):
    return dot(a, b, ((1,), (1,)))


def dot_tn(a, b):
    return dot(a, b, ((0,), (0,)))


def iota(shape, axis):
    return lax.broadcasted_iota(jnp.int32, shape, axis)


def wide(tiles):
    return jnp.concatenate(tiles, axis=1)


def tall(tiles):
    return jnp.concatenate(tiles, axis=0)


def fold(x):
    half = x.shape[0] // 2
    return wide([x[:half], x[half:]])


def unfold(x):
    return tall([x[:, :HEAD], x[:, HEAD:]])


def normalize(x):
    center = x - jnp.mean(x, axis=-1, keepdims=True)
    inverse = lax.rsqrt(jnp.mean(center * center, axis=-1, keepdims=True) + 1e-05)
    return center * inverse, inverse


def norm_back(e, n, inverse):
    return inverse * (e - jnp.mean(e, axis=-1, keepdims=True) - n * jnp.mean(e * n, axis=-1, keepdims=True))


def colsum(x):
    return jnp.sum(x, axis=0, keepdims=True)


class Wires:
    def __init__(self, sends, recvs):
        self.sends, self.recvs, self.received, self.pending = sends, recvs, 0, []
        self.free = list(range(SENDS))
        self.peak = 0

    def slots(self, count):
        first = self.received
        self.received += count
        return first

    def copy(self, src, dst, slot, to, when=None):
        index = self.free.pop(0)
        self.peak = max(self.peak, SENDS - len(self.free))
        made = pltpu.make_async_remote_copy(
            src_ref=src,
            dst_ref=dst,
            send_sem=self.sends.at[index],
            recv_sem=self.recvs.at[slot],
            device_id=to,
            device_id_type=MESH,
        )
        self.pending.append((made, when, index))
        if when is None:
            made.start()
        else:
            pl.when(when)(made.start)

    def arrived(self, dst, slot, to):
        pltpu.make_async_remote_copy(
            src_ref=dst,
            dst_ref=dst,
            send_sem=self.sends.at[0],
            recv_sem=self.recvs.at[slot],
            device_id=to,
            device_id_type=MESH,
        ).wait_recv()

    def reap(self, keep=0):
        count = len(self.pending) - keep
        for made, when, index in self.pending[:count]:
            if when is None:
                made.wait_send()
            else:
                pl.when(when)(made.wait_send)
            self.free.append(index)
        self.pending = self.pending[count:]


SENDS, RECVS = 104, 75
def layer_kernel(
    n,
    small,
    ins,
    outs,
    *scratch,
):
    (
        TAB,
        TOK,
        NRM,
        W1S,
        W1,
        JW,
        MW,
        EW,
        RW,
        ES,
        PX,
        PG,
        KV,
        QC,
        QO,
        OFF,
        SCR,
        PST,
        ATF,
        LIN,
        ATS,
        ATR,
        ACT,
        GH,
        GSS,
        GSR,
        OUS,
        OUR,
        GAS,
        GAR,
        DKVT,
        DROWT,
        DKVS,
        DKVR,
        DKVF,
        DQF,
        RKV,
        RDQ,
        MG,
        EG,
        RG,
        CM,
        CE,
        CR,
        AM,
        BM,
        BE,
        BR,
        ZM,
        ZE,
        ZR,
        YM,
        YE,
        YR,
        EO,
        EX,
        EY,
        JGA,
        JGM,
        JRC,
        JGX,
        JRS,
        JF,
        JR2,
        x_ref,
        jw_ref,
        ow_ref,
        g_ref,
        ew_ref,
        mw_ref,
        rw_ref,
        result_ref,
        rg_ref,
        eg_ref,
        mg_ref,
        gradient_ref,
        jg_ref,
        og_ref,
        vg_ref,
        local,
        sends,
        recvs,
        seg_ref,
        *vec_refs,
    ) = scratch
    T = x_ref.shape[1]
    D = x_ref.shape[2]
    FF = ew_ref.shape[1]
    r = jw_ref.shape[0]
    b = lax.axis_index("batch")
    c = lax.axis_index("ctx")
    h, s = c // SS, c % SS
    z, y = h // YS, h % YS
    shard = b * n + c

    def dev(b_, h_, s_):
        return {"batch": b_, "ctx": h_ * SS + s_}

    core = dev(1 - b, h, s)
    side = dev(b, h, 1 - s)
    flip_y = dev(b, h ^ 1, s)
    heads = [(q, h ^ q) for q in range(1, HEADS)]
    group = [(1 - b, s), (b, 1 - s), (1 - b, 1 - s)]
    wires = Wires(sends, recvs)

    barrier = pltpu.get_barrier_semaphore()
    for _, peer in heads:
        pl.semaphore_signal(barrier, inc=1, device_id=dev(b, peer, s), device_id_type=MESH)
    for b_, s_ in group:
        pl.semaphore_signal(barrier, inc=1, device_id=dev(b_, h, s_), device_id_type=MESH)

    here = (x_ref, jw_ref, ow_ref, g_ref, ew_ref, mw_ref, rw_ref, TAB)
    loads = [pltpu.make_async_copy(src, dst, local.at[i]) for i, (src, dst) in enumerate(zip(ins, here))]
    few = [pltpu.make_async_copy(src, dst, local.at[8]) for src, dst in zip(small, (seg_ref, *vec_refs))]
    for load in few + loads:
        load.start()
    made = (result_ref, rg_ref, eg_ref, mg_ref, gradient_ref, jg_ref, og_ref, vg_ref)
    stores = [
        pltpu.make_async_copy(src, dst, local.at[i]) for i, (src, dst) in enumerate(zip(made, outs))
    ]

    for load in few:
        load.wait()
    lines = []
    for ref in vec_refs:
        line = ref[...].astype(F32).reshape(1, ref.shape[0])
        lines.append(wide([line, jnp.zeros((1, 128 - ref.shape[0]), F32)]))
    vec = tall(lines + [jnp.zeros((r - len(lines), 128), F32)])
    by_16 = pltpu.roll(vec, (shard % 8) * 16, 1)
    by_64 = pltpu.roll(vec, (shard // 2 % 2) * 64, 1)
    vec = jnp.where(iota(vec.shape, 0) == 7, by_64, by_16).astype(BF16)
    for load in loads[:3]:
        load.wait()
    jw, ow = jw_ref[...], ow_ref[...]
    for k in range(HEADS):
        at = k * HEAD
        W1S[k] = wide(
            [
                jw[:, D + at : D + at + HEAD],
                jw[:, 2 * D + at : 2 * D + at + HEAD],
                jw[:, at : at + HEAD],
                ow[:, at : at + HEAD],
                vec,
            ]
        )
    TOK[h] = x_ref[0]
    W1[b, h, s] = W1S[h]
    for load in loads[3:7]:
        load.wait()
    pl.semaphore_wait(barrier, len(heads) + len(group))
    inner = (z == 1) | (z == 2)
    edge = (z == 0) | (z == 3)
    low_lane = iota((1, 128), 1) < HEAD

    w1_slot, w1_group = wires.slots(1), wires.slots(2)

    def w1_send():
        for _, peer in heads:
            wires.copy(W1S.at[peer], W1.at[b, h, s], w1_slot, dev(b, peer, s))

    def w1_pass():
        wires.arrived(W1.at[b, 0 : HEADS - 1, s], w1_slot, side)
        wires.copy(W1.at[b, :, s], W1.at[b, :, s], w1_group, side)
        wires.copy(W1.at[b, :, s], W1.at[b, :, s], w1_group + 1, core)

    def w1_core():
        wires.arrived(W1.at[b, :, 1 - s], w1_group, side)
        wires.copy(W1.at[b, :, 1 - s], W1.at[b, :, 1 - s], w1_group + 1, core)

    def w1_wait():
        wires.arrived(W1.at[1 - b], w1_group + 1, core)

    tok_slot, far_slot = wires.slots(3), wires.slots(ZS)

    def tok_at(z_):
        return TOK.at[z_ * YS + y]

    def x_send():
        for dz, when in ((2, edge), (1, None), (2, inner), (3, inner)):
            wires.copy(x_ref.at[0], tok_at(z), tok_slot + dz - 1, dev(b, h ^ (2 * dz), s), when=when)
        wires.copy(x_ref.at[0], tok_at(z), far_slot + z, flip_y)

    def take(dz, when=None):
        block = tok_at(z ^ dz)

        def wait():
            wires.arrived(block, tok_slot + dz - 1, side)

        if when is None:
            wait()
        else:
            pl.when(when)(wait)
        if dz == 2:
            wires.copy(block, block, tok_slot + 2, dev(b, h ^ 2, s), when=inner)
        wires.copy(block, block, far_slot + (z ^ dz), flip_y, when=when)

    def x_near():
        take(1, edge)
        take(2)
        take(1, inner)

    def x_far():
        take(3)

    def along_z(at, slot):
        for dz in (1, 2, 3):
            far = dz == 3
            wires.copy(at(z), at(z), slot + dz - 1, dev(b, h ^ (2 * dz), s), when=inner if far else None)

    def from_z(at, slot, dz):
        block = at(z ^ dz)
        wires.arrived(block, slot + dz - 1, side)
        if dz == 2:
            wires.copy(block, block, slot + 2, dev(b, h ^ 2, s), when=inner)

    def gather(W, ref):
        z_slot, y_slot, s_slot, slot, core_slot = (wires.slots(k) for k in (3, 1, 1, 1, 1))

        def at(z_):
            return W.at[b, z_, y, s]

        def own(z_):
            wires.copy(at(z_), at(z_), y_slot, flip_y)
            wires.copy(at(z_), at(z_), s_slot, side)

        def across(y_, s_):
            wires.copy(W.at[b, :, y_, s_], W.at[b, :, y_, s_], core_slot, core)

        def own_():
            W[b, z, y, s] = ref[...]
            own(z)

        def start():
            along_z(at, z_slot)

        def near():
            for dz in (2, 1):
                from_z(at, z_slot, dz)
                own(z ^ dz)

        def far_():
            from_z(at, z_slot, 3)
            own(z ^ 3)
            across(y, s)

        def diag():
            wires.arrived(W.at[b, :, 1 - y, s], y_slot, flip_y)
            wires.copy(W.at[b, :, 1 - y, s], W.at[b, :, 1 - y, s], slot, side)
            wires.arrived(W.at[b, :, y, 1 - s], s_slot, side)
            across(1 - y, s)
            across(y, 1 - s)

        def over():
            wires.arrived(W.at[b, :, 1 - y, 1 - s], slot, side)
            across(1 - y, 1 - s)

        def wait():
            wires.arrived(W.at[1 - b], core_slot, core)

        return SimpleNamespace(own=own_, start=start, near=near, far=far_, diag=diag, over=over, wait=wait)

    m, j = gather(MW, mw_ref), gather(JW, jw_ref)

    def gather_half(W):
        z_slot, y_slot, core_slot = wires.slots(3), wires.slots(1), wires.slots(1)

        def at(z_):
            return W.at[b, z_, y]

        def across(y_):
            wires.copy(W.at[b, :, y_], W.at[b, :, y_], core_slot, core)

        def to_y(z_):
            wires.copy(at(z_), at(z_), y_slot, flip_y)

        def start():
            along_z(at, z_slot)
            to_y(z)

        def near():
            for dz in (2, 1):
                from_z(at, z_slot, dz)
                to_y(z ^ dz)

        def far_():
            from_z(at, z_slot, 3)
            to_y(z ^ 3)
            across(y)

        def over():
            wires.arrived(W.at[b, :, 1 - y], y_slot, flip_y)
            across(1 - y)

        def wait():
            wires.arrived(W.at[1 - b], core_slot, core)

        return SimpleNamespace(start=start, near=near, far=far_, over=over, wait=wait)

    es_slot, pair_slot = wires.slots(1), wires.slots(4)

    def r_own():
        RW[b, z, y] = rw_ref[...]

    def e_own():
        evens, odds = [], []
        for t in range(FF // 256):
            first = ew_ref[:, 256 * t : 256 * t + 128].astype(F32)
            second = ew_ref[:, 256 * t + 128 : 256 * t + 256].astype(F32)
            evens.append(jnp.where(low_lane, first, pltpu.roll(second, 64, 1)))
            odds.append(jnp.where(low_lane, pltpu.roll(first, 64, 1), second))
        evens, odds = wide(evens).astype(BF16), wide(odds).astype(BF16)
        EW[b, z, y, s] = jnp.where(s == 0, evens, odds)
        ES[...] = jnp.where(s == 0, odds, evens)
        wires.copy(ES, EW.at[b, z, y, s], es_slot, side)

    def e_pair():
        wires.arrived(EW.at[b, z, y, 1 - s], es_slot, side)

    e, r_ = gather_half(EW), gather_half(RW)

    def pair_send():
        wires.copy(x_ref.at[0], PX, pair_slot, side)
        wires.copy(g_ref.at[0], PG, pair_slot + 1, side)

    def pair_wait():
        wires.arrived(PX, pair_slot, side)
        wires.arrived(PG, pair_slot + 1, side)

    kept = {}

    def vecs_step():
        vecs = W1[:, :, :, :, 256:384].reshape(2 * n, r, 128).astype(F32)
        rows = wide([jnp.sum(vecs[8 * t : 8 * t + 8], axis=0) for t in range(D // 128)])
        gain_one, shift_one, bias_c, bias_o = rows[0:1], rows[1:2], rows[2:3], rows[3:4]
        gain_two, shift_two, reduce_bias = rows[4:5], rows[5:6], rows[6:7]
        even = wide([vecs[4 * t] + vecs[4 * t + 2] for t in range(FF // 256)])[7:8]
        odd = wide([vecs[4 * t + 1] + vecs[4 * t + 3] for t in range(FF // 256)])[7:8]
        expand_bias = jnp.where(s == 0, even, odd)

        def own_head(row):
            pairs = jnp.zeros((1, 128), F32)
            for t in range(HEADS // 2):
                pairs = pairs + jnp.where(h // 2 == t, row[:, 128 * t : 128 * t + 128], 0.0)
            turned = pltpu.roll(pairs, HEAD, 1)
            return jnp.where(h % 2 == 0, pairs, turned)

        bias_c, bias_o = own_head(bias_c), own_head(bias_o)
        own_w = W1[:, :, :, :, 0:256].reshape(D, 256)
        kept.update(
            gain_one=gain_one,
            shift_one=shift_one,
            bias_c=bias_c,
            bias_o=bias_o,
            gain_two=gain_two,
            shift_two=shift_two,
            reduce_bias=reduce_bias,
            expand_bias=expand_bias,
            own_w=own_w,
        )

    kv_slot = wires.slots(HEADS // 2)

    def project(*blocks):
        normed, _ = normalize(tall([TOK[k] for k in blocks]).astype(F32))
        normed = (normed * kept["gain_one"] + kept["shift_one"]).astype(BF16)
        out = dot(normed, kept["own_w"])
        query = out[:, 128:]
        first = jnp.where(low_lane, (query + kept["bias_c"]).astype(BF16).astype(F32) * 0.125, 0.0).astype(BF16)
        second = (query + kept["bias_o"]).astype(BF16).astype(F32) * 0.125
        second = pltpu.roll(jnp.where(low_lane, second, 0.0), HEAD, 1).astype(BF16)
        for i, k in enumerate(blocks):
            rows = slice(i * T, i * T + T)
            NRM[k] = normed[rows]
            KV[k * SS + s] = out[rows, :128].astype(BF16)
            wires.copy(KV.at[k * SS + s], KV.at[k * SS + s], kv_slot + k // 2, side)
            QC[k] = first[rows]
            QO[k] = second[rows]

    def far_block(dz):
        far = h ^ (2 * dz + 1)
        wires.arrived(TOK.at[far], far_slot + (z ^ dz), side)
        return far

    def project_steps(near, far):
        project(*[h ^ (2 * dz) for dz in near], *[far_block(dz) for dz in far])

    first_blocks = [functools.partial(project_steps, *blocks) for blocks in (((0,), (0,)), ((1, 2), ()), ((), (1, 2)), ((3,), (3,)))]

    tiles = TAB.shape[0] // T

    parts = 4
    per = tiles // parts

    def offset_part(part):
        if part == 0:
            loads[7].wait()
            for t in range(4):
                OFF[tiles + t] = jnp.zeros((T, 128), BF16)
        rows = slice(part * per * T, (part + 1) * per * T)
        out = dot(TAB[rows, :], kept["own_w"][:, 128:])
        OFF[part * per : (part + 1) * per] = out.astype(BF16).reshape(per, T, 128)

    offs = [functools.partial(offset_part, part) for part in range(parts)]

    tril = iota((T, T), 1) <= iota((T, T), 0)
    diff = iota((T, T), 1) - iota((T, T), 0)
    eye = iota((T, T), 1) == iota((T, T), 0)
    flip = jnp.where(iota((T, T), 0) + iota((T, T), 1) == T - 1, 1.0, 0.0).astype(BF16)
    att_slot = wires.slots(2)

    def forward(k):
        block = k * SS + s
        base = n - 1 - block
        trips = (k * SS + SS + 3) // 4
        qc, qo = QC[k], QO[k]
        seg_row = seg_ref[0:1, pl.ds(pl.multiple_of(block * T, T), T)].astype(F32)
        seg_q = jnp.sum(jnp.where(eye, seg_row, 0.0), axis=1, keepdims=True)
        peak = jnp.full((T, T), NEG, F32)
        for ch in range(trips):
            first = ch * 4
            kv = KV[first : first + 4].reshape(4 * T, 128)
            content = dot_nt(qc, kv)
            window = OFF[pl.ds(base + first, 5)].reshape(5 * T, 128)
            rel = dot_nt(qo, window)
            turned = [pltpu.roll(rel[:, t * T : (t + 1) * T], 1, 1, stride=1, stride_axis=0) for t in range(5)]
            for t in range(4):
                seg_k = seg_ref[0:1, (first + t) * T : (first + t + 1) * T].astype(F32)
                ok = (diff <= (block - first - t) * T) & (seg_k == seg_q)
                score = content[:, t * T : (t + 1) * T] + jnp.where(tril, turned[t], turned[t + 1])
                score = jnp.where(ok, score, NEG)
                SCR[first + t] = score
                peak = jnp.maximum(peak, score)
        peak = jnp.max(peak, axis=1, keepdims=True)
        total, out = jnp.zeros((T, T), F32), jnp.zeros((T, 128), F32)
        for ch in range(trips):
            first = ch * 4
            kv = KV[first : first + 4].reshape(4 * T, 128)
            low = []
            for t in range(4):
                p = jnp.exp(SCR[first + t] - peak)
                total = total + p
                low.append(p.astype(BF16))
            low = wide(low)
            out = out + dot(low, kv)
            turned = dot(flip, low).astype(BF16)
            for t in range(4):
                PST[k, first + t] = turned[:, t * T : (t + 1) * T]
        inverse = 1.0 / jnp.sum(total, axis=1, keepdims=True)
        att = out[:, HEAD:] * inverse
        ATF[k] = att
        LIN[k] = jnp.broadcast_to(inverse, (T, T))
        ATS[k] = fold(att).astype(BF16)
        wires.copy(ATS.at[k], ATR.at[s, h], att_slot, dev(b, k, s), when=h != k)
        wires.copy(ATS.at[k], ATR.at[s, h], att_slot + 1, dev(b, k, 1 - s))

    def keys_wait(pair):
        wires.arrived(KV.at[pair * 2 : pair * 2 + 2], kv_slot + pair, side)

    kv = [functools.partial(keys_wait, pair) for pair in range(HEADS // 2)]
    fwd = [functools.partial(forward, k) for k in range(HEADS)]

    def att_wait():
        ATR[s, h] = ATS[h]
        wires.arrived(ATR.at[s, 0 : HEADS - 1], att_slot, side)
        wires.arrived(ATR.at[1 - s], att_slot + 1, side)

    def by_heads(R):
        return wide([unfold(R[k].astype(F32)) for k in range(HEADS)]).astype(BF16)

    ga_slot = wires.slots(1)
    step = min(512, FF)

    def feed(first, heads_out, tokens, g_low):
        middle = tokens + dot(by_heads(heads_out), MW[...].reshape(D, D))
        normed, inverse = normalize(middle)
        second_low = (normed * kept["gain_two"] + kept["shift_two"]).astype(BF16)
        grad_second = jnp.zeros((T, D), F32)
        root, cube = math.sqrt(2.0 / math.pi), 0.044715
        rows = slice(first, first + T)
        for f in range(FF // 2 // step):
            cols = slice(f * step, f * step + step)
            e_w = EW[:, :, :, :, :, cols].reshape(D, step)
            r_w = RW[...].reshape(FF // 2, D)[cols]
            v = dot(second_low, e_w) + kept["expand_bias"][:, cols]
            tanh = jnp.tanh(root * (v + cube * v * v * v))
            ACT[rows, cols] = (0.5 * v * (1.0 + tanh)).astype(BF16)
            slope = 0.5 * (1.0 + tanh) + 0.5 * v * (1.0 - tanh * tanh) * (root * (1.0 + 3.0 * cube * v * v))
            grad_hidden = (dot_nt(g_low, r_w) * slope).astype(BF16)
            GH[rows, cols] = grad_hidden
            grad_second = grad_second + dot_nt(grad_hidden, e_w)
        return middle, normed, inverse, second_low, grad_second

    def ffn_other():
        _, _, _, second_low, grad_second = feed(T, ATR.at[1 - s], PX[...].astype(F32), PG[...])
        GSS[...] = grad_second.astype(BF16)
        wires.copy(GSS, GSR, pair_slot + 2, side)
        kept["second_other"] = second_low

    def ffn_own():
        middle, normed, inverse, second_low, grad_second = feed(0, ATR.at[s], x_ref[0].astype(F32), g_ref[0])
        kept.update(
            att_low=by_heads(ATR.at[s]),
            second_low=tall([second_low, kept["second_other"]]),
            g_low=tall([g_ref[0], PG[...]]),
            grad_second=grad_second,
            middle=middle,
            n_two=normed,
            inverse_two=inverse,
        )

    def ffn_out():
        output = dot(ACT[...], RW[...].reshape(FF // 2, D))
        OUS[...] = output[T:].astype(BF16)
        kept["output"] = kept["middle"] + kept["reduce_bias"] + output[:T]
        kept["bias_expand"] = colsum(GH[...].astype(F32))

    def ffn_send():
        wires.copy(OUS, OUR, pair_slot + 3, side)

    def ffn_back():
        n_two = kept["n_two"]
        wires.arrived(GSR, pair_slot + 2, side)
        grad_second = kept["grad_second"] + GSR[...].astype(F32)
        g = g_ref[0].astype(F32)
        grad_middle = g + norm_back(grad_second * kept["gain_two"], n_two, kept["inverse_two"])
        middle_low = grad_middle.astype(BF16)
        gradient_ref[0] = grad_middle
        grad_att = dot_nt(middle_low, MW[...].reshape(D, D))
        for k in range(HEADS):
            GAS[k] = fold(grad_att[:, k * HEAD : (k + 1) * HEAD]).astype(BF16)
        for _, peer in heads:
            wires.copy(GAS.at[peer], GAR.at[h], ga_slot, dev(b, peer, s))
        GAR[h] = GAS[h]
        kept.update(
            middle_low=middle_low,
            vec_feed=[colsum(grad_second * n_two), colsum(grad_second), colsum(g)],
        )

    def result_step():
        wires.arrived(OUR, pair_slot + 3, side)
        result_ref[0] = (kept["output"] + OUR[...].astype(F32)).astype(BF16)
        stores[0].start()

    def ga_wait():
        wires.arrived(GAR.at[0 : HEADS - 1], ga_slot, side)

    def add_into(W, index, other):
        W[index] = (W[index].astype(F32) + other.astype(F32)).astype(BF16)

    def scatter(W, C, A, B, Z, Z2, finish):
        slot = wires.slots(5)
        lead = (s,) if A is not None else ()

        def core_():
            wires.copy(W.at[1 - b], C, slot, core)

        def merge():
            wires.arrived(C, slot, core)

            def add(i, carry):
                for j in range(YS):
                    add_into(W, (b, i, j), C[i, j])
                return carry

            lax.fori_loop(0, ZS, add, 0)
            if A is not None:
                wires.copy(W.at[b, :, :, 1 - s], A, slot + 1, side)
            else:
                wires.copy(W.at[b, :, 1 - y], B, slot + 2, flip_y)

        def side_():
            wires.arrived(A, slot + 1, side)

            def add(i, carry):
                for j in range(YS):
                    add_into(W, (b, i, j, s), A[i, j])
                return carry

            lax.fori_loop(0, ZS, add, 0)
            wires.copy(W.at[b, :, 1 - y, s], B, slot + 2, flip_y)

        def plane():
            wires.arrived(B, slot + 2, flip_y)
            for i in range(ZS):
                add_into(W, (b, i, y) + lead, B[i])
            for dz in (1, 3):
                wires.copy(W.at[(b, z ^ dz, y) + lead], Z.at[dz // 2], slot + 3, dev(b, h ^ 2, s))

        def pair():
            wires.arrived(Z, slot + 3, side)
            for i in range(2):
                add_into(W, (b, z ^ (2 * i), y) + lead, Z[i])
            wires.copy(W.at[(b, z ^ 2, y) + lead], Z2, slot + 4, dev(b, h ^ 4, s))

        def total_():
            wires.arrived(Z2, slot + 4, side)
            finish(W[(b, z, y) + lead].astype(F32) + Z2[...].astype(F32))

        return SimpleNamespace(core=core_, merge=merge, side=side_, plane=plane, pair=pair, total=total_)

    def keep_rows(ref, store):
        def put(total):
            ref[...] = total
            store.start()

        return put

    eg_slot = wires.slots(1)

    def swap_columns(total):
        EO[...] = jnp.where(s == 0, total[0], total[1])
        EX[...] = jnp.where(s == 0, total[1], total[0]).astype(BF16)
        wires.copy(EX, EY, eg_slot, side)

    def E_columns():
        wires.arrived(EY, eg_slot, side)
        own, other = EO[...], EY[...].astype(F32)
        even, odd = jnp.where(s == 0, own, other), jnp.where(s == 0, other, own)
        for t in range(FF // 256):
            a_, b_ = even[:, 128 * t : 128 * t + 128], odd[:, 128 * t : 128 * t + 128]
            eg_ref[:, 256 * t : 256 * t + 128] = jnp.where(low_lane, a_, pltpu.roll(b_, 64, 1))
            eg_ref[:, 256 * t + 128 : 256 * t + 256] = jnp.where(low_lane, pltpu.roll(a_, 64, 1), b_)
        stores[2].start()

    def R_make():
        RG[...] = dot_tn(ACT[...], kept["g_low"]).astype(BF16).reshape(RG.shape)

    def E_make():
        for f in range(FF // 2 // step):
            cols = slice(f * step, f * step + step)
            out = dot_tn(kept["second_low"], GH[:, cols])
            EG[:, :, :, :, :, cols] = out.astype(BF16).reshape(2, ZS, YS, SS, r, step)

    def M_make():
        MG[...] = dot_tn(kept["att_low"], kept["middle_low"]).astype(BF16).reshape(MG.shape)

    R = scatter(RG, CR, None, BR, ZR, YR, keep_rows(rg_ref, stores[1]))
    E = scatter(EG, CE, None, BE, ZE, YE, swap_columns)
    M = scatter(MG, CM, AM, BM, ZM, YM, keep_rows(mg_ref, stores[3]))

    cut = iota((T, T), 1) >= iota((T, T), 0)
    low_rows = iota((T, T), 0) < HEAD
    dkv_slot = wires.slots(HEADS)
    rkv_slot, rdq_slot = wires.slots(1), wires.slots(1)

    def zero(t, carry):
        DKVT[t] = jnp.zeros((128, T), F32)
        return carry

    lax.fori_loop(0, n, zero, 0)

    def zero_rows(t, carry):
        DROWT[t] = jnp.zeros((HEAD, T), F32)
        return carry

    lax.fori_loop(0, n + 4, zero_rows, 0)
    JGA[...] = jnp.zeros((D, 256), F32)
    sums = {"c": jnp.zeros((1, 128), F32), "o": jnp.zeros((1, 128), F32), "kv": jnp.zeros((1, 128), F32), "q": jnp.zeros((1, 128), F32)}

    def backward(k):
        block = k * SS + s
        base = n - 1 - block
        trips = (k * SS + SS + 3) // 4
        ga = unfold(GAR[k].astype(F32))
        inverse = LIN[k][:, :1]
        spread = jnp.sum(ga * ATF[k], axis=1, keepdims=True) * inverse
        spread = dot(flip.astype(F32), jnp.broadcast_to(spread, (T, T)), precision=lax.Precision.HIGHEST)
        scaled = (ga * inverse).astype(BF16)
        both = dot(flip, wide([QC[k][:, :HEAD], scaled]))
        ga_pad = jnp.where(low_lane, 0.0, both).astype(BF16)
        both_t = both.T
        left = wide([jnp.where(low_rows, both_t, 0.0), jnp.where(low_rows, 0.0, both_t)]).astype(BF16)
        qo_t = dot(flip, QO[k]).T[HEAD:].astype(BF16)
        dq, dqo = jnp.zeros((T, 128), F32), jnp.zeros((T, 128), F32)
        for ch in range(trips):
            first = ch * 4
            kv = KV[first : first + 4].reshape(4 * T, 128)
            gp = dot_nt(ga_pad, kv)
            low, turned, probs = [], [], []
            for t in range(4):
                p = PST[k, first + t]
                ds = p.astype(F32) * (gp[:, t * T : (t + 1) * T] - spread)
                probs.append(p)
                low.append(ds.astype(BF16))
                turned.append(pltpu.roll(ds, 0, 1, stride=1, stride_axis=0))
            low, probs = wide(low), wide(probs)
            dq = dq + dot(low, kv)
            add = dot(left, tall([low, probs]))
            for t in range(4):
                DKVT[first + t] += add[:, t * T : (t + 1) * T]
            dr = [jnp.where(cut, turned[0], 0.0)]
            for t in range(1, 4):
                dr.append(jnp.where(cut, turned[t], turned[t - 1]))
            dr.append(jnp.where(cut, 0.0, turned[3]))
            dr = wide(dr).astype(BF16)
            window = OFF[pl.ds(base + first, 5)].reshape(5 * T, 128)
            dqo = dqo + dot(dr, window)
            back = dot(qo_t, dr)
            for t in range(5):
                DROWT[base + first + t] += back[:, t * T : (t + 1) * T]
        dqo = pltpu.roll(dqo, HEAD, 1)
        sums["c"] = sums["c"] + colsum(dq) * 0.125
        sums["o"] = sums["o"] + colsum(dqo) * 0.125
        dq = ((dq + dqo) * 0.125).astype(BF16)
        dq = dot(flip, dq)
        DQF[k] = fold(dq[:, :HEAD]).astype(BF16)
        wires.copy(DQF.at[k], RDQ.at[h], rdq_slot, dev(b, k, s), when=h != k)
        DKVS[k] = DKVT[k * SS + 1 - s].T.astype(BF16)
        wires.copy(DKVS.at[k], DKVR.at[k], dkv_slot + k, side)
        return dq

    def settle(k, dq):
        wires.arrived(DKVR.at[k], dkv_slot + k, side)
        dkv = (DKVT[k * SS + s].T + DKVR[k].astype(F32)).astype(BF16)
        DKVF[k] = dkv
        wires.copy(DKVF.at[k], RKV.at[h], rkv_slot, dev(b, k, s), when=h != k)
        sums["kv"] = sums["kv"] + colsum(dkv.astype(F32))
        sums["q"] = sums["q"] + jnp.where(low_lane, colsum(dq), 0.0)
        low = wide([dkv, jnp.where(low_lane, dq, 0.0).astype(BF16)])
        JGA[...] += dot_tn(NRM[k], low)

    lows = {}

    def backward_step(k):
        lows[k] = backward(k)

    def settle_step(k):
        settle(k, lows[k])

    bwd = [functools.partial(backward_step, k) for k in range(HEADS)]
    put = [functools.partial(settle_step, k) for k in range(HEADS)]

    def offset_grad():
        rows_t = wide([DROWT[t] for t in range(tiles)])
        upper = rows_t.astype(BF16)
        lower = (rows_t - upper.astype(F32)).astype(BF16)
        og_t = dot(tall([upper, lower]), TAB[...])
        og = (og_t[:HEAD] + og_t[HEAD:]).T
        kept["og"] = og

    def jg_make():
        og, own_w, gain_one, shift_one = kept["og"], kept["own_w"], kept["gain_one"], kept["shift_one"]
        vec_feed, bias_expand = kept["vec_feed"], kept["bias_expand"]
        RKV[h] = DKVF[h]
        RDQ[h] = DQF[h]
        og = pltpu.roll(wide([og, jnp.zeros((D, HEAD), F32)]), HEAD, 1)
        grads = JGA[...]
        w_f = own_w.astype(F32)
        col_w = jnp.where(iota((D, 256), 1) < 192, w_f, 0.0)
        ones = jnp.ones((8, 256), F32)
        totals = jnp.broadcast_to(wide([sums["kv"], sums["q"]]), (8, 256))
        highest = lax.Precision.HIGHEST
        shift_mixer = dot(totals, col_w, ((1,), (1,)), highest)[0:1]
        gain_mixer = dot(ones, col_w * grads, ((1,), (1,)), highest)[0:1]
        gain_mixer = (gain_mixer - shift_one * shift_mixer) / gain_one

        def place_head(row):
            row = jnp.where(low_lane, row, 0.0)
            row = row + pltpu.roll(row, HEAD, 1)
            row = wide([row] * (D // 128))
            return jnp.where(iota((1, D), 1) // HEAD == h, row, 0.0)

        partial = tall(
            [gain_mixer, shift_mixer, place_head(sums["c"]), place_head(sums["o"])]
            + vec_feed
            + [jnp.zeros((9, D), F32)]
        )
        row_index = iota((r, 128), 0)
        last = wide([grads[:, :128], grads[:, 128:] + og]).astype(BF16).reshape(2, HEADS, SS, r, 256)
        for b_ in range(2):
            for k in range(HEADS):
                for s_ in range(SS):
                    d_ = (b_ * HEADS + k) * SS + s_
                    tile = partial[:, d_ // 8 * 128 : d_ // 8 * 128 + 128]
                    if d_ % 8:
                        tile = pltpu.roll(tile, 128 - d_ % 8 * 16, 1)
                    bias = bias_expand[:, d_ // 4 * 128 : d_ // 4 * 128 + 128]
                    if d_ // 2 % 2:
                        bias = pltpu.roll(bias, 64, 1)
                    bias = jnp.where(s == s_, bias, 0.0)
                    tile = jnp.where(row_index == 7, bias, tile)
                    JGM[b_, k, s_] = wide([last[b_, k, s_], tile.astype(BF16)])
        wires.copy(JGM.at[1 - b], JRC, jr_slot, core)

    jr_slot, jf_slot = wires.slots(2), wires.slots(1)

    def jg_core():
        wires.arrived(JRC, jr_slot, core)
        JGX[...] = (JGM[b, :, 1 - s].astype(F32) + JRC[:, 1 - s].astype(F32)).astype(BF16)
        wires.copy(JGX, JRS, jr_slot + 1, side)

    def jg_side():
        total = JGM[b, :, s].astype(F32) + JRC[:, s].astype(F32)
        wires.arrived(JRS, jr_slot + 1, side)
        JF[...] = (total + JRS[...].astype(F32)).astype(BF16)
        for _, peer in heads:
            wires.copy(JF.at[peer], JR2.at[h], jf_slot, dev(b, peer, s))
        JR2[h] = JF[h]

    def rkv_wait():
        wires.arrived(RKV.at[0 : HEADS - 1], rkv_slot, side)
        wires.arrived(RDQ.at[0 : HEADS - 1], rdq_slot, side)

    def grad_step():
        gain_one = kept["gain_one"]
        x = x_ref[0].astype(F32)
        pieces_k, pieces_v = [], []
        for k in range(0, HEADS, 2):
            a_, b_ = RKV[k].astype(F32), RKV[k + 1].astype(F32)
            pieces_k.append(jnp.where(low_lane, a_, pltpu.roll(b_, HEAD, 1)))
            pieces_v.append(jnp.where(low_lane, pltpu.roll(a_, HEAD, 1), b_))
        grad_joint = wide([by_heads(RDQ), wide(pieces_k).astype(BF16), wide(pieces_v).astype(BF16)])
        joint_w = JW[...].reshape(D, 3 * D)
        grad_normed = dot_nt(grad_joint, joint_w)
        n_one, inverse_one = normalize(x)
        gradient_ref[0] += norm_back(grad_normed * gain_one, n_one, inverse_one)
        stores[4].start()

    def jg_wait():
        wires.arrived(JR2.at[0 : HEADS - 1], jf_slot, side)

    def outs_step():
        got = [JR2[k].astype(F32) for k in range(HEADS)]
        jg_ref[...] = wide([a[:, 128:192] for a in got] + [a[:, 0:64] for a in got] + [a[:, 64:128] for a in got])
        og_ref[...] = wide([a[:, 192:256] for a in got])
        vectors = got[0][:, 256:]
        for a in got[1:]:
            vectors = vectors + a[:, 256:]
        vg_ref[...] = vectors
        for store in stores[5:]:
            store.start()

    def reap():
        wires.reap(12)

    order = (
        w1_send,
        x_send,
        m.own,
        e_own,
        r_own,
        w1_pass,
        pair_send,
        x_near,
        e_pair,
        e.start,
        w1_core,
        x_far,
        m.start,
        r_.start,
        w1_wait,
        vecs_step,
        first_blocks[0],
        first_blocks[1],
        offs[0],
        offs[1],
        offs[2],
        offs[3],
        first_blocks[2],
        first_blocks[3],
        e.near,
        m.near,
        kv[0],
        fwd[0],
        fwd[1],
        e.far,
        m.far,
        kv[1],
        kv[2],
        fwd[4],
        fwd[5],
        r_.near,
        kv[3],
        fwd[6],
        fwd[7],
        r_.far,
        m.diag,
        e.over,
        fwd[2],
        fwd[3],
        m.over,
        r_.over,
        reap,
        m.wait,
        e.wait,
        r_.wait,
        pair_wait,
        att_wait,
        ffn_other,
        j.own,
        j.start,
        ffn_own,
        R_make,
        R.core,
        E_make,
        E.core,
        reap,
        ffn_back,
        j.near,
        ffn_out,
        ffn_send,
        M_make,
        M.core,
        M.merge,
        j.far,
        ga_wait,
        R.merge,
        E.merge,
        bwd[7],
        bwd[6],
        j.diag,
        bwd[5],
        put[7],
        bwd[4],
        R.plane,
        put[6],
        M.side,
        bwd[3],
        put[5],
        bwd[2],
        E.plane,
        put[4],
        R.pair,
        j.over,
        bwd[1],
        M.plane,
        put[3],
        bwd[0],
        offset_grad,
        put[2],
        put[1],
        put[0],
        jg_make,
        R.total,
        E.pair,
        M.pair,
        jg_core,
        jg_side,
        result_step,
        j.wait,
        rkv_wait,
        grad_step,
        E.total,
        M.total,
        reap,
        jg_wait,
        outs_step,
        reap,
        E_columns,
    )
    for step_ in order:
        step_()
    wires.reap()
    for store in stores:
        store.wait()


def spread_refs(n, *refs):
    layer_kernel(n, refs[:9], refs[9:17], refs[17:25], *refs[25:])


def hand_over(*refs):
    count = (len(refs) - 9) // 2
    ins, vectors, outs, smalls = refs[:count], refs[count], refs[count + 1 : 2 * count + 1], refs[2 * count + 1 :]
    for a, o in zip(ins, outs):
        o[...] = a[...]
    for i, o in enumerate(smalls):
        o[...] = vectors[i, 0 : o.shape[0]]


def table_reversed(length, width):
    half = width // 2
    freq = 10000.0 ** (-2.0 * np.arange(half) / width)
    angle = np.arange(length - 1, -1, -1)[:, None] * freq[None, :]
    return np.concatenate([np.sin(angle), np.cos(angle)], axis=1).astype(np.float32).astype(ml_dtypes.bfloat16)


def fast(
    n,
    inputs,
    segments,
    mixer_gain,
    mixer_shift,
    joint_weight,
    offset_weight,
    content_bias,
    offset_bias,
    merge_weight,
    feed_gain,
    feed_shift,
    expand_weight,
    expand_bias,
    reduce_weight,
    reduce_bias,
    cotangent,
):
    T, D = inputs.shape[1:]
    r = joint_weight.shape[0]
    FF = expand_weight.shape[1]
    rr = reduce_weight.shape[0]
    length = segments.shape[1]
    vecs = [mixer_gain, mixer_shift, content_bias, offset_bias, feed_gain, feed_shift, reduce_bias, expand_bias]
    table = jnp.asarray(table_reversed(length, D))
    V = pltpu.VMEM
    half = FF // 2
    blocks, folded = (HEADS, T, 128), (HEADS, T // 2, 128)
    scratch = [
        V((length, D), BF16),
        V((HEADS, T, D), BF16),
        V((HEADS, T, D), BF16),
        V((HEADS, r, 384), BF16),
        V((2, HEADS, SS, r, 384), BF16),
        V((2, ZS, YS, SS, r, 3 * D), BF16),
        V((2, ZS, YS, SS, r, D), BF16),
        V((2, ZS, YS, SS, r, half), BF16),
        V((2, ZS, YS, rr, D), BF16),
        V((r, half), BF16),
        V((T, D), BF16),
        V((T, D), BF16),
        V((n, T, 128), BF16),
        V(blocks, BF16),
        V(blocks, BF16),
        V((n + 4, T, 128), BF16),
        V((n, T, T), F32),
        V((HEADS, n, T, T), BF16),
        V((HEADS, T, HEAD), F32),
        V((HEADS, T, T), F32),
        V(folded, BF16),
        V((SS,) + folded, BF16),
        V((2 * T, half), BF16),
        V((2 * T, half), BF16),
        V((T, D), BF16),
        V((T, D), BF16),
        V((T, D), BF16),
        V((T, D), BF16),
        V(folded, BF16),
        V(folded, BF16),
        V((n, 128, T), F32),
        V((n + 4, HEAD, T), F32),
        V(blocks, BF16),
        V(blocks, BF16),
        V(blocks, BF16),
        V(folded, BF16),
        V(blocks, BF16),
        V(folded, BF16),
        V((2, ZS, YS, SS, r, D), BF16),
        V((2, ZS, YS, SS, r, half), BF16),
        V((2, ZS, YS, rr, D), BF16),
        V((ZS, YS, SS, r, D), BF16),
        V((ZS, YS, SS, r, half), BF16),
        V((ZS, YS, rr, D), BF16),
        V((ZS, YS, r, D), BF16),
        V((ZS, r, D), BF16),
        V((ZS, SS, r, half), BF16),
        V((ZS, rr, D), BF16),
        V((2, r, D), BF16),
        V((2, SS, r, half), BF16),
        V((2, rr, D), BF16),
        V((r, D), BF16),
        V((SS, r, half), BF16),
        V((rr, D), BF16),
        V((r, half), F32),
        V((r, half), BF16),
        V((r, half), BF16),
        V((D, 256), F32),
        V((2, HEADS, SS, r, 384), BF16),
        V((HEADS, SS, r, 384), BF16),
        V((HEADS, r, 384), BF16),
        V((HEADS, r, 384), BF16),
        V((HEADS, r, 384), BF16),
        V((HEADS, r, 384), BF16),
        V((1, T, D), BF16),
        V((r, 3 * D), BF16),
        V((r, D), BF16),
        V((1, T, D), BF16),
        V((r, FF), BF16),
        V((r, D), BF16),
        V((rr, D), BF16),
    ]
    out_shape = [
        jax.ShapeDtypeStruct((1, T, D), BF16),
        jax.ShapeDtypeStruct((rr, D), F32),
        jax.ShapeDtypeStruct((r, FF), F32),
        jax.ShapeDtypeStruct((r, D), F32),
        jax.ShapeDtypeStruct((1, T, D), F32),
        jax.ShapeDtypeStruct((r, 3 * D), F32),
        jax.ShapeDtypeStruct((r, D), F32),
        jax.ShapeDtypeStruct((r, 128), F32),
    ]
    scratch += [V(a.shape, a.dtype) for a in out_shape]
    scratch += [pltpu.SemaphoreType.DMA((count,)) for count in (9, SENDS, RECVS)]
    scratch += [V(a.shape, a.dtype) for a in (segments, *vecs)]
    vmem, hbm = pl.BlockSpec(memory_space=V), pl.BlockSpec(memory_space=pl.ANY)
    outs = pl.pallas_call(
        functools.partial(spread_refs, n),
        out_shape=out_shape,
        in_specs=[hbm] * 17,
        out_specs=[hbm] * 8,
        scratch_shapes=scratch,
        compiler_params=pltpu.CompilerParams(
            collective_id=0, has_side_effects=True, vmem_limit_bytes=60 * 2**20
        ),
    )(
        segments,
        *vecs,
        inputs,
        joint_weight,
        offset_weight,
        cotangent,
        expand_weight,
        merge_weight,
        reduce_weight,
        table,
    )
    big, vg = outs[:-1], outs[-1]
    final = pl.pallas_call(
        hand_over,
        out_shape=[jax.ShapeDtypeStruct(a.shape, a.dtype) for a in big]
        + [jax.ShapeDtypeStruct(v.shape, F32) for v in vecs],
        in_specs=[vmem] * (len(big) + 1),
        out_specs=[vmem] * (len(big) + len(vecs)),
    )(*big, vg)
    result, rg, eg, mg, gradient, jg, og = final[: len(big)]
    gain_m, shift_m, bias_c, bias_o, gain_f, shift_f, bias_r, bias_e = final[len(big) :]
    return (
        result,
        gradient,
        gain_m,
        shift_m,
        jg,
        og,
        bias_c,
        bias_o,
        mg,
        gain_f,
        shift_f,
        eg,
        bias_e,
        rg,
        bias_r,
    )


def solution(mesh):
    in_specs = (
        P("batch", "ctx", None),
        P("batch", None),
        P(("batch", "ctx")),
        P(("batch", "ctx")),
        P(("batch", "ctx"), None),
        P(("batch", "ctx"), None),
        P(("batch", "ctx")),
        P(("batch", "ctx")),
        P(("batch", "ctx"), None),
        P(("batch", "ctx")),
        P(("batch", "ctx")),
        P(("batch", "ctx"), None),
        P(("batch", "ctx")),
        P(("batch", "ctx"), None),
        P(("batch", "ctx")),
        P("batch", "ctx", None),
    )
    out_specs = (
        P("batch", "ctx", None),
        P("batch", "ctx", None),
        P(("batch", "ctx")),
        P(("batch", "ctx")),
        P(("batch", "ctx"), None),
        P(("batch", "ctx"), None),
        P(("batch", "ctx")),
        P(("batch", "ctx")),
        P(("batch", "ctx"), None),
        P(("batch", "ctx")),
        P(("batch", "ctx")),
        P(("batch", "ctx"), None),
        P(("batch", "ctx")),
        P(("batch", "ctx"), None),
        P(("batch", "ctx")),
    )
    n, cores = mesh.shape["ctx"], mesh.shape["batch"]

    def layer(*args):
        suits = n == HEADS * SS and cores == 2 and args[0].shape[1] == 128 and args[4].shape[0] == 16
        return fast(n, *args) if suits else local(*args)

    return jax.shard_map(layer, mesh=mesh, in_specs=in_specs, out_specs=out_specs, check_vma=False)
```

```python
import functools
import math
from types import SimpleNamespace

import jax
import jax.numpy as jnp
import ml_dtypes
import numpy as np
from jax import lax
from jax.experimental import pallas as pl
from jax.experimental.pallas import tpu as pltpu
from jax.sharding import PartitionSpec as P

HEADS = 8
HEAD = 64


masked_score = -1e30


def shifted(array, axis, by):
    peers = lax.axis_size(axis)
    pairs = [(i, i + by) for i in range(peers) if 0 <= i + by < peers]
    return lax.ppermute(array, axis, pairs)


def shifted_2(value, axis, steps):
    count = lax.axis_size(axis)
    pairs = [(source, (source + steps) % count) for source in range(count)]
    return lax.ppermute(value, axis, pairs)


def layer_norm(values, gain, shift):
    center = values - jnp.mean(values, axis=-1, keepdims=True)
    spread = jnp.mean(center * center, axis=-1, keepdims=True)
    return center * lax.rsqrt(spread + 1e-05) * gain + shift


def sinusoid(first, count, width):
    half = width // 2
    freq = jnp.power(10000.0, -2.0 * jnp.arange(half, dtype=jnp.float32) / width)
    place = (first + jnp.arange(count, dtype=jnp.int32)).astype(jnp.float32)
    angle = place[:, None] * freq[None, :]
    return jnp.concatenate([jnp.sin(angle), jnp.cos(angle)], axis=1)


def contract_rows(left, right):
    return lax.dot_general(
        left, right, (((0,), (0,)), ((), ())), preferred_element_type=jnp.float32
    )


def contract_cols(left, right):
    return lax.dot_general(
        left, right, (((1,), (1,)), ((), ())), preferred_element_type=jnp.float32
    )


def split_contract(table, grad_rows):
    upper = grad_rows.astype(jnp.bfloat16)
    lower = (grad_rows - upper.astype(jnp.float32)).astype(jnp.bfloat16)
    return contract_rows(table, upper) + contract_rows(table, lower)


def fold_blocks(step, carry, pieces, limit):
    count = pieces[0].shape[0]
    size = min(count, limit)
    number = count // size
    stacked = tuple((item.reshape((number, size) + item.shape[1:]) for item in pieces))

    def inner(state, item):
        offset, parts = item
        return (step(state, parts, offset * size), None)

    folded, _ = lax.scan(inner, carry, (jnp.arange(number, dtype=jnp.int32), stacked))
    return folded


def realign(relative_scores, count):
    heads, rows, width = relative_scores.shape
    flat = relative_scores.reshape(heads, rows * width)
    band = flat[:, rows - 1 : rows - 1 + rows * (width - 1)]
    return band.reshape(heads, rows, width - 1)[:, :, :count]


def pair_terms(
    query_content_term, query_position_term, keys, query_first, key_first, seg_row, offsets_pad
):
    rows, heads, size = query_content_term.shape
    count = keys.shape[0]
    length = offsets_pad.shape[0] // 2
    anchor = query_first - key_first - count + length
    attention_span = lax.dynamic_slice_in_dim(offsets_pad, anchor, rows + count, 0)[::-1].reshape(
        rows + count, heads, size
    )
    content = jnp.einsum(
        "ahd,bhd->hab", query_content_term, keys, preferred_element_type=jnp.float32
    )
    relative_scores = jnp.einsum(
        "scx,icx->csi", query_position_term, attention_span, preferred_element_type=jnp.float32
    )
    scores = (content + realign(relative_scores, count)) * (1.0 / math.sqrt(size))
    query_seg = lax.dynamic_slice_in_dim(seg_row, query_first, rows, 0)
    key_seg = lax.dynamic_slice_in_dim(seg_row, key_first, count, 0)
    query_pos = query_first + jnp.arange(rows, dtype=jnp.int32)
    key_pos = key_first + jnp.arange(count, dtype=jnp.int32)
    allowed = (key_pos[None, :] <= query_pos[:, None]) & (key_seg[None, :] == query_seg[:, None])
    return (scores, allowed, attention_span, anchor)


def pair_grads(
    query_content_term,
    query_position_term,
    keys,
    values,
    query_first,
    key_first,
    seg_row,
    offsets_pad,
    logsum,
    spread,
    grad_attended,
):
    rows, heads, size = query_content_term.shape
    count = keys.shape[0]
    scale = 1.0 / math.sqrt(size)
    scores, allowed, attention_span, anchor = pair_terms(
        query_content_term, query_position_term, keys, query_first, key_first, seg_row, offsets_pad
    )
    probs = jnp.where(allowed[None], jnp.exp(scores - logsum[..., None]), 0.0)
    grad_values = jnp.einsum(
        "hab,ahd->bhd",
        probs.astype(jnp.bfloat16),
        grad_attended,
        preferred_element_type=jnp.float32,
    )
    grad_probs = jnp.einsum(
        "ahd,bhd->hab", grad_attended, values, preferred_element_type=jnp.float32
    )
    grad_scores = (probs * (grad_probs - spread[..., None])).astype(jnp.bfloat16)
    grad_content = scale * jnp.einsum(
        "hab,bhd->ahd", grad_scores, keys, preferred_element_type=jnp.float32
    )
    grad_keys = scale * jnp.einsum(
        "hab,ahd->bhd", grad_scores, query_content_term, preferred_element_type=jnp.float32
    )
    blank = jnp.zeros((heads, rows, rows + count), jnp.float32)
    _, realign_back = jax.vjp(lambda relative_scores: realign(relative_scores, count), blank)
    gradient_relative_scores = realign_back(grad_scores.astype(jnp.float32))[0].astype(jnp.bfloat16)
    grad_offset = scale * jnp.einsum(
        "nsk,kno->sno", gradient_relative_scores, attention_span, preferred_element_type=jnp.float32
    )
    grad_window = scale * jnp.einsum(
        "cqu,qcn->ucn",
        gradient_relative_scores,
        query_position_term,
        preferred_element_type=jnp.float32,
    )
    grad_window = grad_window.reshape(rows + count, heads * size)[::-1]
    return (grad_content, grad_offset, grad_keys, grad_values, grad_window, anchor)


def add_window(grad_rows, grad_window, anchor):
    current = lax.dynamic_slice_in_dim(grad_rows, anchor, grad_window.shape[0], 0)
    return lax.dynamic_update_slice_in_dim(grad_rows, current + grad_window, anchor, 0)


def local(
    inputs,
    segments,
    mixer_gain,
    mixer_shift,
    joint_weight,
    offset_weight,
    content_bias,
    offset_bias,
    merge_weight,
    feed_gain,
    feed_shift,
    expand_weight,
    expand_bias,
    reduce_weight,
    reduce_bias,
    cotangent,
):
    (
        first_gain,
        first_shift,
        joint_matrix,
        offset_matrix,
        bias_content,
        bias_position,
        merge_matrix,
    ) = (
        lax.all_gather(mixer_gain, ("batch", "ctx"), axis=0, tiled=True),
        lax.all_gather(mixer_shift, ("batch", "ctx"), axis=0, tiled=True),
        lax.all_gather(joint_weight, ("batch", "ctx"), axis=0, tiled=True),
        lax.all_gather(offset_weight, ("batch", "ctx"), axis=0, tiled=True),
        lax.all_gather(content_bias, ("batch", "ctx"), axis=0, tiled=True),
        lax.all_gather(offset_bias, ("batch", "ctx"), axis=0, tiled=True),
        lax.all_gather(merge_weight, ("batch", "ctx"), axis=0, tiled=True),
    )
    tokens = inputs[0].astype(jnp.float32)
    rows, width = tokens.shape
    seg_row = segments[0]
    length = seg_row.shape[0]
    place = lax.axis_index("ctx")
    cycle = lax.axis_size("ctx")
    block_first = place * rows
    heads_shape = (rows, HEADS, HEAD)
    gain_one = first_gain.astype(jnp.float32)
    shift_one = first_shift.astype(jnp.float32)
    normed = layer_norm(tokens, gain_one, shift_one)
    normed_low = normed.astype(jnp.bfloat16)
    joint = jnp.dot(normed_low, joint_matrix, preferred_element_type=jnp.float32)
    query = joint[:, :width]
    keys = joint[:, width : 2 * width].astype(jnp.bfloat16).reshape(heads_shape)
    values = joint[:, 2 * width :].astype(jnp.bfloat16).reshape(heads_shape)
    query_content_term = (
        (query + bias_content.astype(jnp.float32)).astype(jnp.bfloat16).reshape(heads_shape)
    )
    query_position_term = (
        (query + bias_position.astype(jnp.float32)).astype(jnp.bfloat16).reshape(heads_shape)
    )
    everyone = lax.axis_size(("batch", "ctx"))
    share = length // everyone
    table = sinusoid(lax.axis_index(("batch", "ctx")) * share, share, width).astype(jnp.bfloat16)
    offsets_local = jnp.dot(table, offset_matrix, preferred_element_type=jnp.float32).astype(
        jnp.bfloat16
    )
    offsets_all = lax.all_gather(offsets_local, ("batch", "ctx"), axis=0, tiled=True)
    offsets_pad = jnp.concatenate([jnp.zeros_like(offsets_all), offsets_all], axis=0)

    def stats_block(carry, pieces, start):
        peak, total = carry
        scores, allowed, attention_span, anchor = pair_terms(
            query_content_term,
            query_position_term,
            pieces[0],
            block_first,
            start,
            seg_row,
            offsets_pad,
        )
        masked = jnp.where(allowed[None], scores, masked_score)
        new_peak = jnp.maximum(peak, jnp.max(masked, axis=-1))
        added = jnp.sum(
            jnp.where(allowed[None], jnp.exp(masked - new_peak[..., None]), 0.0), axis=-1
        )
        return (new_peak, total * jnp.exp(peak - new_peak) + added)

    peak_start = jnp.full((HEADS, rows), masked_score, jnp.float32)
    total_start = jnp.zeros((HEADS, rows), jnp.float32)
    peak, total = fold_blocks(
        stats_block,
        (peak_start, total_start),
        (lax.all_gather(keys, "ctx", axis=0, tiled=True),),
        rows,
    )
    logsum = peak + jnp.log(total)

    def output_block(carry, pieces, start):
        scores, allowed, attention_span, anchor = pair_terms(
            query_content_term,
            query_position_term,
            pieces[0],
            block_first,
            start,
            seg_row,
            offsets_pad,
        )
        probs = jnp.where(allowed[None], jnp.exp(scores - logsum[..., None]), 0.0).astype(
            jnp.bfloat16
        )
        return carry + jnp.einsum(
            "hab,bhd->ahd", probs, pieces[1], preferred_element_type=jnp.float32
        )

    mixed = fold_blocks(
        output_block,
        jnp.zeros(heads_shape, jnp.float32),
        (
            lax.all_gather(keys, "ctx", axis=0, tiled=True),
            lax.all_gather(values, "ctx", axis=0, tiled=True),
        ),
        rows,
    )
    attended_low = mixed.reshape(rows, width).astype(jnp.bfloat16)
    middle = tokens + jnp.dot(attended_low, merge_matrix, preferred_element_type=jnp.float32)
    second_gain, second_shift, expand_matrix, expand_vector, reduce_matrix, reduce_vector = (
        lax.all_gather(feed_gain, ("batch", "ctx"), axis=0, tiled=True),
        lax.all_gather(feed_shift, ("batch", "ctx"), axis=0, tiled=True),
        lax.all_gather(expand_weight, ("batch", "ctx"), axis=0, tiled=True),
        lax.all_gather(expand_bias, ("batch", "ctx"), axis=0, tiled=True),
        lax.all_gather(reduce_weight, ("batch", "ctx"), axis=0, tiled=True),
        lax.all_gather(reduce_bias, ("batch", "ctx"), axis=0, tiled=True),
    )
    gain_two = second_gain.astype(jnp.float32)
    shift_two = second_shift.astype(jnp.float32)
    second_low = layer_norm(middle, gain_two, shift_two).astype(jnp.bfloat16)
    hidden = jnp.dot(
        second_low, expand_matrix, preferred_element_type=jnp.float32
    ) + expand_vector.astype(jnp.float32)
    active_low = jax.nn.gelu(hidden, approximate=True).astype(jnp.bfloat16)
    output = (
        middle
        + jnp.dot(active_low, reduce_matrix, preferred_element_type=jnp.float32)
        + reduce_vector.astype(jnp.float32)
    )
    result = output.astype(jnp.bfloat16)[None]
    grad_out = cotangent[0]
    grad_outf = grad_out.astype(jnp.float32)
    grad_reduce_bias = jnp.sum(grad_outf, axis=0)
    grad_reduce = contract_rows(active_low, grad_out)
    grad_active = contract_cols(grad_out, reduce_matrix)
    _, gelu_back = jax.vjp(lambda value: jax.nn.gelu(value, approximate=True), hidden)
    grad_hidden = gelu_back(grad_active)[0].astype(jnp.bfloat16)
    grad_expand_bias = jnp.sum(grad_hidden.astype(jnp.float32), axis=0)
    grad_expand = contract_rows(second_low, grad_hidden)
    grad_second = contract_cols(grad_hidden, expand_matrix)
    _, second_back = jax.vjp(layer_norm, middle, gain_two, shift_two)
    grad_mid, grad_gain_two, grad_shift_two = second_back(grad_second)
    grad_middle = grad_outf + grad_mid
    feed_sums = (
        lax.psum_scatter(grad_gain_two, ("batch", "ctx"), scatter_dimension=0, tiled=True),
        lax.psum_scatter(grad_shift_two, ("batch", "ctx"), scatter_dimension=0, tiled=True),
        lax.psum_scatter(grad_expand, ("batch", "ctx"), scatter_dimension=0, tiled=True),
        lax.psum_scatter(grad_expand_bias, ("batch", "ctx"), scatter_dimension=0, tiled=True),
        lax.psum_scatter(grad_reduce, ("batch", "ctx"), scatter_dimension=0, tiled=True),
        lax.psum_scatter(grad_reduce_bias, ("batch", "ctx"), scatter_dimension=0, tiled=True),
    )
    middle_low = grad_middle.astype(jnp.bfloat16)
    grad_merge = contract_rows(attended_low, middle_low)
    grad_attended = (
        contract_cols(middle_low, merge_matrix).astype(jnp.bfloat16).reshape(heads_shape)
    )
    spread = jnp.einsum("ahd,ahd->ha", grad_attended.astype(jnp.float32), mixed)
    zero_heads = jnp.zeros(heads_shape, jnp.float32)
    zero_rows = jnp.zeros((2 * length, width), jnp.float32)

    def cycle_step(turn, carry):
        visiting, carried, grad_content, grad_offset, grad_rows = carry
        owner = (place - turn) % cycle
        terms = pair_grads(
            query_content_term,
            query_position_term,
            visiting[0],
            visiting[1],
            block_first,
            owner * rows,
            seg_row,
            offsets_pad,
            logsum,
            spread,
            grad_attended,
        )
        carried = carried + jnp.stack([terms[2], terms[3]])
        grad_rows = add_window(grad_rows, terms[4], terms[5])
        visiting = shifted(visiting, "ctx", 1)
        carried = shifted_2(carried.astype(jnp.bfloat16), "ctx", 1).astype(carried.dtype)
        return (visiting, carried, grad_content + terms[0], grad_offset + terms[1], grad_rows)

    start_state = (
        jnp.stack([keys, values]),
        jnp.zeros((2,) + heads_shape, jnp.float32),
        zero_heads,
        zero_heads,
        zero_rows,
    )
    _, carried, grad_content, grad_offset, grad_rows = lax.fori_loop(
        0, cycle, cycle_step, start_state
    )
    grad_keys = carried[0]
    grad_values = carried[1]
    grad_content_bias = jnp.sum(grad_content, axis=0).reshape(width)
    gradient_position_bias = jnp.sum(grad_offset, axis=0).reshape(width)
    grad_joint = jnp.concatenate(
        [
            (grad_content + grad_offset).reshape(rows, width),
            grad_keys.reshape(rows, width),
            grad_values.reshape(rows, width),
        ],
        axis=1,
    ).astype(jnp.bfloat16)
    grad_joint_matrix = contract_rows(normed_low, grad_joint)
    grad_normed = contract_cols(grad_joint, joint_matrix)
    _, first_back = jax.vjp(layer_norm, tokens, gain_one, shift_one)
    grad_tokens, grad_gain_one, grad_shift_one = first_back(grad_normed)
    gradient = (grad_middle + grad_tokens)[None]
    full_table = sinusoid(0, length, width).astype(jnp.bfloat16)
    grad_offset_matrix = split_contract(full_table, grad_rows[length:])
    mixer_sums = (
        lax.psum_scatter(grad_gain_one, ("batch", "ctx"), scatter_dimension=0, tiled=True),
        lax.psum_scatter(grad_shift_one, ("batch", "ctx"), scatter_dimension=0, tiled=True),
        lax.psum_scatter(grad_joint_matrix, ("batch", "ctx"), scatter_dimension=0, tiled=True),
        lax.psum_scatter(grad_offset_matrix, ("batch", "ctx"), scatter_dimension=0, tiled=True),
        lax.psum_scatter(grad_content_bias, ("batch", "ctx"), scatter_dimension=0, tiled=True),
        lax.psum_scatter(gradient_position_bias, ("batch", "ctx"), scatter_dimension=0, tiled=True),
        lax.psum_scatter(grad_merge, ("batch", "ctx"), scatter_dimension=0, tiled=True),
    )
    return (
        result,
        gradient,
        mixer_sums[0],
        mixer_sums[1],
        mixer_sums[2],
        mixer_sums[3],
        mixer_sums[4],
        mixer_sums[5],
        mixer_sums[6],
        feed_sums[0],
        feed_sums[1],
        feed_sums[2],
        feed_sums[3],
        feed_sums[4],
        feed_sums[5],
    )


F32, BF16 = jnp.float32, jnp.bfloat16
MESH = pl.DeviceIdType.MESH
NEG = -1e30
ZS, YS, SS = 4, 2, 2


def dot(a, b, dims=((1,), (0,)), precision=None):
    return lax.dot_general(a, b, (dims, ((), ())), preferred_element_type=F32, precision=precision)


def dot_nt(a, b):
    return dot(a, b, ((1,), (1,)))


def dot_tn(a, b):
    return dot(a, b, ((0,), (0,)))


def iota(shape, axis):
    return lax.broadcasted_iota(jnp.int32, shape, axis)


def wide(tiles):
    return jnp.concatenate(tiles, axis=1)


def tall(tiles):
    return jnp.concatenate(tiles, axis=0)


def fold(x):
    half = x.shape[0] // 2
    return wide([x[:half], x[half:]])


def unfold(x):
    return tall([x[:, :HEAD], x[:, HEAD:]])


def normalize(x):
    center = x - jnp.mean(x, axis=-1, keepdims=True)
    inverse = lax.rsqrt(jnp.mean(center * center, axis=-1, keepdims=True) + 1e-05)
    return center * inverse, inverse


def norm_back(e, n, inverse):
    return inverse * (e - jnp.mean(e, axis=-1, keepdims=True) - n * jnp.mean(e * n, axis=-1, keepdims=True))


def colsum(x):
    return jnp.sum(x, axis=0, keepdims=True)


class Wires:
    def __init__(self, sends, recvs):
        self.sends, self.recvs, self.received, self.pending = sends, recvs, 0, []
        self.free = list(range(SENDS))
        self.peak = 0

    def slots(self, count):
        first = self.received
        self.received += count
        return first

    def copy(self, src, dst, slot, to, when=None):
        index = self.free.pop(0)
        self.peak = max(self.peak, SENDS - len(self.free))
        made = pltpu.make_async_remote_copy(
            src_ref=src,
            dst_ref=dst,
            send_sem=self.sends.at[index],
            recv_sem=self.recvs.at[slot],
            device_id=to,
            device_id_type=MESH,
        )
        self.pending.append((made, when, index))
        if when is None:
            made.start()
        else:
            pl.when(when)(made.start)

    def arrived(self, dst, slot, to):
        pltpu.make_async_remote_copy(
            src_ref=dst,
            dst_ref=dst,
            send_sem=self.sends.at[0],
            recv_sem=self.recvs.at[slot],
            device_id=to,
            device_id_type=MESH,
        ).wait_recv()

    def reap(self, keep=0):
        count = len(self.pending) - keep
        for made, when, index in self.pending[:count]:
            if when is None:
                made.wait_send()
            else:
                pl.when(when)(made.wait_send)
            self.free.append(index)
        self.pending = self.pending[count:]


SENDS, RECVS = 104, 74
def layer_kernel(
    n,
    small,
    ins,
    outs,
    *scratch,
):
    (
        TAB,
        TOK,
        NRM,
        W1S,
        W1,
        JW,
        MW,
        EW,
        RW,
        ES,
        PX,
        PG,
        KV,
        QC,
        QO,
        QCT,
        QOT,
        OFF,
        SCR,
        PST,
        ATF,
        LIN,
        ATS,
        ATR,
        ACT,
        GH,
        GSS,
        GSR,
        OUS,
        OUR,
        GAS,
        GAR,
        DKVT,
        DROWT,
        DKVS,
        DKVR,
        DKVF,
        DQF,
        RKV,
        RDQ,
        MG,
        EG,
        RG,
        CM,
        CE,
        CR,
        AM,
        BM,
        BE,
        BR,
        ZM,
        ZE,
        ZR,
        YM,
        YE,
        YR,
        EO,
        EX,
        EY,
        JGA,
        JGM,
        JRC,
        JGX,
        JRS,
        JF,
        JR2,
        x_ref,
        jw_ref,
        ow_ref,
        g_ref,
        ew_ref,
        mw_ref,
        rw_ref,
        result_ref,
        rg_ref,
        eg_ref,
        mg_ref,
        gradient_ref,
        jg_ref,
        og_ref,
        vg_ref,
        local,
        sends,
        recvs,
        seg_ref,
        *vec_refs,
    ) = scratch
    T = x_ref.shape[1]
    D = x_ref.shape[2]
    FF = ew_ref.shape[1]
    r = jw_ref.shape[0]
    b = lax.axis_index("batch")
    c = lax.axis_index("ctx")
    h, s = c // SS, c % SS
    z, y = h // YS, h % YS
    shard = b * n + c

    def dev(b_, h_, s_):
        return {"batch": b_, "ctx": h_ * SS + s_}

    core = dev(1 - b, h, s)
    side = dev(b, h, 1 - s)
    flip_y = dev(b, h ^ 1, s)
    heads = [(q, h ^ q) for q in range(1, HEADS)]
    group = [(1 - b, s), (b, 1 - s), (1 - b, 1 - s)]
    wires = Wires(sends, recvs)

    barrier = pltpu.get_barrier_semaphore()
    for _, peer in heads:
        pl.semaphore_signal(barrier, inc=1, device_id=dev(b, peer, s), device_id_type=MESH)
    for b_, s_ in group:
        pl.semaphore_signal(barrier, inc=1, device_id=dev(b_, h, s_), device_id_type=MESH)

    here = (x_ref, jw_ref, ow_ref, g_ref, ew_ref, mw_ref, rw_ref, TAB)
    loads = [pltpu.make_async_copy(src, dst, local.at[i]) for i, (src, dst) in enumerate(zip(ins, here))]
    few = [pltpu.make_async_copy(src, dst, local.at[8]) for src, dst in zip(small, (seg_ref, *vec_refs))]
    for load in few + loads:
        load.start()
    made = (result_ref, rg_ref, eg_ref, mg_ref, gradient_ref, jg_ref, og_ref, vg_ref)
    stores = [
        pltpu.make_async_copy(src, dst, local.at[i]) for i, (src, dst) in enumerate(zip(made, outs))
    ]

    for load in few:
        load.wait()
    lines = []
    for ref in vec_refs:
        line = ref[...].astype(F32).reshape(1, ref.shape[0])
        lines.append(wide([line, jnp.zeros((1, 128 - ref.shape[0]), F32)]))
    vec = tall(lines + [jnp.zeros((r - len(lines), 128), F32)])
    by_16 = pltpu.roll(vec, (shard % 8) * 16, 1)
    by_64 = pltpu.roll(vec, (shard // 2 % 2) * 64, 1)
    vec = jnp.where(iota(vec.shape, 0) == 7, by_64, by_16).astype(BF16)
    for load in loads[:3]:
        load.wait()
    jw, ow = jw_ref[...], ow_ref[...]
    for k in range(HEADS):
        at = k * HEAD
        W1S[k] = wide(
            [
                jw[:, D + at : D + at + HEAD],
                jw[:, 2 * D + at : 2 * D + at + HEAD],
                jw[:, at : at + HEAD],
                ow[:, at : at + HEAD],
                vec,
            ]
        )
    TOK[h] = x_ref[0]
    W1[b, h, s] = W1S[h]
    for load in loads[3:7]:
        load.wait()
    pl.semaphore_wait(barrier, len(heads) + len(group))
    inner = (z == 1) | (z == 2)
    edge = (z == 0) | (z == 3)
    low_lane = iota((1, 128), 1) < HEAD

    w1_slot, w1_group = wires.slots(1), wires.slots(2)

    def w1_send():
        for _, peer in heads:
            wires.copy(W1S.at[peer], W1.at[b, h, s], w1_slot, dev(b, peer, s))

    def w1_pass():
        wires.arrived(W1.at[b, 0 : HEADS - 1, s], w1_slot, side)
        wires.copy(W1.at[b, :, s], W1.at[b, :, s], w1_group, side)
        wires.copy(W1.at[b, :, s], W1.at[b, :, s], w1_group + 1, core)

    def w1_core():
        wires.arrived(W1.at[b, :, 1 - s], w1_group, side)
        wires.copy(W1.at[b, :, 1 - s], W1.at[b, :, 1 - s], w1_group + 1, core)

    def w1_wait():
        wires.arrived(W1.at[1 - b], w1_group + 1, core)

    tok_slot, far_slot = wires.slots(6), wires.slots(ZS)

    def tok_at(z_):
        return TOK.at[z_ * YS + y]

    def half_at(z_, half):
        return TOK.at[z_ * YS + y, half * (T // 2) : (half + 1) * (T // 2)]

    def x_send():
        for half in range(2):
            src = x_ref.at[0, half * (T // 2) : (half + 1) * (T // 2)]
            for dz, when in ((2, edge), (1, None), (2, inner), (3, inner)):
                slot = tok_slot + 3 * half + dz - 1
                wires.copy(src, half_at(z, half), slot, dev(b, h ^ (2 * dz), s), when=when)
        wires.copy(x_ref.at[0], tok_at(z), far_slot + z, flip_y)

    def take(dz, half, when=None):
        block = half_at(z ^ dz, half)

        def wait():
            wires.arrived(block, tok_slot + 3 * half + dz - 1, side)

        if when is None:
            wait()
        else:
            pl.when(when)(wait)
        if dz == 2:
            wires.copy(block, block, tok_slot + 3 * half + 2, dev(b, h ^ 2, s), when=inner)
        wires.copy(block, block, far_slot + (z ^ dz), flip_y, when=when)

    def x_near(half):
        take(1, half, edge)
        take(2, half)
        take(1, half, inner)

    def x_far(half):
        take(3, half)

    def along_z(at, slot, relay=True):
        for dz in (1, 2, 3):
            far = dz == 3 and relay
            wires.copy(at(z), at(z), slot + dz - 1, dev(b, h ^ (2 * dz), s), when=inner if far else None)

    def from_z(at, slot, dz, relay=True):
        block = at(z ^ dz)
        wires.arrived(block, slot + dz - 1, side)
        if dz == 2 and relay:
            wires.copy(block, block, slot + 2, dev(b, h ^ 2, s), when=inner)

    def gather(W, ref):
        z_slot, y_slot, s_slot, slot, core_slot = (wires.slots(k) for k in (3, 1, 1, 1, 1))

        def at(z_):
            return W.at[b, z_, y, s]

        def own(z_):
            wires.copy(at(z_), at(z_), y_slot, flip_y)
            wires.copy(at(z_), at(z_), s_slot, side)

        def across(y_, s_):
            wires.copy(W.at[b, :, y_, s_], W.at[b, :, y_, s_], core_slot, core)

        def own_():
            W[b, z, y, s] = ref[...]
            own(z)

        def start():
            along_z(at, z_slot)

        def near():
            for dz in (2, 1):
                from_z(at, z_slot, dz)
                own(z ^ dz)

        def far_():
            from_z(at, z_slot, 3)
            own(z ^ 3)
            across(y, s)

        def diag():
            wires.arrived(W.at[b, :, 1 - y, s], y_slot, flip_y)
            wires.copy(W.at[b, :, 1 - y, s], W.at[b, :, 1 - y, s], slot, side)
            wires.arrived(W.at[b, :, y, 1 - s], s_slot, side)
            across(1 - y, s)
            across(y, 1 - s)

        def over():
            wires.arrived(W.at[b, :, 1 - y, 1 - s], slot, side)
            across(1 - y, 1 - s)

        def wait():
            wires.arrived(W.at[1 - b], core_slot, core)

        return SimpleNamespace(own=own_, start=start, near=near, far=far_, diag=diag, over=over, wait=wait)

    m, j = gather(MW, mw_ref), gather(JW, jw_ref)

    def gather_half(W, relay=True):
        z_slot, y_slot, core_slot = wires.slots(3), wires.slots(1), wires.slots(1)

        def at(z_):
            return W.at[b, z_, y]

        def across(y_):
            wires.copy(W.at[b, :, y_], W.at[b, :, y_], core_slot, core)

        def to_y(z_):
            wires.copy(at(z_), at(z_), y_slot, flip_y)

        def start():
            along_z(at, z_slot, relay)
            to_y(z)

        def near():
            for dz in (2, 1):
                from_z(at, z_slot, dz, relay)
                to_y(z ^ dz)

        def far_():
            from_z(at, z_slot, 3)
            to_y(z ^ 3)
            across(y)

        def over():
            wires.arrived(W.at[b, :, 1 - y], y_slot, flip_y)
            across(1 - y)

        def wait():
            wires.arrived(W.at[1 - b], core_slot, core)

        return SimpleNamespace(start=start, near=near, far=far_, over=over, wait=wait)

    es_slot, pair_slot = wires.slots(1), wires.slots(4)

    def r_own():
        RW[b, z, y] = rw_ref[...]

    def e_own():
        evens, odds = [], []
        for t in range(FF // 256):
            first = ew_ref[:, 256 * t : 256 * t + 128].astype(F32)
            second = ew_ref[:, 256 * t + 128 : 256 * t + 256].astype(F32)
            evens.append(jnp.where(low_lane, first, pltpu.roll(second, 64, 1)))
            odds.append(jnp.where(low_lane, pltpu.roll(first, 64, 1), second))
        evens, odds = wide(evens).astype(BF16), wide(odds).astype(BF16)
        EW[b, z, y, s] = jnp.where(s == 0, evens, odds)
        ES[...] = jnp.where(s == 0, odds, evens)
        wires.copy(ES, EW.at[b, z, y, s], es_slot, side)

    def e_pair():
        wires.arrived(EW.at[b, z, y, 1 - s], es_slot, side)

    e, r_ = gather_half(EW), gather_half(RW, relay=False)

    def pair_send():
        wires.copy(x_ref.at[0], PX, pair_slot, side)
        wires.copy(g_ref.at[0], PG, pair_slot + 1, side)

    def pair_wait():
        wires.arrived(PX, pair_slot, side)
        wires.arrived(PG, pair_slot + 1, side)

    kept = {}

    def vecs_step():
        vecs = W1[:, :, :, :, 256:384].reshape(2 * n, r, 128).astype(F32)
        rows = wide([jnp.sum(vecs[8 * t : 8 * t + 8], axis=0) for t in range(D // 128)])
        gain_one, shift_one, bias_c, bias_o = rows[0:1], rows[1:2], rows[2:3], rows[3:4]
        gain_two, shift_two, reduce_bias = rows[4:5], rows[5:6], rows[6:7]
        even = wide([vecs[4 * t] + vecs[4 * t + 2] for t in range(FF // 256)])[7:8]
        odd = wide([vecs[4 * t + 1] + vecs[4 * t + 3] for t in range(FF // 256)])[7:8]
        expand_bias = jnp.where(s == 0, even, odd)

        def own_head(row):
            pairs = jnp.zeros((1, 128), F32)
            for t in range(HEADS // 2):
                pairs = pairs + jnp.where(h // 2 == t, row[:, 128 * t : 128 * t + 128], 0.0)
            turned = pltpu.roll(pairs, HEAD, 1)
            return jnp.where(h % 2 == 0, pairs, turned)

        bias_c, bias_o = own_head(bias_c), own_head(bias_o)
        own_w = W1[:, :, :, :, 0:256].reshape(D, 256)
        kept.update(
            gain_one=gain_one,
            shift_one=shift_one,
            bias_c=bias_c,
            bias_o=bias_o,
            gain_two=gain_two,
            shift_two=shift_two,
            reduce_bias=reduce_bias,
            expand_bias=expand_bias,
            own_w=own_w,
        )

    kv_slot = wires.slots(HEADS // 2)

    def project(*blocks):
        normed, _ = normalize(tall([TOK[k] for k in blocks]).astype(F32))
        normed = (normed * kept["gain_one"] + kept["shift_one"]).astype(BF16)
        out = dot(normed, kept["own_w"])
        query = out[:, 128:]
        first = jnp.where(low_lane, (query + kept["bias_c"]).astype(BF16).astype(F32) * 0.125, 0.0).astype(BF16)
        second = (query + kept["bias_o"]).astype(BF16).astype(F32) * 0.125
        second = pltpu.roll(jnp.where(low_lane, second, 0.0), HEAD, 1).astype(BF16)
        for i, k in enumerate(blocks):
            rows = slice(i * T, i * T + T)
            NRM[k] = normed[rows]
            KV[k * SS + s] = out[rows, :128].astype(BF16)
            wires.copy(KV.at[k * SS + s], KV.at[k * SS + s], kv_slot + k // 2, side)
            QC[k] = first[rows]
            QO[k] = second[rows]

    def far_block(dz):
        far = h ^ (2 * dz + 1)
        wires.arrived(TOK.at[far], far_slot + (z ^ dz), side)
        return far

    def project_steps(near, far):
        project(*[h ^ (2 * dz) for dz in near], *[far_block(dz) for dz in far])

    first_blocks = [functools.partial(project_steps, *blocks) for blocks in (((0,), (0,)), ((1, 2), ()), ((), (1, 2)), ((3,), (3,)))]

    tiles = TAB.shape[0] // T

    parts = 4
    per = tiles // parts

    def offset_part(part):
        if part == 0:
            loads[7].wait()
            for t in range(4):
                OFF[tiles + t] = jnp.zeros((T, 128), BF16)
        rows = slice(part * per * T, (part + 1) * per * T)
        out = dot(TAB[rows, :], kept["own_w"][:, 128:])
        OFF[part * per : (part + 1) * per] = out.astype(BF16).reshape(per, T, 128)

    offs = [functools.partial(offset_part, part) for part in range(parts)]

    tril = iota((T, T), 1) <= iota((T, T), 0)
    diff = iota((T, T), 1) - iota((T, T), 0)
    eye = iota((T, T), 1) == iota((T, T), 0)
    flip = jnp.where(iota((T, T), 0) + iota((T, T), 1) == T - 1, 1.0, 0.0).astype(BF16)
    att_slot = wires.slots(2)

    def forward(pair):
        ks = (2 * pair, 2 * pair + 1)
        blocks = [k * SS + s for k in ks]
        q_both = tall([QC[k] for k in ks])
        qo = [QO[k] for k in ks]
        seg_q = []
        for block in blocks:
            seg_row = seg_ref[0:1, pl.ds(pl.multiple_of(block * T, T), T)].astype(F32)
            seg_q.append(jnp.sum(jnp.where(eye, seg_row, 0.0), axis=1, keepdims=True))
        peaks = [jnp.full((T, T), NEG, F32)] * 2
        for ch in range(pair + 1):
            first = ch * 4
            content = dot_nt(q_both, KV[first : first + 4].reshape(4 * T, 128))
            for i, block in enumerate(blocks):
                window = OFF[pl.ds(n - 1 - block + first, 5)].reshape(5 * T, 128)
                rel = dot_nt(qo[i], window)
                turned = [pltpu.roll(rel[:, t * T : (t + 1) * T], 1, 1, stride=1, stride_axis=0) for t in range(5)]
                for t in range(4):
                    seg_k = seg_ref[0:1, (first + t) * T : (first + t + 1) * T].astype(F32)
                    ok = (diff <= (block - first - t) * T) & (seg_k == seg_q[i])
                    score = content[i * T : (i + 1) * T, t * T : (t + 1) * T]
                    score = jnp.where(ok, score + jnp.where(tril, turned[t], turned[t + 1]), NEG)
                    SCR[i, first + t] = score
                    peaks[i] = jnp.maximum(peaks[i], score)
        peaks = [jnp.max(peak, axis=1, keepdims=True) for peak in peaks]
        totals, out = [jnp.zeros((T, T), F32)] * 2, jnp.zeros((2 * T, 128), F32)
        for ch in range(pair + 1):
            first = ch * 4
            lows = []
            for i, k in enumerate(ks):
                low = []
                for t in range(4):
                    p = jnp.exp(SCR[i, first + t] - peaks[i])
                    totals[i] = totals[i] + p
                    low.append(p.astype(BF16))
                lows.append(wide(low))
                turned = dot(flip, lows[i]).astype(BF16)
                for t in range(4):
                    PST[k, first + t] = turned[:, t * T : (t + 1) * T]
            out = out + dot(tall(lows), KV[first : first + 4].reshape(4 * T, 128))
        for i, k in enumerate(ks):
            inverse = 1.0 / jnp.sum(totals[i], axis=1, keepdims=True)
            att = out[i * T : (i + 1) * T, HEAD:] * inverse
            ATF[k] = wide([att, att])
            LIN[k] = jnp.broadcast_to(inverse, (T, T))
            ATS[k] = fold(att).astype(BF16)
        for k in ks:
            wires.copy(ATS.at[k], ATR.at[s, h], att_slot, dev(b, k, s), when=h != k)
            wires.copy(ATS.at[k], ATR.at[s, h], att_slot + 1, dev(b, k, 1 - s))

    def keys_wait(pair):
        wires.arrived(KV.at[pair * 2 : pair * 2 + 2], kv_slot + pair, side)

    kv = [functools.partial(keys_wait, pair) for pair in range(HEADS // 2)]
    fwd = [functools.partial(forward, pair) for pair in range(HEADS // 2)]

    def att_wait():
        ATR[s, h] = ATS[h]
        wires.arrived(ATR.at[s, 0 : HEADS - 1], att_slot, side)
        wires.arrived(ATR.at[1 - s], att_slot + 1, side)

    def by_heads(R):
        return wide([unfold(R[k].astype(F32)) for k in range(HEADS)]).astype(BF16)

    ga_slot = wires.slots(1)
    step = min(512, FF)

    def feed(first, heads_out, tokens, g_low):
        middle = tokens + dot(by_heads(heads_out), MW[...].reshape(D, D))
        normed, inverse = normalize(middle)
        second_low = (normed * kept["gain_two"] + kept["shift_two"]).astype(BF16)
        grad_second = jnp.zeros((T, D), F32)
        root, cube = math.sqrt(2.0 / math.pi), 0.044715
        rows = slice(first, first + T)
        for f in range(FF // 2 // step):
            cols = slice(f * step, f * step + step)
            e_w = EW[:, :, :, :, :, cols].reshape(D, step)
            r_w = RW[...].reshape(FF // 2, D)[cols]
            v = dot(second_low, e_w) + kept["expand_bias"][:, cols]
            tanh = jnp.tanh(root * (v + cube * v * v * v))
            ACT[rows, cols] = (0.5 * v * (1.0 + tanh)).astype(BF16)
            slope = 0.5 * (1.0 + tanh) + 0.5 * v * (1.0 - tanh * tanh) * (root * (1.0 + 3.0 * cube * v * v))
            grad_hidden = (dot_nt(g_low, r_w) * slope).astype(BF16)
            GH[rows, cols] = grad_hidden
            grad_second = grad_second + dot_nt(grad_hidden, e_w)
        return middle, normed, inverse, second_low, grad_second

    def ffn_other():
        _, _, _, second_low, grad_second = feed(T, ATR.at[1 - s], PX[...].astype(F32), PG[...])
        GSS[...] = grad_second.astype(BF16)
        wires.copy(GSS, GSR, pair_slot + 2, side)
        kept["second_other"] = second_low

    def ffn_own():
        middle, normed, inverse, second_low, grad_second = feed(0, ATR.at[s], x_ref[0].astype(F32), g_ref[0])
        kept.update(
            att_low=by_heads(ATR.at[s]),
            second_low=tall([second_low, kept["second_other"]]),
            g_low=tall([g_ref[0], PG[...]]),
            grad_second=grad_second,
            middle=middle,
            n_two=normed,
            inverse_two=inverse,
        )

    def ffn_out():
        output = dot(ACT[...], RW[...].reshape(FF // 2, D))
        OUS[...] = output[T:].astype(BF16)
        kept["output"] = kept["middle"] + kept["reduce_bias"] + output[:T]
        kept["bias_expand"] = colsum(GH[...].astype(F32))

    def ffn_send():
        wires.copy(OUS, OUR, pair_slot + 3, side)

    def ffn_back():
        n_two = kept["n_two"]
        wires.arrived(GSR, pair_slot + 2, side)
        grad_second = kept["grad_second"] + GSR[...].astype(F32)
        g = g_ref[0].astype(F32)
        grad_middle = g + norm_back(grad_second * kept["gain_two"], n_two, kept["inverse_two"])
        middle_low = grad_middle.astype(BF16)
        gradient_ref[0] = grad_middle
        grad_att = dot_nt(middle_low, MW[...].reshape(D, D))
        for k in range(HEADS):
            GAS[k] = fold(grad_att[:, k * HEAD : (k + 1) * HEAD]).astype(BF16)
        for _, peer in heads:
            wires.copy(GAS.at[peer], GAR.at[h], ga_slot, dev(b, peer, s))
        GAR[h] = GAS[h]
        kept.update(
            middle_low=middle_low,
            vec_feed=[colsum(grad_second * n_two), colsum(grad_second), colsum(g)],
        )

    def result_step():
        wires.arrived(OUR, pair_slot + 3, side)
        result_ref[0] = (kept["output"] + OUR[...].astype(F32)).astype(BF16)
        stores[0].start()

    def ga_wait():
        wires.arrived(GAR.at[0 : HEADS - 1], ga_slot, side)

    def add_into(W, index, other):
        W[index] = (W[index].astype(F32) + other.astype(F32)).astype(BF16)

    def scatter(W, C, A, B, Z, Z2, finish):
        slot = wires.slots(5)
        lead = (s,) if A is not None else ()

        def core_():
            wires.copy(W.at[1 - b], C, slot, core)

        def merge():
            wires.arrived(C, slot, core)

            def add(i, carry):
                for j in range(YS):
                    add_into(W, (b, i, j), C[i, j])
                return carry

            lax.fori_loop(0, ZS, add, 0)
            if A is not None:
                wires.copy(W.at[b, :, :, 1 - s], A, slot + 1, side)
            else:
                wires.copy(W.at[b, :, 1 - y], B, slot + 2, flip_y)

        def side_():
            wires.arrived(A, slot + 1, side)

            def add(i, carry):
                for j in range(YS):
                    add_into(W, (b, i, j, s), A[i, j])
                return carry

            lax.fori_loop(0, ZS, add, 0)
            wires.copy(W.at[b, :, 1 - y, s], B, slot + 2, flip_y)

        def plane():
            wires.arrived(B, slot + 2, flip_y)
            for i in range(ZS):
                add_into(W, (b, i, y) + lead, B[i])
            for dz in (1, 3):
                wires.copy(W.at[(b, z ^ dz, y) + lead], Z.at[dz // 2], slot + 3, dev(b, h ^ 2, s))

        def pair():
            wires.arrived(Z, slot + 3, side)
            for i in range(2):
                add_into(W, (b, z ^ (2 * i), y) + lead, Z[i])
            wires.copy(W.at[(b, z ^ 2, y) + lead], Z2, slot + 4, dev(b, h ^ 4, s))

        def total_():
            wires.arrived(Z2, slot + 4, side)
            finish(W[(b, z, y) + lead].astype(F32) + Z2[...].astype(F32))

        return SimpleNamespace(core=core_, merge=merge, side=side_, plane=plane, pair=pair, total=total_)

    def scatter_z(W, C, Z, Z2, B, finish):
        slot = wires.slots(4)

        def core_():
            wires.copy(W.at[1 - b], C, slot, core)

        def merge():
            wires.arrived(C, slot, core)

            def add(i, carry):
                for j in range(YS):
                    add_into(W, (b, i, j), C[i, j])
                return carry

            lax.fori_loop(0, ZS, add, 0)
            for dz in (1, 3):
                wires.copy(W.at[b, z ^ dz], Z.at[dz // 2], slot + 1, dev(b, h ^ 2, s))

        def pair():
            wires.arrived(Z, slot + 1, side)
            for i in range(2):
                for j in range(YS):
                    add_into(W, (b, z ^ (2 * i), j), Z[i, j])
            wires.copy(W.at[b, z ^ 2], Z2, slot + 2, dev(b, h ^ 4, s))

        def plane():
            wires.arrived(Z2, slot + 2, side)
            for j in range(YS):
                add_into(W, (b, z, j), Z2[j])
            wires.copy(W.at[b, z, 1 - y], B, slot + 3, flip_y)

        def total_():
            wires.arrived(B, slot + 3, flip_y)
            finish(W[b, z, y].astype(F32) + B[...].astype(F32))

        return SimpleNamespace(core=core_, merge=merge, pair=pair, plane=plane, total=total_)

    def keep_rows(ref, store):
        def put(total):
            ref[...] = total
            store.start()

        return put

    eg_slot = wires.slots(1)

    def swap_columns(total):
        EO[...] = jnp.where(s == 0, total[0], total[1])
        EX[...] = jnp.where(s == 0, total[1], total[0]).astype(BF16)
        wires.copy(EX, EY, eg_slot, side)

    def E_columns():
        wires.arrived(EY, eg_slot, side)
        own, other = EO[...], EY[...].astype(F32)
        even, odd = jnp.where(s == 0, own, other), jnp.where(s == 0, other, own)
        for t in range(FF // 256):
            a_, b_ = even[:, 128 * t : 128 * t + 128], odd[:, 128 * t : 128 * t + 128]
            eg_ref[:, 256 * t : 256 * t + 128] = jnp.where(low_lane, a_, pltpu.roll(b_, 64, 1))
            eg_ref[:, 256 * t + 128 : 256 * t + 256] = jnp.where(low_lane, pltpu.roll(a_, 64, 1), b_)
        stores[2].start()

    def R_make():
        RG[...] = dot_tn(ACT[...], kept["g_low"]).astype(BF16).reshape(RG.shape)

    def E_make():
        for f in range(FF // 2 // step):
            cols = slice(f * step, f * step + step)
            out = dot_tn(kept["second_low"], GH[:, cols])
            EG[:, :, :, :, :, cols] = out.astype(BF16).reshape(2, ZS, YS, SS, r, step)

    def M_make():
        MG[...] = dot_tn(kept["att_low"], kept["middle_low"]).astype(BF16).reshape(MG.shape)

    R = scatter_z(RG, CR, ZR, YR, BR, keep_rows(rg_ref, stores[1]))
    E = scatter(EG, CE, None, BE, ZE, YE, swap_columns)
    M = scatter(MG, CM, AM, BM, ZM, YM, keep_rows(mg_ref, stores[3]))

    cut = iota((T, T), 1) >= iota((T, T), 0)
    dkv_slot = wires.slots(HEADS // 2)
    rkv_slot, rdq_slot = wires.slots(1), wires.slots(1)
    zero_row = jnp.zeros((1, 128), F32)
    sums = {"c": zero_row, "o": zero_row, "kv": zero_row, "q": zero_row}

    def reverse():
        for t in range(n + 4):
            DROWT[t] = jnp.zeros((HEAD, T), F32)
        for k in range(HEADS):
            att, inverse = ATF[k], LIN[k]
            high = att.astype(BF16)
            rest = (att - high.astype(F32)).astype(BF16)
            inv_1 = inverse.astype(BF16).astype(F32)
            inv_2 = (inverse - inv_1).astype(BF16).astype(F32)
            inv_3 = inverse - inv_1 - inv_2
            place = iota((T, T), 1)
            parts_ = jnp.where(place == 0, inv_1, jnp.where(place == 1, inv_2, jnp.where(place == 2, inv_3, 0.0)))
            turned = dot(flip, wide([QC[k], QO[k], high, rest, parts_.astype(BF16)]))
            QCT[k] = turned[:, :128].T[:HEAD].astype(BF16)
            QOT[k] = turned[:, 128:256].T[HEAD:].astype(BF16)
            ATF[k] = turned[:, 256:384] + turned[:, 384:512]
            LIN[k] = jnp.broadcast_to(jnp.sum(turned[:, 512:], axis=1, keepdims=True), (T, T))

    def backward(pair):
        ks = (2 * pair, 2 * pair + 1)
        bases = [n - 1 - (k * SS + s) for k in ks]
        twice = []
        for k in ks:
            ga = GAR[k].astype(F32)
            other = pltpu.roll(ga, HEAD, 1)
            twice.append(tall([jnp.where(low_lane, ga, other), jnp.where(low_lane, other, ga)]).astype(BF16))
        twice = dot(flip, wide(twice))
        spreads, pads, lefts = [], [], []
        none = jnp.zeros((HEAD, T), BF16)
        for i, k in enumerate(ks):
            ga = twice[:, i * 128 : (i + 1) * 128]
            spreads.append(jnp.sum(ga * ATF[k], axis=1, keepdims=True) * 0.5 * LIN[k])
            scaled = ga * LIN[k]
            pads.append(jnp.where(low_lane, 0.0, scaled).astype(BF16))
            lefts.append(tall([QCT[k], none]))
            lefts.append(tall([none, scaled.T[HEAD:].astype(BF16)]))
        pads, lefts = tall(pads), wide(lefts)
        dq, dqo = jnp.zeros((2 * T, 128), F32), [jnp.zeros((T, 128), F32)] * 2
        for ch in range(pair + 1):
            first = ch * 4
            keys = KV[first : first + 4].reshape(4 * T, 128)
            gp = dot_nt(pads, keys)
            lows, stack = [], []
            for i, k in enumerate(ks):
                low, turned, probs = [], [], []
                for t in range(4):
                    p = PST[k, first + t]
                    ds = p.astype(F32) * (gp[i * T : (i + 1) * T, t * T : (t + 1) * T] - spreads[i])
                    probs.append(p)
                    low.append(ds.astype(BF16))
                    turned.append(pltpu.roll(ds, 0, 1, stride=1, stride_axis=0))
                lows.append(wide(low))
                stack += [lows[i], wide(probs)]
                dr = [jnp.where(cut, turned[0], 0.0)]
                for t in range(1, 4):
                    dr.append(jnp.where(cut, turned[t], turned[t - 1]))
                dr.append(jnp.where(cut, 0.0, turned[3]))
                dr = wide(dr).astype(BF16)
                window = OFF[pl.ds(bases[i] + first, 5)].reshape(5 * T, 128)
                dqo[i] = dqo[i] + dot(dr, window)
                back = dot(QOT[k], dr)
                for t in range(5):
                    DROWT[bases[i] + first + t] += back[:, t * T : (t + 1) * T]
            dq = dq + dot(tall(lows), keys)
            add = dot(lefts, tall(stack))
            for t in range(4):
                part = add[:, t * T : (t + 1) * T]
                DKVT[first + t] = part if pair == HEADS // 2 - 1 else DKVT[first + t] + part
        dqo = pltpu.roll(tall(dqo), HEAD, 1)
        sums["c"] = sums["c"] + colsum(dq) * 0.125
        sums["o"] = sums["o"] + colsum(dqo) * 0.125
        dq = ((dq + dqo) * 0.125).astype(BF16)
        dq = dot(flip, wide([dq[:T], dq[T:]]))
        for i, k in enumerate(ks):
            DQF[k] = fold(dq[:, i * 128 : i * 128 + HEAD]).astype(BF16)
            DKVS[k] = DKVT[k * SS + 1 - s].T.astype(BF16)
        for k in ks:
            wires.copy(DKVS.at[k], DKVR.at[k], dkv_slot + pair, side)
        for k in ks:
            wires.copy(DQF.at[k], RDQ.at[h], rdq_slot, dev(b, k, s), when=h != k)
        return dq

    def settle(pair, dq):
        ks = (2 * pair, 2 * pair + 1)
        wires.arrived(DKVR.at[ks[0] : ks[1] + 1], dkv_slot + pair, side)
        lows = []
        for i, k in enumerate(ks):
            dkv = (DKVT[k * SS + s].T + DKVR[k].astype(F32)).astype(BF16)
            DKVF[k] = dkv
            mine = jnp.where(low_lane, dq[:, i * 128 : (i + 1) * 128], 0.0)
            sums["kv"] = sums["kv"] + colsum(dkv.astype(F32))
            sums["q"] = sums["q"] + colsum(mine)
            lows.append(wide([dkv, mine.astype(BF16)]))
        for k in ks:
            wires.copy(DKVF.at[k], RKV.at[h], rkv_slot, dev(b, k, s), when=h != k)
        add = dot_tn(tall([NRM[k] for k in ks]), tall(lows))
        JGA[...] = add if pair == HEADS // 2 - 1 else JGA[...] + add

    kept_dq = {}

    def backward_step(pair):
        kept_dq[pair] = backward(pair)

    def settle_step(pair):
        settle(pair, kept_dq[pair])

    bwd = [functools.partial(backward_step, pair) for pair in range(HEADS // 2)]
    put = [functools.partial(settle_step, pair) for pair in range(HEADS // 2)]

    def offset_grad():
        rows_t = wide([DROWT[t] for t in range(tiles)])
        upper = rows_t.astype(BF16)
        lower = (rows_t - upper.astype(F32)).astype(BF16)
        og_t = dot(tall([upper, lower]), TAB[...])
        og = (og_t[:HEAD] + og_t[HEAD:]).T
        kept["og"] = og

    def jg_make():
        og, own_w, gain_one, shift_one = kept["og"], kept["own_w"], kept["gain_one"], kept["shift_one"]
        vec_feed, bias_expand = kept["vec_feed"], kept["bias_expand"]
        RKV[h] = DKVF[h]
        RDQ[h] = DQF[h]
        og = pltpu.roll(wide([og, jnp.zeros((D, HEAD), F32)]), HEAD, 1)
        grads = JGA[...]
        w_f = own_w.astype(F32)
        col_w = jnp.where(iota((D, 256), 1) < 192, w_f, 0.0)
        ones = jnp.ones((8, 256), F32)
        totals = jnp.broadcast_to(wide([sums["kv"], sums["q"]]), (8, 256))
        highest = lax.Precision.HIGHEST
        shift_mixer = dot(totals, col_w, ((1,), (1,)), highest)[0:1]
        gain_mixer = dot(ones, col_w * grads, ((1,), (1,)), highest)[0:1]
        gain_mixer = (gain_mixer - shift_one * shift_mixer) / gain_one

        def place_head(row):
            row = jnp.where(low_lane, row, 0.0)
            row = row + pltpu.roll(row, HEAD, 1)
            row = wide([row] * (D // 128))
            return jnp.where(iota((1, D), 1) // HEAD == h, row, 0.0)

        partial = tall(
            [gain_mixer, shift_mixer, place_head(sums["c"]), place_head(sums["o"])]
            + vec_feed
            + [jnp.zeros((9, D), F32)]
        )
        row_index = iota((r, 128), 0)
        last = wide([grads[:, :128], grads[:, 128:] + og]).astype(BF16).reshape(2, HEADS, SS, r, 256)
        for b_ in range(2):
            for k in range(HEADS):
                for s_ in range(SS):
                    d_ = (b_ * HEADS + k) * SS + s_
                    tile = partial[:, d_ // 8 * 128 : d_ // 8 * 128 + 128]
                    if d_ % 8:
                        tile = pltpu.roll(tile, 128 - d_ % 8 * 16, 1)
                    bias = bias_expand[:, d_ // 4 * 128 : d_ // 4 * 128 + 128]
                    if d_ // 2 % 2:
                        bias = pltpu.roll(bias, 64, 1)
                    bias = jnp.where(s == s_, bias, 0.0)
                    tile = jnp.where(row_index == 7, bias, tile)
                    JGM[b_, k, s_] = wide([last[b_, k, s_], tile.astype(BF16)])
        wires.copy(JGM.at[1 - b], JRC, jr_slot, core)

    jr_slot, jf_slot = wires.slots(2), wires.slots(1)

    def jg_core():
        wires.arrived(JRC, jr_slot, core)
        JGX[...] = (JGM[b, :, 1 - s].astype(F32) + JRC[:, 1 - s].astype(F32)).astype(BF16)
        wires.copy(JGX, JRS, jr_slot + 1, side)

    def jg_side():
        total = JGM[b, :, s].astype(F32) + JRC[:, s].astype(F32)
        wires.arrived(JRS, jr_slot + 1, side)
        JF[...] = (total + JRS[...].astype(F32)).astype(BF16)
        for _, peer in heads:
            wires.copy(JF.at[peer], JR2.at[h], jf_slot, dev(b, peer, s))
        JR2[h] = JF[h]

    def rkv_wait():
        wires.arrived(RKV.at[0 : HEADS - 1], rkv_slot, side)
        wires.arrived(RDQ.at[0 : HEADS - 1], rdq_slot, side)

    def grad_step():
        gain_one = kept["gain_one"]
        x = x_ref[0].astype(F32)
        pieces_k, pieces_v = [], []
        for k in range(0, HEADS, 2):
            a_, b_ = RKV[k].astype(F32), RKV[k + 1].astype(F32)
            pieces_k.append(jnp.where(low_lane, a_, pltpu.roll(b_, HEAD, 1)))
            pieces_v.append(jnp.where(low_lane, pltpu.roll(a_, HEAD, 1), b_))
        grad_joint = wide([by_heads(RDQ), wide(pieces_k).astype(BF16), wide(pieces_v).astype(BF16)])
        joint_w = JW[...].reshape(D, 3 * D)
        grad_normed = dot_nt(grad_joint, joint_w)
        n_one, inverse_one = normalize(x)
        gradient_ref[0] += norm_back(grad_normed * gain_one, n_one, inverse_one)
        stores[4].start()

    def jg_wait():
        wires.arrived(JR2.at[0 : HEADS - 1], jf_slot, side)

    def outs_step():
        got = [JR2[k].astype(F32) for k in range(HEADS)]
        jg_ref[...] = wide([a[:, 128:192] for a in got] + [a[:, 0:64] for a in got] + [a[:, 64:128] for a in got])
        og_ref[...] = wide([a[:, 192:256] for a in got])
        vectors = got[0][:, 256:]
        for a in got[1:]:
            vectors = vectors + a[:, 256:]
        vg_ref[...] = vectors
        for store in stores[5:]:
            store.start()

    def reap():
        wires.reap(12)

    order = (
        w1_send,
        x_send,
        m.own,
        e_own,
        r_own,
        w1_pass,
        pair_send,
        functools.partial(x_near, 0),
        functools.partial(x_near, 1),
        e_pair,
        m.start,
        e.start,
        w1_core,
        functools.partial(x_far, 0),
        functools.partial(x_far, 1),
        r_.start,
        w1_wait,
        vecs_step,
        first_blocks[0],
        first_blocks[1],
        offs[0],
        offs[1],
        offs[2],
        offs[3],
        first_blocks[2],
        first_blocks[3],
        m.near,
        e.near,
        kv[0],
        fwd[0],
        kv[1],
        kv[2],
        fwd[2],
        m.far,
        e.far,
        r_.near,
        kv[3],
        fwd[3],
        m.diag,
        r_.far,
        fwd[1],
        e.over,
        m.over,
        r_.over,
        reap,
        m.wait,
        e.wait,
        r_.wait,
        pair_wait,
        att_wait,
        ffn_other,
        j.own,
        j.start,
        ffn_own,
        R_make,
        R.core,
        E_make,
        E.core,
        reap,
        ffn_back,
        R.merge,
        E.merge,
        ffn_out,
        ffn_send,
        M_make,
        M.core,
        M.merge,
        j.near,
        reverse,
        ga_wait,
        bwd[3],
        R.pair,
        E.plane,
        M.side,
        bwd[2],
        j.far,
        put[3],
        bwd[1],
        M.plane,
        put[2],
        bwd[0],
        R.plane,
        E.pair,
        offset_grad,
        put[1],
        j.diag,
        put[0],
        jg_make,
        M.pair,
        R.total,
        jg_core,
        E.total,
        jg_side,
        j.over,
        result_step,
        rkv_wait,
        j.wait,
        grad_step,
        E_columns,
        M.total,
        reap,
        jg_wait,
        outs_step,
    )
    for step_ in order:
        step_()
    wires.reap()
    for store in stores:
        store.wait()


def spread_refs(n, *refs):
    layer_kernel(n, refs[:9], refs[9:17], refs[17:25], *refs[25:])


def hand_over(*refs):
    count = (len(refs) - 9) // 2
    ins, vectors, outs, smalls = refs[:count], refs[count], refs[count + 1 : 2 * count + 1], refs[2 * count + 1 :]
    for a, o in zip(ins, outs):
        o[...] = a[...]
    for i, o in enumerate(smalls):
        o[...] = vectors[i, 0 : o.shape[0]]


def table_reversed(length, width):
    half = width // 2
    freq = 10000.0 ** (-2.0 * np.arange(half) / width)
    angle = np.arange(length - 1, -1, -1)[:, None] * freq[None, :]
    return np.concatenate([np.sin(angle), np.cos(angle)], axis=1).astype(np.float32).astype(ml_dtypes.bfloat16)


def fast(
    n,
    inputs,
    segments,
    mixer_gain,
    mixer_shift,
    joint_weight,
    offset_weight,
    content_bias,
    offset_bias,
    merge_weight,
    feed_gain,
    feed_shift,
    expand_weight,
    expand_bias,
    reduce_weight,
    reduce_bias,
    cotangent,
):
    T, D = inputs.shape[1:]
    r = joint_weight.shape[0]
    FF = expand_weight.shape[1]
    rr = reduce_weight.shape[0]
    length = segments.shape[1]
    vecs = [mixer_gain, mixer_shift, content_bias, offset_bias, feed_gain, feed_shift, reduce_bias, expand_bias]
    table = jnp.asarray(table_reversed(length, D))
    V = pltpu.VMEM
    half = FF // 2
    blocks, folded = (HEADS, T, 128), (HEADS, T // 2, 128)
    scratch = [
        V((length, D), BF16),
        V((HEADS, T, D), BF16),
        V((HEADS, T, D), BF16),
        V((HEADS, r, 384), BF16),
        V((2, HEADS, SS, r, 384), BF16),
        V((2, ZS, YS, SS, r, 3 * D), BF16),
        V((2, ZS, YS, SS, r, D), BF16),
        V((2, ZS, YS, SS, r, half), BF16),
        V((2, ZS, YS, rr, D), BF16),
        V((r, half), BF16),
        V((T, D), BF16),
        V((T, D), BF16),
        V((n, T, 128), BF16),
        V(blocks, BF16),
        V(blocks, BF16),
        V((HEADS, HEAD, T), BF16),
        V((HEADS, HEAD, T), BF16),
        V((n + 4, T, 128), BF16),
        V((2, n, T, T), F32),
        V((HEADS, n, T, T), BF16),
        V((HEADS, T, T), F32),
        V((HEADS, T, T), F32),
        V(folded, BF16),
        V((SS,) + folded, BF16),
        V((2 * T, half), BF16),
        V((2 * T, half), BF16),
        V((T, D), BF16),
        V((T, D), BF16),
        V((T, D), BF16),
        V((T, D), BF16),
        V(folded, BF16),
        V(folded, BF16),
        V((n, 128, T), F32),
        V((n + 4, HEAD, T), F32),
        V(blocks, BF16),
        V(blocks, BF16),
        V(blocks, BF16),
        V(folded, BF16),
        V(blocks, BF16),
        V(folded, BF16),
        V((2, ZS, YS, SS, r, D), BF16),
        V((2, ZS, YS, SS, r, half), BF16),
        V((2, ZS, YS, rr, D), BF16),
        V((ZS, YS, SS, r, D), BF16),
        V((ZS, YS, SS, r, half), BF16),
        V((ZS, YS, rr, D), BF16),
        V((ZS, YS, r, D), BF16),
        V((ZS, r, D), BF16),
        V((ZS, SS, r, half), BF16),
        V((rr, D), BF16),
        V((2, r, D), BF16),
        V((2, SS, r, half), BF16),
        V((2, YS, rr, D), BF16),
        V((r, D), BF16),
        V((SS, r, half), BF16),
        V((YS, rr, D), BF16),
        V((r, half), F32),
        V((r, half), BF16),
        V((r, half), BF16),
        V((D, 256), F32),
        V((2, HEADS, SS, r, 384), BF16),
        V((HEADS, SS, r, 384), BF16),
        V((HEADS, r, 384), BF16),
        V((HEADS, r, 384), BF16),
        V((HEADS, r, 384), BF16),
        V((HEADS, r, 384), BF16),
        V((1, T, D), BF16),
        V((r, 3 * D), BF16),
        V((r, D), BF16),
        V((1, T, D), BF16),
        V((r, FF), BF16),
        V((r, D), BF16),
        V((rr, D), BF16),
    ]
    out_shape = [
        jax.ShapeDtypeStruct((1, T, D), BF16),
        jax.ShapeDtypeStruct((rr, D), F32),
        jax.ShapeDtypeStruct((r, FF), F32),
        jax.ShapeDtypeStruct((r, D), F32),
        jax.ShapeDtypeStruct((1, T, D), F32),
        jax.ShapeDtypeStruct((r, 3 * D), F32),
        jax.ShapeDtypeStruct((r, D), F32),
        jax.ShapeDtypeStruct((r, 128), F32),
    ]
    scratch += [V(a.shape, a.dtype) for a in out_shape]
    scratch += [pltpu.SemaphoreType.DMA((count,)) for count in (9, SENDS, RECVS)]
    scratch += [V(a.shape, a.dtype) for a in (segments, *vecs)]
    vmem, hbm = pl.BlockSpec(memory_space=V), pl.BlockSpec(memory_space=pl.ANY)
    outs = pl.pallas_call(
        functools.partial(spread_refs, n),
        out_shape=out_shape,
        in_specs=[hbm] * 17,
        out_specs=[hbm] * 8,
        scratch_shapes=scratch,
        compiler_params=pltpu.CompilerParams(
            collective_id=0, has_side_effects=True, vmem_limit_bytes=60 * 2**20
        ),
    )(
        segments,
        *vecs,
        inputs,
        joint_weight,
        offset_weight,
        cotangent,
        expand_weight,
        merge_weight,
        reduce_weight,
        table,
    )
    big, vg = outs[:-1], outs[-1]
    final = pl.pallas_call(
        hand_over,
        out_shape=[jax.ShapeDtypeStruct(a.shape, a.dtype) for a in big]
        + [jax.ShapeDtypeStruct(v.shape, F32) for v in vecs],
        in_specs=[vmem] * (len(big) + 1),
        out_specs=[vmem] * (len(big) + len(vecs)),
    )(*big, vg)
    result, rg, eg, mg, gradient, jg, og = final[: len(big)]
    gain_m, shift_m, bias_c, bias_o, gain_f, shift_f, bias_r, bias_e = final[len(big) :]
    return (
        result,
        gradient,
        gain_m,
        shift_m,
        jg,
        og,
        bias_c,
        bias_o,
        mg,
        gain_f,
        shift_f,
        eg,
        bias_e,
        rg,
        bias_r,
    )


def solution(mesh):
    in_specs = (
        P("batch", "ctx", None),
        P("batch", None),
        P(("batch", "ctx")),
        P(("batch", "ctx")),
        P(("batch", "ctx"), None),
        P(("batch", "ctx"), None),
        P(("batch", "ctx")),
        P(("batch", "ctx")),
        P(("batch", "ctx"), None),
        P(("batch", "ctx")),
        P(("batch", "ctx")),
        P(("batch", "ctx"), None),
        P(("batch", "ctx")),
        P(("batch", "ctx"), None),
        P(("batch", "ctx")),
        P("batch", "ctx", None),
    )
    out_specs = (
        P("batch", "ctx", None),
        P("batch", "ctx", None),
        P(("batch", "ctx")),
        P(("batch", "ctx")),
        P(("batch", "ctx"), None),
        P(("batch", "ctx"), None),
        P(("batch", "ctx")),
        P(("batch", "ctx")),
        P(("batch", "ctx"), None),
        P(("batch", "ctx")),
        P(("batch", "ctx")),
        P(("batch", "ctx"), None),
        P(("batch", "ctx")),
        P(("batch", "ctx"), None),
        P(("batch", "ctx")),
    )
    n, cores = mesh.shape["ctx"], mesh.shape["batch"]

    def layer(*args):
        suits = n == HEADS * SS and cores == 2 and args[0].shape[1] == 128 and args[4].shape[0] == 16
        return fast(n, *args) if suits else local(*args)

    return jax.shard_map(layer, mesh=mesh, in_specs=in_specs, out_specs=out_specs, check_vma=False)
```

```python
import functools
import math
from types import SimpleNamespace

import jax
import jax.numpy as jnp
import ml_dtypes
import numpy as np
from jax import lax
from jax.experimental import pallas as pl
from jax.experimental.pallas import tpu as pltpu
from jax.sharding import PartitionSpec as P

HEADS = 8
HEAD = 64


masked_score = -1e30


def shifted(array, axis, by):
    peers = lax.axis_size(axis)
    pairs = [(i, i + by) for i in range(peers) if 0 <= i + by < peers]
    return lax.ppermute(array, axis, pairs)


def shifted_2(value, axis, steps):
    count = lax.axis_size(axis)
    pairs = [(source, (source + steps) % count) for source in range(count)]
    return lax.ppermute(value, axis, pairs)


def layer_norm(values, gain, shift):
    center = values - jnp.mean(values, axis=-1, keepdims=True)
    spread = jnp.mean(center * center, axis=-1, keepdims=True)
    return center * lax.rsqrt(spread + 1e-05) * gain + shift


def sinusoid(first, count, width):
    half = width // 2
    freq = jnp.power(10000.0, -2.0 * jnp.arange(half, dtype=jnp.float32) / width)
    place = (first + jnp.arange(count, dtype=jnp.int32)).astype(jnp.float32)
    angle = place[:, None] * freq[None, :]
    return jnp.concatenate([jnp.sin(angle), jnp.cos(angle)], axis=1)


def contract_rows(left, right):
    return lax.dot_general(
        left, right, (((0,), (0,)), ((), ())), preferred_element_type=jnp.float32
    )


def contract_cols(left, right):
    return lax.dot_general(
        left, right, (((1,), (1,)), ((), ())), preferred_element_type=jnp.float32
    )


def split_contract(table, grad_rows):
    upper = grad_rows.astype(jnp.bfloat16)
    lower = (grad_rows - upper.astype(jnp.float32)).astype(jnp.bfloat16)
    return contract_rows(table, upper) + contract_rows(table, lower)


def fold_blocks(step, carry, pieces, limit):
    count = pieces[0].shape[0]
    size = min(count, limit)
    number = count // size
    stacked = tuple((item.reshape((number, size) + item.shape[1:]) for item in pieces))

    def inner(state, item):
        offset, parts = item
        return (step(state, parts, offset * size), None)

    folded, _ = lax.scan(inner, carry, (jnp.arange(number, dtype=jnp.int32), stacked))
    return folded


def realign(relative_scores, count):
    heads, rows, width = relative_scores.shape
    flat = relative_scores.reshape(heads, rows * width)
    band = flat[:, rows - 1 : rows - 1 + rows * (width - 1)]
    return band.reshape(heads, rows, width - 1)[:, :, :count]


def pair_terms(
    query_content_term, query_position_term, keys, query_first, key_first, seg_row, offsets_pad
):
    rows, heads, size = query_content_term.shape
    count = keys.shape[0]
    length = offsets_pad.shape[0] // 2
    anchor = query_first - key_first - count + length
    attention_span = lax.dynamic_slice_in_dim(offsets_pad, anchor, rows + count, 0)[::-1].reshape(
        rows + count, heads, size
    )
    content = jnp.einsum(
        "ahd,bhd->hab", query_content_term, keys, preferred_element_type=jnp.float32
    )
    relative_scores = jnp.einsum(
        "scx,icx->csi", query_position_term, attention_span, preferred_element_type=jnp.float32
    )
    scores = (content + realign(relative_scores, count)) * (1.0 / math.sqrt(size))
    query_seg = lax.dynamic_slice_in_dim(seg_row, query_first, rows, 0)
    key_seg = lax.dynamic_slice_in_dim(seg_row, key_first, count, 0)
    query_pos = query_first + jnp.arange(rows, dtype=jnp.int32)
    key_pos = key_first + jnp.arange(count, dtype=jnp.int32)
    allowed = (key_pos[None, :] <= query_pos[:, None]) & (key_seg[None, :] == query_seg[:, None])
    return (scores, allowed, attention_span, anchor)


def pair_grads(
    query_content_term,
    query_position_term,
    keys,
    values,
    query_first,
    key_first,
    seg_row,
    offsets_pad,
    logsum,
    spread,
    grad_attended,
):
    rows, heads, size = query_content_term.shape
    count = keys.shape[0]
    scale = 1.0 / math.sqrt(size)
    scores, allowed, attention_span, anchor = pair_terms(
        query_content_term, query_position_term, keys, query_first, key_first, seg_row, offsets_pad
    )
    probs = jnp.where(allowed[None], jnp.exp(scores - logsum[..., None]), 0.0)
    grad_values = jnp.einsum(
        "hab,ahd->bhd",
        probs.astype(jnp.bfloat16),
        grad_attended,
        preferred_element_type=jnp.float32,
    )
    grad_probs = jnp.einsum(
        "ahd,bhd->hab", grad_attended, values, preferred_element_type=jnp.float32
    )
    grad_scores = (probs * (grad_probs - spread[..., None])).astype(jnp.bfloat16)
    grad_content = scale * jnp.einsum(
        "hab,bhd->ahd", grad_scores, keys, preferred_element_type=jnp.float32
    )
    grad_keys = scale * jnp.einsum(
        "hab,ahd->bhd", grad_scores, query_content_term, preferred_element_type=jnp.float32
    )
    blank = jnp.zeros((heads, rows, rows + count), jnp.float32)
    _, realign_back = jax.vjp(lambda relative_scores: realign(relative_scores, count), blank)
    gradient_relative_scores = realign_back(grad_scores.astype(jnp.float32))[0].astype(jnp.bfloat16)
    grad_offset = scale * jnp.einsum(
        "nsk,kno->sno", gradient_relative_scores, attention_span, preferred_element_type=jnp.float32
    )
    grad_window = scale * jnp.einsum(
        "cqu,qcn->ucn",
        gradient_relative_scores,
        query_position_term,
        preferred_element_type=jnp.float32,
    )
    grad_window = grad_window.reshape(rows + count, heads * size)[::-1]
    return (grad_content, grad_offset, grad_keys, grad_values, grad_window, anchor)


def add_window(grad_rows, grad_window, anchor):
    current = lax.dynamic_slice_in_dim(grad_rows, anchor, grad_window.shape[0], 0)
    return lax.dynamic_update_slice_in_dim(grad_rows, current + grad_window, anchor, 0)


def local(
    inputs,
    segments,
    mixer_gain,
    mixer_shift,
    joint_weight,
    offset_weight,
    content_bias,
    offset_bias,
    merge_weight,
    feed_gain,
    feed_shift,
    expand_weight,
    expand_bias,
    reduce_weight,
    reduce_bias,
    cotangent,
):
    (
        first_gain,
        first_shift,
        joint_matrix,
        offset_matrix,
        bias_content,
        bias_position,
        merge_matrix,
    ) = (
        lax.all_gather(mixer_gain, ("batch", "ctx"), axis=0, tiled=True),
        lax.all_gather(mixer_shift, ("batch", "ctx"), axis=0, tiled=True),
        lax.all_gather(joint_weight, ("batch", "ctx"), axis=0, tiled=True),
        lax.all_gather(offset_weight, ("batch", "ctx"), axis=0, tiled=True),
        lax.all_gather(content_bias, ("batch", "ctx"), axis=0, tiled=True),
        lax.all_gather(offset_bias, ("batch", "ctx"), axis=0, tiled=True),
        lax.all_gather(merge_weight, ("batch", "ctx"), axis=0, tiled=True),
    )
    tokens = inputs[0].astype(jnp.float32)
    rows, width = tokens.shape
    seg_row = segments[0]
    length = seg_row.shape[0]
    place = lax.axis_index("ctx")
    cycle = lax.axis_size("ctx")
    block_first = place * rows
    heads_shape = (rows, HEADS, HEAD)
    gain_one = first_gain.astype(jnp.float32)
    shift_one = first_shift.astype(jnp.float32)
    normed = layer_norm(tokens, gain_one, shift_one)
    normed_low = normed.astype(jnp.bfloat16)
    joint = jnp.dot(normed_low, joint_matrix, preferred_element_type=jnp.float32)
    query = joint[:, :width]
    keys = joint[:, width : 2 * width].astype(jnp.bfloat16).reshape(heads_shape)
    values = joint[:, 2 * width :].astype(jnp.bfloat16).reshape(heads_shape)
    query_content_term = (
        (query + bias_content.astype(jnp.float32)).astype(jnp.bfloat16).reshape(heads_shape)
    )
    query_position_term = (
        (query + bias_position.astype(jnp.float32)).astype(jnp.bfloat16).reshape(heads_shape)
    )
    everyone = lax.axis_size(("batch", "ctx"))
    share = length // everyone
    table = sinusoid(lax.axis_index(("batch", "ctx")) * share, share, width).astype(jnp.bfloat16)
    offsets_local = jnp.dot(table, offset_matrix, preferred_element_type=jnp.float32).astype(
        jnp.bfloat16
    )
    offsets_all = lax.all_gather(offsets_local, ("batch", "ctx"), axis=0, tiled=True)
    offsets_pad = jnp.concatenate([jnp.zeros_like(offsets_all), offsets_all], axis=0)

    def stats_block(carry, pieces, start):
        peak, total = carry
        scores, allowed, attention_span, anchor = pair_terms(
            query_content_term,
            query_position_term,
            pieces[0],
            block_first,
            start,
            seg_row,
            offsets_pad,
        )
        masked = jnp.where(allowed[None], scores, masked_score)
        new_peak = jnp.maximum(peak, jnp.max(masked, axis=-1))
        added = jnp.sum(
            jnp.where(allowed[None], jnp.exp(masked - new_peak[..., None]), 0.0), axis=-1
        )
        return (new_peak, total * jnp.exp(peak - new_peak) + added)

    peak_start = jnp.full((HEADS, rows), masked_score, jnp.float32)
    total_start = jnp.zeros((HEADS, rows), jnp.float32)
    peak, total = fold_blocks(
        stats_block,
        (peak_start, total_start),
        (lax.all_gather(keys, "ctx", axis=0, tiled=True),),
        rows,
    )
    logsum = peak + jnp.log(total)

    def output_block(carry, pieces, start):
        scores, allowed, attention_span, anchor = pair_terms(
            query_content_term,
            query_position_term,
            pieces[0],
            block_first,
            start,
            seg_row,
            offsets_pad,
        )
        probs = jnp.where(allowed[None], jnp.exp(scores - logsum[..., None]), 0.0).astype(
            jnp.bfloat16
        )
        return carry + jnp.einsum(
            "hab,bhd->ahd", probs, pieces[1], preferred_element_type=jnp.float32
        )

    mixed = fold_blocks(
        output_block,
        jnp.zeros(heads_shape, jnp.float32),
        (
            lax.all_gather(keys, "ctx", axis=0, tiled=True),
            lax.all_gather(values, "ctx", axis=0, tiled=True),
        ),
        rows,
    )
    attended_low = mixed.reshape(rows, width).astype(jnp.bfloat16)
    middle = tokens + jnp.dot(attended_low, merge_matrix, preferred_element_type=jnp.float32)
    second_gain, second_shift, expand_matrix, expand_vector, reduce_matrix, reduce_vector = (
        lax.all_gather(feed_gain, ("batch", "ctx"), axis=0, tiled=True),
        lax.all_gather(feed_shift, ("batch", "ctx"), axis=0, tiled=True),
        lax.all_gather(expand_weight, ("batch", "ctx"), axis=0, tiled=True),
        lax.all_gather(expand_bias, ("batch", "ctx"), axis=0, tiled=True),
        lax.all_gather(reduce_weight, ("batch", "ctx"), axis=0, tiled=True),
        lax.all_gather(reduce_bias, ("batch", "ctx"), axis=0, tiled=True),
    )
    gain_two = second_gain.astype(jnp.float32)
    shift_two = second_shift.astype(jnp.float32)
    second_low = layer_norm(middle, gain_two, shift_two).astype(jnp.bfloat16)
    hidden = jnp.dot(
        second_low, expand_matrix, preferred_element_type=jnp.float32
    ) + expand_vector.astype(jnp.float32)
    active_low = jax.nn.gelu(hidden, approximate=True).astype(jnp.bfloat16)
    output = (
        middle
        + jnp.dot(active_low, reduce_matrix, preferred_element_type=jnp.float32)
        + reduce_vector.astype(jnp.float32)
    )
    result = output.astype(jnp.bfloat16)[None]
    grad_out = cotangent[0]
    grad_outf = grad_out.astype(jnp.float32)
    grad_reduce_bias = jnp.sum(grad_outf, axis=0)
    grad_reduce = contract_rows(active_low, grad_out)
    grad_active = contract_cols(grad_out, reduce_matrix)
    _, gelu_back = jax.vjp(lambda value: jax.nn.gelu(value, approximate=True), hidden)
    grad_hidden = gelu_back(grad_active)[0].astype(jnp.bfloat16)
    grad_expand_bias = jnp.sum(grad_hidden.astype(jnp.float32), axis=0)
    grad_expand = contract_rows(second_low, grad_hidden)
    grad_second = contract_cols(grad_hidden, expand_matrix)
    _, second_back = jax.vjp(layer_norm, middle, gain_two, shift_two)
    grad_mid, grad_gain_two, grad_shift_two = second_back(grad_second)
    grad_middle = grad_outf + grad_mid
    feed_sums = (
        lax.psum_scatter(grad_gain_two, ("batch", "ctx"), scatter_dimension=0, tiled=True),
        lax.psum_scatter(grad_shift_two, ("batch", "ctx"), scatter_dimension=0, tiled=True),
        lax.psum_scatter(grad_expand, ("batch", "ctx"), scatter_dimension=0, tiled=True),
        lax.psum_scatter(grad_expand_bias, ("batch", "ctx"), scatter_dimension=0, tiled=True),
        lax.psum_scatter(grad_reduce, ("batch", "ctx"), scatter_dimension=0, tiled=True),
        lax.psum_scatter(grad_reduce_bias, ("batch", "ctx"), scatter_dimension=0, tiled=True),
    )
    middle_low = grad_middle.astype(jnp.bfloat16)
    grad_merge = contract_rows(attended_low, middle_low)
    grad_attended = (
        contract_cols(middle_low, merge_matrix).astype(jnp.bfloat16).reshape(heads_shape)
    )
    spread = jnp.einsum("ahd,ahd->ha", grad_attended.astype(jnp.float32), mixed)
    zero_heads = jnp.zeros(heads_shape, jnp.float32)
    zero_rows = jnp.zeros((2 * length, width), jnp.float32)

    def cycle_step(turn, carry):
        visiting, carried, grad_content, grad_offset, grad_rows = carry
        owner = (place - turn) % cycle
        terms = pair_grads(
            query_content_term,
            query_position_term,
            visiting[0],
            visiting[1],
            block_first,
            owner * rows,
            seg_row,
            offsets_pad,
            logsum,
            spread,
            grad_attended,
        )
        carried = carried + jnp.stack([terms[2], terms[3]])
        grad_rows = add_window(grad_rows, terms[4], terms[5])
        visiting = shifted(visiting, "ctx", 1)
        carried = shifted_2(carried.astype(jnp.bfloat16), "ctx", 1).astype(carried.dtype)
        return (visiting, carried, grad_content + terms[0], grad_offset + terms[1], grad_rows)

    start_state = (
        jnp.stack([keys, values]),
        jnp.zeros((2,) + heads_shape, jnp.float32),
        zero_heads,
        zero_heads,
        zero_rows,
    )
    _, carried, grad_content, grad_offset, grad_rows = lax.fori_loop(
        0, cycle, cycle_step, start_state
    )
    grad_keys = carried[0]
    grad_values = carried[1]
    grad_content_bias = jnp.sum(grad_content, axis=0).reshape(width)
    gradient_position_bias = jnp.sum(grad_offset, axis=0).reshape(width)
    grad_joint = jnp.concatenate(
        [
            (grad_content + grad_offset).reshape(rows, width),
            grad_keys.reshape(rows, width),
            grad_values.reshape(rows, width),
        ],
        axis=1,
    ).astype(jnp.bfloat16)
    grad_joint_matrix = contract_rows(normed_low, grad_joint)
    grad_normed = contract_cols(grad_joint, joint_matrix)
    _, first_back = jax.vjp(layer_norm, tokens, gain_one, shift_one)
    grad_tokens, grad_gain_one, grad_shift_one = first_back(grad_normed)
    gradient = (grad_middle + grad_tokens)[None]
    full_table = sinusoid(0, length, width).astype(jnp.bfloat16)
    grad_offset_matrix = split_contract(full_table, grad_rows[length:])
    mixer_sums = (
        lax.psum_scatter(grad_gain_one, ("batch", "ctx"), scatter_dimension=0, tiled=True),
        lax.psum_scatter(grad_shift_one, ("batch", "ctx"), scatter_dimension=0, tiled=True),
        lax.psum_scatter(grad_joint_matrix, ("batch", "ctx"), scatter_dimension=0, tiled=True),
        lax.psum_scatter(grad_offset_matrix, ("batch", "ctx"), scatter_dimension=0, tiled=True),
        lax.psum_scatter(grad_content_bias, ("batch", "ctx"), scatter_dimension=0, tiled=True),
        lax.psum_scatter(gradient_position_bias, ("batch", "ctx"), scatter_dimension=0, tiled=True),
        lax.psum_scatter(grad_merge, ("batch", "ctx"), scatter_dimension=0, tiled=True),
    )
    return (
        result,
        gradient,
        mixer_sums[0],
        mixer_sums[1],
        mixer_sums[2],
        mixer_sums[3],
        mixer_sums[4],
        mixer_sums[5],
        mixer_sums[6],
        feed_sums[0],
        feed_sums[1],
        feed_sums[2],
        feed_sums[3],
        feed_sums[4],
        feed_sums[5],
    )


F32, BF16 = jnp.float32, jnp.bfloat16
MESH = pl.DeviceIdType.MESH
NEG = -1e30
ZS, YS, SS = 4, 2, 2


def dot(a, b, dims=((1,), (0,)), precision=None):
    return lax.dot_general(a, b, (dims, ((), ())), preferred_element_type=F32, precision=precision)


def dot_nt(a, b):
    return dot(a, b, ((1,), (1,)))


def dot_tn(a, b):
    return dot(a, b, ((0,), (0,)))


def iota(shape, axis):
    return lax.broadcasted_iota(jnp.int32, shape, axis)


def wide(tiles):
    return jnp.concatenate(tiles, axis=1)


def tall(tiles):
    return jnp.concatenate(tiles, axis=0)


def fold(x):
    half = x.shape[0] // 2
    return wide([x[:half], x[half:]])


def unfold(x):
    return tall([x[:, :HEAD], x[:, HEAD:]])


def normalize(x):
    center = x - jnp.mean(x, axis=-1, keepdims=True)
    inverse = lax.rsqrt(jnp.mean(center * center, axis=-1, keepdims=True) + 1e-05)
    return center * inverse, inverse


def norm_back(e, n, inverse):
    return inverse * (e - jnp.mean(e, axis=-1, keepdims=True) - n * jnp.mean(e * n, axis=-1, keepdims=True))


def colsum(x):
    return jnp.sum(x, axis=0, keepdims=True)


class Wires:
    def __init__(self, sends, recvs):
        self.sends, self.recvs, self.received, self.pending = sends, recvs, 0, []
        self.free = list(range(SENDS))
        self.peak = 0

    def slots(self, count):
        first = self.received
        self.received += count
        return first

    def copy(self, src, dst, slot, to, when=None):
        index = self.free.pop(0)
        self.peak = max(self.peak, SENDS - len(self.free))
        made = pltpu.make_async_remote_copy(
            src_ref=src,
            dst_ref=dst,
            send_sem=self.sends.at[index],
            recv_sem=self.recvs.at[slot],
            device_id=to,
            device_id_type=MESH,
        )
        self.pending.append((made, when, index))
        if when is None:
            made.start()
        else:
            pl.when(when)(made.start)

    def arrived(self, dst, slot, to):
        pltpu.make_async_remote_copy(
            src_ref=dst,
            dst_ref=dst,
            send_sem=self.sends.at[0],
            recv_sem=self.recvs.at[slot],
            device_id=to,
            device_id_type=MESH,
        ).wait_recv()

    def reap(self, keep=0):
        count = len(self.pending) - keep
        for made, when, index in self.pending[:count]:
            if when is None:
                made.wait_send()
            else:
                pl.when(when)(made.wait_send)
            self.free.append(index)
        self.pending = self.pending[count:]


SENDS, RECVS = 70, 74
def layer_kernel(
    n,
    small,
    ins,
    outs,
    *scratch,
):
    (
        TAB,
        TOK,
        NRM,
        W1S,
        W1,
        JW,
        MW,
        EW,
        RW,
        ES,
        PX,
        PG,
        KV,
        QC,
        QO,
        QCT,
        QOT,
        OFF,
        SCR,
        PST,
        ATF,
        LIN,
        ATS,
        ATR,
        ACT,
        GH,
        GSS,
        GSR,
        OUS,
        OUR,
        GAS,
        GAR,
        DKVT,
        DROWT,
        DKVS,
        DKVR,
        DKVF,
        DQF,
        RKV,
        RDQ,
        MG,
        EG,
        RG,
        CM,
        CE,
        CR,
        AM,
        BM,
        BE,
        BR,
        ZM,
        ZE,
        ZR,
        YM,
        YE,
        YR,
        EO,
        EX,
        EY,
        JGA,
        JGM,
        VGM,
        JR1,
        VR1,
        JF,
        VF,
        JR2,
        VR2,
        x_ref,
        jw_ref,
        ow_ref,
        g_ref,
        ew_ref,
        mw_ref,
        rw_ref,
        result_ref,
        rg_ref,
        eg_ref,
        mg_ref,
        gradient_ref,
        jg_ref,
        og_ref,
        vg_ref,
        local,
        sends,
        recvs,
        seg_ref,
        *vec_refs,
    ) = scratch
    T = x_ref.shape[1]
    D = x_ref.shape[2]
    FF = ew_ref.shape[1]
    r = jw_ref.shape[0]
    b = lax.axis_index("batch")
    c = lax.axis_index("ctx")
    h, s = c // SS, c % SS
    z, y = h // YS, h % YS
    shard = b * n + c

    def dev(b_, h_, s_):
        return {"batch": b_, "ctx": h_ * SS + s_}

    core = dev(1 - b, h, s)
    side = dev(b, h, 1 - s)
    flip_y = dev(b, h ^ 1, s)
    heads = [(q, h ^ q) for q in range(1, HEADS)]
    group = [(1 - b, s), (b, 1 - s), (1 - b, 1 - s)]
    wires = Wires(sends, recvs)

    barrier = pltpu.get_barrier_semaphore()
    for _, peer in heads:
        pl.semaphore_signal(barrier, inc=1, device_id=dev(b, peer, s), device_id_type=MESH)
    for b_, s_ in group:
        pl.semaphore_signal(barrier, inc=1, device_id=dev(b_, h, s_), device_id_type=MESH)

    here = (x_ref, jw_ref, ow_ref, g_ref, ew_ref, mw_ref, rw_ref, TAB)
    loads = [pltpu.make_async_copy(src, dst, local.at[i]) for i, (src, dst) in enumerate(zip(ins, here))]
    few = [pltpu.make_async_copy(src, dst, local.at[8]) for src, dst in zip(small, (seg_ref, *vec_refs))]
    for load in few + loads:
        load.start()
    made = (result_ref, rg_ref, eg_ref, mg_ref, gradient_ref, jg_ref, og_ref, vg_ref)
    stores = [
        pltpu.make_async_copy(src, dst, local.at[i]) for i, (src, dst) in enumerate(zip(made, outs))
    ]

    for load in few:
        load.wait()
    lines = []
    for ref in vec_refs:
        line = ref[...].astype(F32).reshape(1, ref.shape[0])
        lines.append(wide([line, jnp.zeros((1, 128 - ref.shape[0]), F32)]))
    vec = tall(lines + [jnp.zeros((r - len(lines), 128), F32)])
    by_16 = pltpu.roll(vec, (shard % 8) * 16, 1)
    by_64 = pltpu.roll(vec, (shard // 2 % 2) * 64, 1)
    vec = jnp.where(iota(vec.shape, 0) == 7, by_64, by_16).astype(BF16)
    for load in loads[:3]:
        load.wait()
    jw, ow = jw_ref[...], ow_ref[...]
    for k in range(HEADS):
        at = k * HEAD
        W1S[k] = wide(
            [
                jw[:, D + at : D + at + HEAD],
                jw[:, 2 * D + at : 2 * D + at + HEAD],
                jw[:, at : at + HEAD],
                ow[:, at : at + HEAD],
                vec,
            ]
        )
    TOK[h] = x_ref[0]
    W1[b, h, s] = W1S[h]
    for load in loads[3:7]:
        load.wait()
    pl.semaphore_wait(barrier, len(heads) + len(group))
    inner = (z == 1) | (z == 2)
    edge = (z == 0) | (z == 3)
    low_lane = iota((1, 128), 1) < HEAD

    w1_slot, w1_group = wires.slots(1), wires.slots(2)

    def w1_send():
        for _, peer in heads:
            wires.copy(W1S.at[peer], W1.at[b, h, s], w1_slot, dev(b, peer, s))

    def w1_pass():
        wires.arrived(W1.at[b, 0 : HEADS - 1, s], w1_slot, side)
        wires.copy(W1.at[b, :, s], W1.at[b, :, s], w1_group, side)
        wires.copy(W1.at[b, :, s], W1.at[b, :, s], w1_group + 1, core)

    def w1_core():
        wires.arrived(W1.at[b, :, 1 - s], w1_group, side)
        wires.copy(W1.at[b, :, 1 - s], W1.at[b, :, 1 - s], w1_group + 1, core)

    def w1_wait():
        wires.arrived(W1.at[1 - b], w1_group + 1, core)

    tok_slot, far_slot = wires.slots(6), wires.slots(ZS)

    def tok_at(z_):
        return TOK.at[z_ * YS + y]

    def half_at(z_, half):
        return TOK.at[z_ * YS + y, half * (T // 2) : (half + 1) * (T // 2)]

    def x_send():
        for half in range(2):
            src = x_ref.at[0, half * (T // 2) : (half + 1) * (T // 2)]
            for dz, when in ((2, edge), (1, None), (2, inner), (3, inner)):
                slot = tok_slot + 3 * half + dz - 1
                wires.copy(src, half_at(z, half), slot, dev(b, h ^ (2 * dz), s), when=when)
        wires.copy(x_ref.at[0], tok_at(z), far_slot + z, flip_y)

    def take(dz, half, when=None):
        block = half_at(z ^ dz, half)

        def wait():
            wires.arrived(block, tok_slot + 3 * half + dz - 1, side)

        if when is None:
            wait()
        else:
            pl.when(when)(wait)
        if dz == 2:
            wires.copy(block, block, tok_slot + 3 * half + 2, dev(b, h ^ 2, s), when=inner)
        wires.copy(block, block, far_slot + (z ^ dz), flip_y, when=when)

    def x_near(half):
        take(1, half, edge)
        take(2, half)
        take(1, half, inner)

    def x_far(half):
        take(3, half)

    def along_z(at, slot, relay=True):
        for dz in (1, 2, 3):
            far = dz == 3 and relay
            wires.copy(at(z), at(z), slot + dz - 1, dev(b, h ^ (2 * dz), s), when=inner if far else None)

    def from_z(at, slot, dz, relay=True):
        block = at(z ^ dz)
        wires.arrived(block, slot + dz - 1, side)
        if dz == 2 and relay:
            wires.copy(block, block, slot + 2, dev(b, h ^ 2, s), when=inner)

    def gather(W, ref):
        z_slot, y_slot, s_slot, slot, core_slot = (wires.slots(k) for k in (3, 1, 1, 1, 1))

        def at(z_):
            return W.at[b, z_, y, s]

        def own(z_):
            wires.copy(at(z_), at(z_), y_slot, flip_y)
            wires.copy(at(z_), at(z_), s_slot, side)

        def across(y_, s_):
            wires.copy(W.at[b, :, y_, s_], W.at[b, :, y_, s_], core_slot, core)

        def own_():
            W[b, z, y, s] = ref[...]
            own(z)

        def start():
            along_z(at, z_slot)

        def near():
            for dz in (2, 1):
                from_z(at, z_slot, dz)
                own(z ^ dz)

        def far_():
            from_z(at, z_slot, 3)
            own(z ^ 3)
            across(y, s)

        def diag():
            wires.arrived(W.at[b, :, 1 - y, s], y_slot, flip_y)
            wires.copy(W.at[b, :, 1 - y, s], W.at[b, :, 1 - y, s], slot, side)
            wires.arrived(W.at[b, :, y, 1 - s], s_slot, side)
            across(1 - y, s)
            across(y, 1 - s)

        def over():
            wires.arrived(W.at[b, :, 1 - y, 1 - s], slot, side)
            across(1 - y, 1 - s)

        def wait():
            wires.arrived(W.at[1 - b], core_slot, core)

        return SimpleNamespace(own=own_, start=start, near=near, far=far_, diag=diag, over=over, wait=wait)

    m, j = gather(MW, mw_ref), gather(JW, jw_ref)

    def gather_half(W, relay=True):
        z_slot, y_slot, core_slot = wires.slots(3), wires.slots(1), wires.slots(1)

        def at(z_):
            return W.at[b, z_, y]

        def across(y_):
            wires.copy(W.at[b, :, y_], W.at[b, :, y_], core_slot, core)

        def to_y(z_):
            wires.copy(at(z_), at(z_), y_slot, flip_y)

        def start():
            along_z(at, z_slot, relay)
            to_y(z)

        def near():
            for dz in (2, 1):
                from_z(at, z_slot, dz, relay)
                to_y(z ^ dz)

        def far_():
            from_z(at, z_slot, 3)
            to_y(z ^ 3)
            across(y)

        def over():
            wires.arrived(W.at[b, :, 1 - y], y_slot, flip_y)
            across(1 - y)

        def wait():
            wires.arrived(W.at[1 - b], core_slot, core)

        return SimpleNamespace(start=start, near=near, far=far_, over=over, wait=wait)

    es_slot, pair_slot = wires.slots(1), wires.slots(4)

    def r_own():
        RW[b, z, y] = rw_ref[...]

    def e_own():
        evens, odds = [], []
        for t in range(FF // 256):
            first = ew_ref[:, 256 * t : 256 * t + 128].astype(F32)
            second = ew_ref[:, 256 * t + 128 : 256 * t + 256].astype(F32)
            evens.append(jnp.where(low_lane, first, pltpu.roll(second, 64, 1)))
            odds.append(jnp.where(low_lane, pltpu.roll(first, 64, 1), second))
        evens, odds = wide(evens).astype(BF16), wide(odds).astype(BF16)
        EW[b, z, y, s] = jnp.where(s == 0, evens, odds)
        ES[...] = jnp.where(s == 0, odds, evens)
        wires.copy(ES, EW.at[b, z, y, s], es_slot, side)

    def e_pair():
        wires.arrived(EW.at[b, z, y, 1 - s], es_slot, side)

    e, r_ = gather_half(EW), gather_half(RW, relay=False)

    def pair_send():
        wires.copy(x_ref.at[0], PX, pair_slot, side)
        wires.copy(g_ref.at[0], PG, pair_slot + 1, side)

    def pair_wait():
        wires.arrived(PX, pair_slot, side)
        wires.arrived(PG, pair_slot + 1, side)

    kept = {}

    def vecs_step():
        vecs = W1[:, :, :, :, 256:384].reshape(2 * n, r, 128).astype(F32)
        rows = wide([jnp.sum(vecs[8 * t : 8 * t + 8], axis=0) for t in range(D // 128)])
        gain_one, shift_one, bias_c, bias_o = rows[0:1], rows[1:2], rows[2:3], rows[3:4]
        gain_two, shift_two, reduce_bias = rows[4:5], rows[5:6], rows[6:7]
        even = wide([vecs[4 * t] + vecs[4 * t + 2] for t in range(FF // 256)])[7:8]
        odd = wide([vecs[4 * t + 1] + vecs[4 * t + 3] for t in range(FF // 256)])[7:8]
        expand_bias = jnp.where(s == 0, even, odd)

        def own_head(row):
            pairs = jnp.zeros((1, 128), F32)
            for t in range(HEADS // 2):
                pairs = pairs + jnp.where(h // 2 == t, row[:, 128 * t : 128 * t + 128], 0.0)
            turned = pltpu.roll(pairs, HEAD, 1)
            return jnp.where(h % 2 == 0, pairs, turned)

        bias_c, bias_o = own_head(bias_c), own_head(bias_o)
        own_w = W1[:, :, :, :, 0:256].reshape(D, 256)
        kept.update(
            gain_one=gain_one,
            shift_one=shift_one,
            bias_c=bias_c,
            bias_o=bias_o,
            gain_two=gain_two,
            shift_two=shift_two,
            reduce_bias=reduce_bias,
            expand_bias=expand_bias,
            own_w=own_w,
        )

    kv_slot = wires.slots(HEADS // 2)

    def project(*blocks):
        normed, _ = normalize(tall([TOK[k] for k in blocks]).astype(F32))
        normed = (normed * kept["gain_one"] + kept["shift_one"]).astype(BF16)
        out = dot(normed, kept["own_w"])
        query = out[:, 128:]
        first = jnp.where(low_lane, (query + kept["bias_c"]).astype(BF16).astype(F32) * 0.125, 0.0).astype(BF16)
        second = (query + kept["bias_o"]).astype(BF16).astype(F32) * 0.125
        second = pltpu.roll(jnp.where(low_lane, second, 0.0), HEAD, 1).astype(BF16)
        for i, k in enumerate(blocks):
            rows = slice(i * T, i * T + T)
            NRM[k] = normed[rows]
            KV[k * SS + s] = out[rows, :128].astype(BF16)
            wires.copy(KV.at[k * SS + s], KV.at[k * SS + s], kv_slot + k // 2, side)
            QC[k] = first[rows]
            QO[k] = second[rows]

    def far_block(dz):
        far = h ^ (2 * dz + 1)
        wires.arrived(TOK.at[far], far_slot + (z ^ dz), side)
        return far

    def project_steps(near, far):
        project(*[h ^ (2 * dz) for dz in near], *[far_block(dz) for dz in far])

    first_blocks = [functools.partial(project_steps, *blocks) for blocks in (((0,), (0,)), ((1, 2), ()), ((), (1, 2)), ((3,), (3,)))]

    tiles = TAB.shape[0] // T

    parts = 4
    per = tiles // parts

    def offset_part(part):
        if part == 0:
            loads[7].wait()
            for t in range(4):
                OFF[tiles + t] = jnp.zeros((T, 128), BF16)
        rows = slice(part * per * T, (part + 1) * per * T)
        out = dot(TAB[rows, :], kept["own_w"][:, 128:])
        OFF[part * per : (part + 1) * per] = out.astype(BF16).reshape(per, T, 128)

    offs = [functools.partial(offset_part, part) for part in range(parts)]

    tril = iota((T, T), 1) <= iota((T, T), 0)
    diff = iota((T, T), 1) - iota((T, T), 0)
    eye = iota((T, T), 1) == iota((T, T), 0)
    flip = jnp.where(iota((T, T), 0) + iota((T, T), 1) == T - 1, 1.0, 0.0).astype(BF16)
    att_slot = wires.slots(2)

    def forward(pair):
        ks = (2 * pair, 2 * pair + 1)
        blocks = [k * SS + s for k in ks]
        q_both = tall([QC[k] for k in ks])
        qo = [QO[k] for k in ks]
        seg_q = []
        for block in blocks:
            seg_row = seg_ref[0:1, pl.ds(pl.multiple_of(block * T, T), T)].astype(F32)
            seg_q.append(jnp.sum(jnp.where(eye, seg_row, 0.0), axis=1, keepdims=True))
        peaks = [jnp.full((T, T), NEG, F32)] * 2
        for ch in range(pair + 1):
            first = ch * 4
            content = dot_nt(q_both, KV[first : first + 4].reshape(4 * T, 128))
            for i, block in enumerate(blocks):
                window = OFF[pl.ds(n - 1 - block + first, 5)].reshape(5 * T, 128)
                rel = dot_nt(qo[i], window)
                turned = [pltpu.roll(rel[:, t * T : (t + 1) * T], 1, 1, stride=1, stride_axis=0) for t in range(5)]
                for t in range(4):
                    seg_k = seg_ref[0:1, (first + t) * T : (first + t + 1) * T].astype(F32)
                    ok = (diff <= (block - first - t) * T) & (seg_k == seg_q[i])
                    score = content[i * T : (i + 1) * T, t * T : (t + 1) * T]
                    score = jnp.where(ok, score + jnp.where(tril, turned[t], turned[t + 1]), NEG)
                    SCR[i, first + t] = score
                    peaks[i] = jnp.maximum(peaks[i], score)
        peaks = [jnp.max(peak, axis=1, keepdims=True) for peak in peaks]
        totals, out = [jnp.zeros((T, T), F32)] * 2, jnp.zeros((2 * T, 128), F32)
        for ch in range(pair + 1):
            first = ch * 4
            lows = []
            for i, k in enumerate(ks):
                low = []
                for t in range(4):
                    p = jnp.exp(SCR[i, first + t] - peaks[i])
                    totals[i] = totals[i] + p
                    low.append(p.astype(BF16))
                lows.append(wide(low))
                turned = dot(flip, lows[i]).astype(BF16)
                for t in range(4):
                    PST[k, first + t] = turned[:, t * T : (t + 1) * T]
            out = out + dot(tall(lows), KV[first : first + 4].reshape(4 * T, 128))
        for i, k in enumerate(ks):
            inverse = 1.0 / jnp.sum(totals[i], axis=1, keepdims=True)
            att = out[i * T : (i + 1) * T, HEAD:] * inverse
            ATF[k] = wide([att, att])
            LIN[k] = jnp.broadcast_to(inverse, (T, T))
            ATS[k] = fold(att).astype(BF16)
        for k in ks:
            wires.copy(ATS.at[k], ATR.at[s, h], att_slot, dev(b, k, s), when=h != k)
            wires.copy(ATS.at[k], ATR.at[s, h], att_slot + 1, dev(b, k, 1 - s))

    def keys_wait(pair):
        wires.arrived(KV.at[pair * 2 : pair * 2 + 2], kv_slot + pair, side)

    kv = [functools.partial(keys_wait, pair) for pair in range(HEADS // 2)]
    fwd = [functools.partial(forward, pair) for pair in range(HEADS // 2)]

    def att_wait():
        ATR[s, h] = ATS[h]
        wires.arrived(ATR.at[s, 0 : HEADS - 1], att_slot, side)
        wires.arrived(ATR.at[1 - s], att_slot + 1, side)

    def by_heads(R):
        return wide([unfold(R[k].astype(F32)) for k in range(HEADS)]).astype(BF16)

    ga_slot = wires.slots(1)
    step = min(512, FF)

    def feed(first, heads_out, tokens, g_low):
        middle = tokens + dot(by_heads(heads_out), MW[...].reshape(D, D))
        normed, inverse = normalize(middle)
        second_low = (normed * kept["gain_two"] + kept["shift_two"]).astype(BF16)
        grad_second = jnp.zeros((T, D), F32)
        root, cube = math.sqrt(2.0 / math.pi), 0.044715
        rows = slice(first, first + T)
        for f in range(FF // 2 // step):
            cols = slice(f * step, f * step + step)
            e_w = EW[:, :, :, :, :, cols].reshape(D, step)
            r_w = RW[...].reshape(FF // 2, D)[cols]
            v = dot(second_low, e_w) + kept["expand_bias"][:, cols]
            tanh = jnp.tanh(root * (v + cube * v * v * v))
            ACT[rows, cols] = (0.5 * v * (1.0 + tanh)).astype(BF16)
            slope = 0.5 * (1.0 + tanh) + 0.5 * v * (1.0 - tanh * tanh) * (root * (1.0 + 3.0 * cube * v * v))
            grad_hidden = (dot_nt(g_low, r_w) * slope).astype(BF16)
            GH[rows, cols] = grad_hidden
            grad_second = grad_second + dot_nt(grad_hidden, e_w)
        return middle, normed, inverse, second_low, grad_second

    def ffn_other():
        _, _, _, second_low, grad_second = feed(T, ATR.at[1 - s], PX[...].astype(F32), PG[...])
        GSS[...] = grad_second.astype(BF16)
        wires.copy(GSS, GSR, pair_slot + 2, side)
        kept["second_other"] = second_low

    def ffn_own():
        middle, normed, inverse, second_low, grad_second = feed(0, ATR.at[s], x_ref[0].astype(F32), g_ref[0])
        kept.update(
            att_low=by_heads(ATR.at[s]),
            second_low=tall([second_low, kept["second_other"]]),
            g_low=tall([g_ref[0], PG[...]]),
            grad_second=grad_second,
            middle=middle,
            n_two=normed,
            inverse_two=inverse,
        )

    def ffn_out():
        output = dot(ACT[...], RW[...].reshape(FF // 2, D))
        OUS[...] = output[T:].astype(BF16)
        kept["output"] = kept["middle"] + kept["reduce_bias"] + output[:T]
        kept["bias_expand"] = colsum(GH[...].astype(F32))

    def ffn_send():
        wires.copy(OUS, OUR, pair_slot + 3, side)

    def ffn_back():
        n_two = kept["n_two"]
        wires.arrived(GSR, pair_slot + 2, side)
        grad_second = kept["grad_second"] + GSR[...].astype(F32)
        g = g_ref[0].astype(F32)
        grad_middle = g + norm_back(grad_second * kept["gain_two"], n_two, kept["inverse_two"])
        middle_low = grad_middle.astype(BF16)
        gradient_ref[0] = grad_middle
        grad_att = dot_nt(middle_low, MW[...].reshape(D, D))
        for k in range(HEADS):
            GAS[k] = fold(grad_att[:, k * HEAD : (k + 1) * HEAD]).astype(BF16)
        for _, peer in heads:
            wires.copy(GAS.at[peer], GAR.at[h], ga_slot, dev(b, peer, s))
        GAR[h] = GAS[h]
        kept.update(
            middle_low=middle_low,
            vec_feed=[colsum(grad_second * n_two), colsum(grad_second), colsum(g)],
        )

    def result_step():
        wires.arrived(OUR, pair_slot + 3, side)
        result_ref[0] = (kept["output"] + OUR[...].astype(F32)).astype(BF16)
        stores[0].start()

    def ga_wait():
        wires.arrived(GAR.at[0 : HEADS - 1], ga_slot, side)

    def add_into(W, index, other):
        W[index] = (W[index].astype(F32) + other.astype(F32)).astype(BF16)

    def scatter(W, C, A, B, Z, Z2, finish):
        slot = wires.slots(5)
        lead = (s,) if A is not None else ()

        def core_():
            wires.copy(W.at[1 - b], C, slot, core)

        def merge():
            wires.arrived(C, slot, core)

            def add(i, carry):
                for j in range(YS):
                    add_into(W, (b, i, j), C[i, j])
                return carry

            lax.fori_loop(0, ZS, add, 0)
            if A is not None:
                wires.copy(W.at[b, :, :, 1 - s], A, slot + 1, side)
            else:
                wires.copy(W.at[b, :, 1 - y], B, slot + 2, flip_y)

        def side_():
            wires.arrived(A, slot + 1, side)

            def add(i, carry):
                for j in range(YS):
                    add_into(W, (b, i, j, s), A[i, j])
                return carry

            lax.fori_loop(0, ZS, add, 0)
            wires.copy(W.at[b, :, 1 - y, s], B, slot + 2, flip_y)

        def plane():
            wires.arrived(B, slot + 2, flip_y)
            for i in range(ZS):
                add_into(W, (b, i, y) + lead, B[i])
            for dz in (1, 3):
                wires.copy(W.at[(b, z ^ dz, y) + lead], Z.at[dz // 2], slot + 3, dev(b, h ^ 2, s))

        def pair():
            wires.arrived(Z, slot + 3, side)
            for i in range(2):
                add_into(W, (b, z ^ (2 * i), y) + lead, Z[i])
            wires.copy(W.at[(b, z ^ 2, y) + lead], Z2, slot + 4, dev(b, h ^ 4, s))

        def total_():
            wires.arrived(Z2, slot + 4, side)
            finish(W[(b, z, y) + lead].astype(F32) + Z2[...].astype(F32))

        return SimpleNamespace(core=core_, merge=merge, side=side_, plane=plane, pair=pair, total=total_)

    def scatter_z(W, C, Z, Z2, B, finish):
        slot = wires.slots(4)

        def core_():
            wires.copy(W.at[1 - b], C, slot, core)

        def merge():
            wires.arrived(C, slot, core)

            def add(i, carry):
                for j in range(YS):
                    add_into(W, (b, i, j), C[i, j])
                return carry

            lax.fori_loop(0, ZS, add, 0)
            for dz in (1, 3):
                wires.copy(W.at[b, z ^ dz], Z.at[dz // 2], slot + 1, dev(b, h ^ 2, s))

        def pair():
            wires.arrived(Z, slot + 1, side)
            for i in range(2):
                for j in range(YS):
                    add_into(W, (b, z ^ (2 * i), j), Z[i, j])
            wires.copy(W.at[b, z ^ 2], Z2, slot + 2, dev(b, h ^ 4, s))

        def plane():
            wires.arrived(Z2, slot + 2, side)
            for j in range(YS):
                add_into(W, (b, z, j), Z2[j])
            wires.copy(W.at[b, z, 1 - y], B, slot + 3, flip_y)

        def total_():
            wires.arrived(B, slot + 3, flip_y)
            finish(W[b, z, y].astype(F32) + B[...].astype(F32))

        return SimpleNamespace(core=core_, merge=merge, pair=pair, plane=plane, total=total_)

    def keep_rows(ref, store):
        def put(total):
            ref[...] = total
            store.start()

        return put

    eg_slot = wires.slots(1)

    def swap_columns(total):
        EO[...] = jnp.where(s == 0, total[0], total[1])
        EX[...] = jnp.where(s == 0, total[1], total[0]).astype(BF16)
        wires.copy(EX, EY, eg_slot, side)

    def E_columns():
        wires.arrived(EY, eg_slot, side)
        own, other = EO[...], EY[...].astype(F32)
        even, odd = jnp.where(s == 0, own, other), jnp.where(s == 0, other, own)
        for t in range(FF // 256):
            a_, b_ = even[:, 128 * t : 128 * t + 128], odd[:, 128 * t : 128 * t + 128]
            eg_ref[:, 256 * t : 256 * t + 128] = jnp.where(low_lane, a_, pltpu.roll(b_, 64, 1))
            eg_ref[:, 256 * t + 128 : 256 * t + 256] = jnp.where(low_lane, pltpu.roll(a_, 64, 1), b_)
        stores[2].start()

    def R_make():
        RG[...] = dot_tn(ACT[...], kept["g_low"]).astype(BF16).reshape(RG.shape)

    def E_make():
        for f in range(FF // 2 // step):
            cols = slice(f * step, f * step + step)
            out = dot_tn(kept["second_low"], GH[:, cols])
            EG[:, :, :, :, :, cols] = out.astype(BF16).reshape(2, ZS, YS, SS, r, step)

    def M_make():
        MG[...] = dot_tn(kept["att_low"], kept["middle_low"]).astype(BF16).reshape(MG.shape)

    R = scatter_z(RG, CR, ZR, YR, BR, keep_rows(rg_ref, stores[1]))
    E = scatter(EG, CE, None, BE, ZE, YE, swap_columns)
    M = scatter(MG, CM, AM, BM, ZM, YM, keep_rows(mg_ref, stores[3]))

    cut = iota((T, T), 1) >= iota((T, T), 0)
    dkv_slot = wires.slots(HEADS // 2)
    rkv_slot, rdq_slot = wires.slots(1), wires.slots(1)
    zero_row = jnp.zeros((1, 128), F32)
    sums = {"c": zero_row, "o": zero_row, "kv": zero_row, "q": zero_row}

    def reverse():
        for t in range(n + 4):
            DROWT[t] = jnp.zeros((HEAD, T), F32)
        for k in range(HEADS):
            att, inverse = ATF[k], LIN[k]
            high = att.astype(BF16)
            rest = (att - high.astype(F32)).astype(BF16)
            inv_1 = inverse.astype(BF16).astype(F32)
            inv_2 = (inverse - inv_1).astype(BF16).astype(F32)
            inv_3 = inverse - inv_1 - inv_2
            place = iota((T, T), 1)
            parts_ = jnp.where(place == 0, inv_1, jnp.where(place == 1, inv_2, jnp.where(place == 2, inv_3, 0.0)))
            turned = dot(flip, wide([QC[k], QO[k], high, rest, parts_.astype(BF16)]))
            QCT[k] = turned[:, :128].T[:HEAD].astype(BF16)
            QOT[k] = turned[:, 128:256].T[HEAD:].astype(BF16)
            ATF[k] = turned[:, 256:384] + turned[:, 384:512]
            LIN[k] = jnp.broadcast_to(jnp.sum(turned[:, 512:], axis=1, keepdims=True), (T, T))

    def backward(pair):
        ks = (2 * pair, 2 * pair + 1)
        bases = [n - 1 - (k * SS + s) for k in ks]
        twice = []
        for k in ks:
            ga = GAR[k].astype(F32)
            other = pltpu.roll(ga, HEAD, 1)
            twice.append(tall([jnp.where(low_lane, ga, other), jnp.where(low_lane, other, ga)]).astype(BF16))
        twice = dot(flip, wide(twice))
        spreads, pads, lefts = [], [], []
        none = jnp.zeros((HEAD, T), BF16)
        for i, k in enumerate(ks):
            ga = twice[:, i * 128 : (i + 1) * 128]
            spreads.append(jnp.sum(ga * ATF[k], axis=1, keepdims=True) * 0.5 * LIN[k])
            scaled = ga * LIN[k]
            pads.append(jnp.where(low_lane, 0.0, scaled).astype(BF16))
            lefts.append(tall([QCT[k], none]))
            lefts.append(tall([none, scaled.T[HEAD:].astype(BF16)]))
        pads, lefts = tall(pads), wide(lefts)
        dq, dqo = jnp.zeros((2 * T, 128), F32), [jnp.zeros((T, 128), F32)] * 2
        for ch in range(pair + 1):
            first = ch * 4
            keys = KV[first : first + 4].reshape(4 * T, 128)
            gp = dot_nt(pads, keys)
            lows, stack = [], []
            for i, k in enumerate(ks):
                low, turned, probs = [], [], []
                for t in range(4):
                    p = PST[k, first + t]
                    ds = p.astype(F32) * (gp[i * T : (i + 1) * T, t * T : (t + 1) * T] - spreads[i])
                    probs.append(p)
                    low.append(ds.astype(BF16))
                    turned.append(pltpu.roll(ds, 0, 1, stride=1, stride_axis=0))
                lows.append(wide(low))
                stack += [lows[i], wide(probs)]
                dr = [jnp.where(cut, turned[0], 0.0)]
                for t in range(1, 4):
                    dr.append(jnp.where(cut, turned[t], turned[t - 1]))
                dr.append(jnp.where(cut, 0.0, turned[3]))
                dr = wide(dr).astype(BF16)
                window = OFF[pl.ds(bases[i] + first, 5)].reshape(5 * T, 128)
                dqo[i] = dqo[i] + dot(dr, window)
                back = dot(QOT[k], dr)
                for t in range(5):
                    DROWT[bases[i] + first + t] += back[:, t * T : (t + 1) * T]
            dq = dq + dot(tall(lows), keys)
            add = dot(lefts, tall(stack))
            for t in range(4):
                part = add[:, t * T : (t + 1) * T]
                DKVT[first + t] = part if pair == HEADS // 2 - 1 else DKVT[first + t] + part
        dqo = pltpu.roll(tall(dqo), HEAD, 1)
        sums["c"] = sums["c"] + colsum(dq) * 0.125
        sums["o"] = sums["o"] + colsum(dqo) * 0.125
        dq = ((dq + dqo) * 0.125).astype(BF16)
        dq = dot(flip, wide([dq[:T], dq[T:]]))
        for i, k in enumerate(ks):
            DQF[k] = fold(dq[:, i * 128 : i * 128 + HEAD]).astype(BF16)
            DKVS[k] = DKVT[k * SS + 1 - s].T.astype(BF16)
        for k in ks:
            wires.copy(DKVS.at[k], DKVR.at[k], dkv_slot + pair, side)
        for k in ks:
            wires.copy(DQF.at[k], RDQ.at[h], rdq_slot, dev(b, k, s), when=h != k)
        return dq

    def settle(pair, dq):
        ks = (2 * pair, 2 * pair + 1)
        wires.arrived(DKVR.at[ks[0] : ks[1] + 1], dkv_slot + pair, side)
        lows = []
        for i, k in enumerate(ks):
            dkv = (DKVT[k * SS + s].T + DKVR[k].astype(F32)).astype(BF16)
            DKVF[k] = dkv
            mine = jnp.where(low_lane, dq[:, i * 128 : (i + 1) * 128], 0.0)
            sums["kv"] = sums["kv"] + colsum(dkv.astype(F32))
            sums["q"] = sums["q"] + colsum(mine)
            lows.append(wide([dkv, mine.astype(BF16)]))
        for k in ks:
            wires.copy(DKVF.at[k], RKV.at[h], rkv_slot, dev(b, k, s), when=h != k)
        add = dot_tn(tall([NRM[k] for k in ks]), tall(lows))
        JGA[...] = add if pair == HEADS // 2 - 1 else JGA[...] + add

    kept_dq = {}

    def backward_step(pair):
        kept_dq[pair] = backward(pair)

    def settle_step(pair):
        settle(pair, kept_dq[pair])

    bwd = [functools.partial(backward_step, pair) for pair in range(HEADS // 2)]
    put = [functools.partial(settle_step, pair) for pair in range(HEADS // 2)]

    def offset_grad():
        rows_t = wide([DROWT[t] for t in range(tiles)])
        upper = rows_t.astype(BF16)
        lower = (rows_t - upper.astype(F32)).astype(BF16)
        og_t = dot(tall([upper, lower]), TAB[...])
        og = (og_t[:HEAD] + og_t[HEAD:]).T
        kept["og"] = og

    def jg_make():
        og, own_w, gain_one, shift_one = kept["og"], kept["own_w"], kept["gain_one"], kept["shift_one"]
        vec_feed, bias_expand = kept["vec_feed"], kept["bias_expand"]
        RKV[h] = DKVF[h]
        RDQ[h] = DQF[h]
        og = pltpu.roll(wide([og, jnp.zeros((D, HEAD), F32)]), HEAD, 1)
        grads = JGA[...]
        w_f = own_w.astype(F32)
        col_w = jnp.where(iota((D, 256), 1) < 192, w_f, 0.0)
        ones = jnp.ones((8, 256), F32)
        totals = jnp.broadcast_to(wide([sums["kv"], sums["q"]]), (8, 256))
        highest = lax.Precision.HIGHEST
        shift_mixer = dot(totals, col_w, ((1,), (1,)), highest)[0:1]
        gain_mixer = dot(ones, col_w * grads, ((1,), (1,)), highest)[0:1]
        gain_mixer = (gain_mixer - shift_one * shift_mixer) / gain_one

        def place_head(row):
            row = jnp.where(low_lane, row, 0.0)
            row = row + pltpu.roll(row, HEAD, 1)
            row = wide([row] * (D // 128))
            return jnp.where(iota((1, D), 1) // HEAD == h, row, 0.0)

        partial = tall(
            [gain_mixer, shift_mixer, place_head(sums["c"]), place_head(sums["o"])]
            + vec_feed
            + [jnp.zeros((9, D), F32)]
        )
        JGM[...] = wide([grads[:, :128], grads[:, 128:] + og]).astype(BF16).reshape(JGM.shape)
        low = partial.astype(BF16)
        source, lane = iota((D // 2, 128), 0), iota((D // 2, 128), 1)
        for s_ in range(SS):
            pick = jnp.where(source == lane // each * (SS * each) + s_ * each + lane % each, 1.0, 0.0).astype(BF16)
            for b_ in range(2):
                at = b_ * (FF // 4)
                bias = [bias_expand[:, at + 128 * q : at + 128 * q + 128] for q in range(FF // 512)]
                bias = tall([jnp.zeros((8, 128), F32)] + bias + [jnp.zeros((r - 8 - len(bias), 128), F32)])
                tile = dot(low[:, b_ * (D // 2) : (b_ + 1) * (D // 2)], pick) + jnp.where(s == s_, bias, 0.0)
                VGM[b_, s_] = tile.astype(BF16)
        for i, (b_, s_) in enumerate(group):
            wires.copy(JGM.at[b_, :, s_], JR1.at[i], jr_slot, dev(b_, h, s_))
            wires.copy(VGM.at[b_, s_], VR1.at[i], jr_slot + 1, dev(b_, h, s_))

    each = D // (2 * HEADS * SS)
    jr_slot, jf_slot = wires.slots(2), wires.slots(2)

    def jg_side():
        wires.arrived(JR1, jr_slot, side)
        wires.arrived(VR1, jr_slot + 1, side)
        total, vectors = JGM[b, :, s].astype(F32), VGM[b, s].astype(F32)
        for i in range(len(group)):
            total = total + JR1[i].astype(F32)
            vectors = vectors + VR1[i].astype(F32)
        JF[...] = total.astype(BF16)
        VF[...] = vectors.astype(BF16)
        for _, peer in heads:
            wires.copy(JF.at[peer], JR2.at[h], jf_slot, dev(b, peer, s))
            wires.copy(VF, VR2.at[h], jf_slot + 1, dev(b, peer, s))
        JR2[h] = JF[h]
        VR2[h] = VF[...]

    def rkv_wait():
        wires.arrived(RKV.at[0 : HEADS - 1], rkv_slot, side)
        wires.arrived(RDQ.at[0 : HEADS - 1], rdq_slot, side)

    def grad_step():
        gain_one = kept["gain_one"]
        x = x_ref[0].astype(F32)
        pieces_k, pieces_v = [], []
        for k in range(0, HEADS, 2):
            a_, b_ = RKV[k].astype(F32), RKV[k + 1].astype(F32)
            pieces_k.append(jnp.where(low_lane, a_, pltpu.roll(b_, HEAD, 1)))
            pieces_v.append(jnp.where(low_lane, pltpu.roll(a_, HEAD, 1), b_))
        grad_joint = wide([by_heads(RDQ), wide(pieces_k).astype(BF16), wide(pieces_v).astype(BF16)])
        joint_w = JW[...].reshape(D, 3 * D)
        grad_normed = dot_nt(grad_joint, joint_w)
        n_one, inverse_one = normalize(x)
        gradient_ref[0] += norm_back(grad_normed * gain_one, n_one, inverse_one)
        stores[4].start()

    def jg_wait():
        wires.arrived(JR2.at[0 : HEADS - 1], jf_slot, side)
        wires.arrived(VR2.at[0 : HEADS - 1], jf_slot + 1, side)

    def outs_step():
        got = [JR2[k].astype(F32) for k in range(HEADS)]
        jg_ref[...] = wide([a[:, 128:192] for a in got] + [a[:, 0:64] for a in got] + [a[:, 64:128] for a in got])
        og_ref[...] = wide([a[:, 192:256] for a in got])
        vectors = VR2[0].astype(F32)
        for k in range(1, HEADS):
            vectors = vectors + VR2[k].astype(F32)
        bias = jnp.zeros((1, 128), F32)
        for q in range(HEADS // 2):
            bias = bias + jnp.where(h // 2 == q, vectors[8 + q : 9 + q], 0.0)
        bias = jnp.where(h % 2 == 0, bias, pltpu.roll(bias, 64, 1))
        vectors = pltpu.roll(vectors, (128 - h * each) % 128, 1)
        vg_ref[...] = jnp.where(iota((r, 128), 0) == 7, bias, vectors)
        for store in stores[5:]:
            store.start()

    def reap(keep=12):
        wires.reap(keep)

    order = (
        w1_send,
        x_send,
        m.own,
        e_own,
        r_own,
        w1_pass,
        pair_send,
        functools.partial(x_near, 0),
        functools.partial(x_near, 1),
        e_pair,
        m.start,
        e.start,
        w1_core,
        functools.partial(x_far, 0),
        functools.partial(x_far, 1),
        r_.start,
        functools.partial(reap, 30),
        w1_wait,
        vecs_step,
        first_blocks[0],
        first_blocks[1],
        offs[0],
        offs[1],
        m.near,
        offs[2],
        offs[3],
        first_blocks[2],
        first_blocks[3],
        e.near,
        m.far,
        kv[0],
        fwd[0],
        e.far,
        kv[1],
        kv[2],
        fwd[2],
        r_.near,
        functools.partial(reap, 30),
        kv[3],
        fwd[3],
        r_.far,
        m.diag,
        fwd[1],
        e.over,
        m.over,
        r_.over,
        reap,
        m.wait,
        e.wait,
        r_.wait,
        pair_wait,
        att_wait,
        j.own,
        j.start,
        ffn_other,
        ffn_own,
        R_make,
        R.core,
        E_make,
        E.core,
        reap,
        ffn_back,
        R.merge,
        E.merge,
        ffn_out,
        ffn_send,
        M_make,
        M.core,
        M.merge,
        j.near,
        reverse,
        functools.partial(reap, 20),
        ga_wait,
        bwd[3],
        R.pair,
        E.plane,
        M.side,
        bwd[2],
        bwd[1],
        j.far,
        bwd[0],
        put[3],
        E.pair,
        M.plane,
        put[2],
        R.plane,
        functools.partial(reap, 20),
        offset_grad,
        put[1],
        j.diag,
        put[0],
        jg_make,
        M.pair,
        R.total,
        jg_side,
        j.over,
        rkv_wait,
        E.total,
        j.wait,
        grad_step,
        M.total,
        result_step,
        E_columns,
        reap,
        jg_wait,
        outs_step,
    )
    for step_ in order:
        step_()
    wires.reap()
    for store in stores:
        store.wait()


def spread_refs(n, *refs):
    layer_kernel(n, refs[:9], refs[9:17], refs[17:25], *refs[25:])


def hand_over(*refs):
    count = (len(refs) - 9) // 2
    ins, vectors, outs, smalls = refs[:count], refs[count], refs[count + 1 : 2 * count + 1], refs[2 * count + 1 :]
    for a, o in zip(ins, outs):
        o[...] = a[...]
    for i, o in enumerate(smalls):
        o[...] = vectors[i, 0 : o.shape[0]]


def table_reversed(length, width):
    half = width // 2
    freq = 10000.0 ** (-2.0 * np.arange(half) / width)
    angle = np.arange(length - 1, -1, -1)[:, None] * freq[None, :]
    return np.concatenate([np.sin(angle), np.cos(angle)], axis=1).astype(np.float32).astype(ml_dtypes.bfloat16)


def fast(
    n,
    inputs,
    segments,
    mixer_gain,
    mixer_shift,
    joint_weight,
    offset_weight,
    content_bias,
    offset_bias,
    merge_weight,
    feed_gain,
    feed_shift,
    expand_weight,
    expand_bias,
    reduce_weight,
    reduce_bias,
    cotangent,
):
    T, D = inputs.shape[1:]
    r = joint_weight.shape[0]
    FF = expand_weight.shape[1]
    rr = reduce_weight.shape[0]
    length = segments.shape[1]
    vecs = [mixer_gain, mixer_shift, content_bias, offset_bias, feed_gain, feed_shift, reduce_bias, expand_bias]
    table = jnp.asarray(table_reversed(length, D))
    V = pltpu.VMEM
    half = FF // 2
    blocks, folded = (HEADS, T, 128), (HEADS, T // 2, 128)
    scratch = [
        V((length, D), BF16),
        V((HEADS, T, D), BF16),
        V((HEADS, T, D), BF16),
        V((HEADS, r, 384), BF16),
        V((2, HEADS, SS, r, 384), BF16),
        V((2, ZS, YS, SS, r, 3 * D), BF16),
        V((2, ZS, YS, SS, r, D), BF16),
        V((2, ZS, YS, SS, r, half), BF16),
        V((2, ZS, YS, rr, D), BF16),
        V((r, half), BF16),
        V((T, D), BF16),
        V((T, D), BF16),
        V((n, T, 128), BF16),
        V(blocks, BF16),
        V(blocks, BF16),
        V((HEADS, HEAD, T), BF16),
        V((HEADS, HEAD, T), BF16),
        V((n + 4, T, 128), BF16),
        V((2, n, T, T), F32),
        V((HEADS, n, T, T), BF16),
        V((HEADS, T, T), F32),
        V((HEADS, T, T), F32),
        V(folded, BF16),
        V((SS,) + folded, BF16),
        V((2 * T, half), BF16),
        V((2 * T, half), BF16),
        V((T, D), BF16),
        V((T, D), BF16),
        V((T, D), BF16),
        V((T, D), BF16),
        V(folded, BF16),
        V(folded, BF16),
        V((n, 128, T), F32),
        V((n + 4, HEAD, T), F32),
        V(blocks, BF16),
        V(blocks, BF16),
        V(blocks, BF16),
        V(folded, BF16),
        V(blocks, BF16),
        V(folded, BF16),
        V((2, ZS, YS, SS, r, D), BF16),
        V((2, ZS, YS, SS, r, half), BF16),
        V((2, ZS, YS, rr, D), BF16),
        V((ZS, YS, SS, r, D), BF16),
        V((ZS, YS, SS, r, half), BF16),
        V((ZS, YS, rr, D), BF16),
        V((ZS, YS, r, D), BF16),
        V((ZS, r, D), BF16),
        V((ZS, SS, r, half), BF16),
        V((rr, D), BF16),
        V((2, r, D), BF16),
        V((2, SS, r, half), BF16),
        V((2, YS, rr, D), BF16),
        V((r, D), BF16),
        V((SS, r, half), BF16),
        V((YS, rr, D), BF16),
        V((r, half), F32),
        V((r, half), BF16),
        V((r, half), BF16),
        V((D, 256), F32),
        V((2, HEADS, SS, r, 256), BF16),
        V((2, SS, r, 128), BF16),
        V((3, HEADS, r, 256), BF16),
        V((3, r, 128), BF16),
        V((HEADS, r, 256), BF16),
        V((r, 128), BF16),
        V((HEADS, r, 256), BF16),
        V((HEADS, r, 128), BF16),
        V((1, T, D), BF16),
        V((r, 3 * D), BF16),
        V((r, D), BF16),
        V((1, T, D), BF16),
        V((r, FF), BF16),
        V((r, D), BF16),
        V((rr, D), BF16),
    ]
    out_shape = [
        jax.ShapeDtypeStruct((1, T, D), BF16),
        jax.ShapeDtypeStruct((rr, D), F32),
        jax.ShapeDtypeStruct((r, FF), F32),
        jax.ShapeDtypeStruct((r, D), F32),
        jax.ShapeDtypeStruct((1, T, D), F32),
        jax.ShapeDtypeStruct((r, 3 * D), F32),
        jax.ShapeDtypeStruct((r, D), F32),
        jax.ShapeDtypeStruct((r, 128), F32),
    ]
    scratch += [V(a.shape, a.dtype) for a in out_shape]
    scratch += [pltpu.SemaphoreType.DMA((count,)) for count in (9, SENDS, RECVS)]
    scratch += [V(a.shape, a.dtype) for a in (segments, *vecs)]
    vmem, hbm = pl.BlockSpec(memory_space=V), pl.BlockSpec(memory_space=pl.ANY)
    outs = pl.pallas_call(
        functools.partial(spread_refs, n),
        out_shape=out_shape,
        in_specs=[hbm] * 17,
        out_specs=[hbm] * 8,
        scratch_shapes=scratch,
        compiler_params=pltpu.CompilerParams(
            collective_id=0, has_side_effects=True, vmem_limit_bytes=60 * 2**20
        ),
    )(
        segments,
        *vecs,
        inputs,
        joint_weight,
        offset_weight,
        cotangent,
        expand_weight,
        merge_weight,
        reduce_weight,
        table,
    )
    big, vg = outs[:-1], outs[-1]
    final = pl.pallas_call(
        hand_over,
        out_shape=[jax.ShapeDtypeStruct(a.shape, a.dtype) for a in big]
        + [jax.ShapeDtypeStruct(v.shape, F32) for v in vecs],
        in_specs=[vmem] * (len(big) + 1),
        out_specs=[vmem] * (len(big) + len(vecs)),
    )(*big, vg)
    result, rg, eg, mg, gradient, jg, og = final[: len(big)]
    gain_m, shift_m, bias_c, bias_o, gain_f, shift_f, bias_r, bias_e = final[len(big) :]
    return (
        result,
        gradient,
        gain_m,
        shift_m,
        jg,
        og,
        bias_c,
        bias_o,
        mg,
        gain_f,
        shift_f,
        eg,
        bias_e,
        rg,
        bias_r,
    )


def solution(mesh):
    in_specs = (
        P("batch", "ctx", None),
        P("batch", None),
        P(("batch", "ctx")),
        P(("batch", "ctx")),
        P(("batch", "ctx"), None),
        P(("batch", "ctx"), None),
        P(("batch", "ctx")),
        P(("batch", "ctx")),
        P(("batch", "ctx"), None),
        P(("batch", "ctx")),
        P(("batch", "ctx")),
        P(("batch", "ctx"), None),
        P(("batch", "ctx")),
        P(("batch", "ctx"), None),
        P(("batch", "ctx")),
        P("batch", "ctx", None),
    )
    out_specs = (
        P("batch", "ctx", None),
        P("batch", "ctx", None),
        P(("batch", "ctx")),
        P(("batch", "ctx")),
        P(("batch", "ctx"), None),
        P(("batch", "ctx"), None),
        P(("batch", "ctx")),
        P(("batch", "ctx")),
        P(("batch", "ctx"), None),
        P(("batch", "ctx")),
        P(("batch", "ctx")),
        P(("batch", "ctx"), None),
        P(("batch", "ctx")),
        P(("batch", "ctx"), None),
        P(("batch", "ctx")),
    )
    n, cores = mesh.shape["ctx"], mesh.shape["batch"]

    def layer(*args):
        suits = n == HEADS * SS and cores == 2 and args[0].shape[1] == 128 and args[4].shape[0] == 16
        return fast(n, *args) if suits else local(*args)

    return jax.shard_map(layer, mesh=mesh, in_specs=in_specs, out_specs=out_specs, check_vma=False)
```

```python
import functools
import math
from types import SimpleNamespace

import jax
import jax.numpy as jnp
import ml_dtypes
import numpy as np
from jax import lax
from jax.experimental import pallas as pl
from jax.experimental.pallas import tpu as pltpu
from jax.sharding import PartitionSpec as P

HEADS = 8
HEAD = 64


masked_score = -1e30


def shifted(array, axis, by):
    peers = lax.axis_size(axis)
    pairs = [(i, i + by) for i in range(peers) if 0 <= i + by < peers]
    return lax.ppermute(array, axis, pairs)


def shifted_2(value, axis, steps):
    count = lax.axis_size(axis)
    pairs = [(source, (source + steps) % count) for source in range(count)]
    return lax.ppermute(value, axis, pairs)


def layer_norm(values, gain, shift):
    center = values - jnp.mean(values, axis=-1, keepdims=True)
    spread = jnp.mean(center * center, axis=-1, keepdims=True)
    return center * lax.rsqrt(spread + 1e-05) * gain + shift


def sinusoid(first, count, width):
    half = width // 2
    freq = jnp.power(10000.0, -2.0 * jnp.arange(half, dtype=jnp.float32) / width)
    place = (first + jnp.arange(count, dtype=jnp.int32)).astype(jnp.float32)
    angle = place[:, None] * freq[None, :]
    return jnp.concatenate([jnp.sin(angle), jnp.cos(angle)], axis=1)


def contract_rows(left, right):
    return lax.dot_general(
        left, right, (((0,), (0,)), ((), ())), preferred_element_type=jnp.float32
    )


def contract_cols(left, right):
    return lax.dot_general(
        left, right, (((1,), (1,)), ((), ())), preferred_element_type=jnp.float32
    )


def split_contract(table, grad_rows):
    upper = grad_rows.astype(jnp.bfloat16)
    lower = (grad_rows - upper.astype(jnp.float32)).astype(jnp.bfloat16)
    return contract_rows(table, upper) + contract_rows(table, lower)


def fold_blocks(step, carry, pieces, limit):
    count = pieces[0].shape[0]
    size = min(count, limit)
    number = count // size
    stacked = tuple((item.reshape((number, size) + item.shape[1:]) for item in pieces))

    def inner(state, item):
        offset, parts = item
        return (step(state, parts, offset * size), None)

    folded, _ = lax.scan(inner, carry, (jnp.arange(number, dtype=jnp.int32), stacked))
    return folded


def realign(relative_scores, count):
    heads, rows, width = relative_scores.shape
    flat = relative_scores.reshape(heads, rows * width)
    band = flat[:, rows - 1 : rows - 1 + rows * (width - 1)]
    return band.reshape(heads, rows, width - 1)[:, :, :count]


def pair_terms(
    query_content_term, query_position_term, keys, query_first, key_first, seg_row, offsets_pad
):
    rows, heads, size = query_content_term.shape
    count = keys.shape[0]
    length = offsets_pad.shape[0] // 2
    anchor = query_first - key_first - count + length
    attention_span = lax.dynamic_slice_in_dim(offsets_pad, anchor, rows + count, 0)[::-1].reshape(
        rows + count, heads, size
    )
    content = jnp.einsum(
        "ahd,bhd->hab", query_content_term, keys, preferred_element_type=jnp.float32
    )
    relative_scores = jnp.einsum(
        "scx,icx->csi", query_position_term, attention_span, preferred_element_type=jnp.float32
    )
    scores = (content + realign(relative_scores, count)) * (1.0 / math.sqrt(size))
    query_seg = lax.dynamic_slice_in_dim(seg_row, query_first, rows, 0)
    key_seg = lax.dynamic_slice_in_dim(seg_row, key_first, count, 0)
    query_pos = query_first + jnp.arange(rows, dtype=jnp.int32)
    key_pos = key_first + jnp.arange(count, dtype=jnp.int32)
    allowed = (key_pos[None, :] <= query_pos[:, None]) & (key_seg[None, :] == query_seg[:, None])
    return (scores, allowed, attention_span, anchor)


def pair_grads(
    query_content_term,
    query_position_term,
    keys,
    values,
    query_first,
    key_first,
    seg_row,
    offsets_pad,
    logsum,
    spread,
    grad_attended,
):
    rows, heads, size = query_content_term.shape
    count = keys.shape[0]
    scale = 1.0 / math.sqrt(size)
    scores, allowed, attention_span, anchor = pair_terms(
        query_content_term, query_position_term, keys, query_first, key_first, seg_row, offsets_pad
    )
    probs = jnp.where(allowed[None], jnp.exp(scores - logsum[..., None]), 0.0)
    grad_values = jnp.einsum(
        "hab,ahd->bhd",
        probs.astype(jnp.bfloat16),
        grad_attended,
        preferred_element_type=jnp.float32,
    )
    grad_probs = jnp.einsum(
        "ahd,bhd->hab", grad_attended, values, preferred_element_type=jnp.float32
    )
    grad_scores = (probs * (grad_probs - spread[..., None])).astype(jnp.bfloat16)
    grad_content = scale * jnp.einsum(
        "hab,bhd->ahd", grad_scores, keys, preferred_element_type=jnp.float32
    )
    grad_keys = scale * jnp.einsum(
        "hab,ahd->bhd", grad_scores, query_content_term, preferred_element_type=jnp.float32
    )
    blank = jnp.zeros((heads, rows, rows + count), jnp.float32)
    _, realign_back = jax.vjp(lambda relative_scores: realign(relative_scores, count), blank)
    gradient_relative_scores = realign_back(grad_scores.astype(jnp.float32))[0].astype(jnp.bfloat16)
    grad_offset = scale * jnp.einsum(
        "nsk,kno->sno", gradient_relative_scores, attention_span, preferred_element_type=jnp.float32
    )
    grad_window = scale * jnp.einsum(
        "cqu,qcn->ucn",
        gradient_relative_scores,
        query_position_term,
        preferred_element_type=jnp.float32,
    )
    grad_window = grad_window.reshape(rows + count, heads * size)[::-1]
    return (grad_content, grad_offset, grad_keys, grad_values, grad_window, anchor)


def add_window(grad_rows, grad_window, anchor):
    current = lax.dynamic_slice_in_dim(grad_rows, anchor, grad_window.shape[0], 0)
    return lax.dynamic_update_slice_in_dim(grad_rows, current + grad_window, anchor, 0)


def local(
    inputs,
    segments,
    mixer_gain,
    mixer_shift,
    joint_weight,
    offset_weight,
    content_bias,
    offset_bias,
    merge_weight,
    feed_gain,
    feed_shift,
    expand_weight,
    expand_bias,
    reduce_weight,
    reduce_bias,
    cotangent,
):
    (
        first_gain,
        first_shift,
        joint_matrix,
        offset_matrix,
        bias_content,
        bias_position,
        merge_matrix,
    ) = (
        lax.all_gather(mixer_gain, ("batch", "ctx"), axis=0, tiled=True),
        lax.all_gather(mixer_shift, ("batch", "ctx"), axis=0, tiled=True),
        lax.all_gather(joint_weight, ("batch", "ctx"), axis=0, tiled=True),
        lax.all_gather(offset_weight, ("batch", "ctx"), axis=0, tiled=True),
        lax.all_gather(content_bias, ("batch", "ctx"), axis=0, tiled=True),
        lax.all_gather(offset_bias, ("batch", "ctx"), axis=0, tiled=True),
        lax.all_gather(merge_weight, ("batch", "ctx"), axis=0, tiled=True),
    )
    tokens = inputs[0].astype(jnp.float32)
    rows, width = tokens.shape
    seg_row = segments[0]
    length = seg_row.shape[0]
    place = lax.axis_index("ctx")
    cycle = lax.axis_size("ctx")
    block_first = place * rows
    heads_shape = (rows, HEADS, HEAD)
    gain_one = first_gain.astype(jnp.float32)
    shift_one = first_shift.astype(jnp.float32)
    normed = layer_norm(tokens, gain_one, shift_one)
    normed_low = normed.astype(jnp.bfloat16)
    joint = jnp.dot(normed_low, joint_matrix, preferred_element_type=jnp.float32)
    query = joint[:, :width]
    keys = joint[:, width : 2 * width].astype(jnp.bfloat16).reshape(heads_shape)
    values = joint[:, 2 * width :].astype(jnp.bfloat16).reshape(heads_shape)
    query_content_term = (
        (query + bias_content.astype(jnp.float32)).astype(jnp.bfloat16).reshape(heads_shape)
    )
    query_position_term = (
        (query + bias_position.astype(jnp.float32)).astype(jnp.bfloat16).reshape(heads_shape)
    )
    everyone = lax.axis_size(("batch", "ctx"))
    share = length // everyone
    table = sinusoid(lax.axis_index(("batch", "ctx")) * share, share, width).astype(jnp.bfloat16)
    offsets_local = jnp.dot(table, offset_matrix, preferred_element_type=jnp.float32).astype(
        jnp.bfloat16
    )
    offsets_all = lax.all_gather(offsets_local, ("batch", "ctx"), axis=0, tiled=True)
    offsets_pad = jnp.concatenate([jnp.zeros_like(offsets_all), offsets_all], axis=0)

    def stats_block(carry, pieces, start):
        peak, total = carry
        scores, allowed, attention_span, anchor = pair_terms(
            query_content_term,
            query_position_term,
            pieces[0],
            block_first,
            start,
            seg_row,
            offsets_pad,
        )
        masked = jnp.where(allowed[None], scores, masked_score)
        new_peak = jnp.maximum(peak, jnp.max(masked, axis=-1))
        added = jnp.sum(
            jnp.where(allowed[None], jnp.exp(masked - new_peak[..., None]), 0.0), axis=-1
        )
        return (new_peak, total * jnp.exp(peak - new_peak) + added)

    peak_start = jnp.full((HEADS, rows), masked_score, jnp.float32)
    total_start = jnp.zeros((HEADS, rows), jnp.float32)
    peak, total = fold_blocks(
        stats_block,
        (peak_start, total_start),
        (lax.all_gather(keys, "ctx", axis=0, tiled=True),),
        rows,
    )
    logsum = peak + jnp.log(total)

    def output_block(carry, pieces, start):
        scores, allowed, attention_span, anchor = pair_terms(
            query_content_term,
            query_position_term,
            pieces[0],
            block_first,
            start,
            seg_row,
            offsets_pad,
        )
        probs = jnp.where(allowed[None], jnp.exp(scores - logsum[..., None]), 0.0).astype(
            jnp.bfloat16
        )
        return carry + jnp.einsum(
            "hab,bhd->ahd", probs, pieces[1], preferred_element_type=jnp.float32
        )

    mixed = fold_blocks(
        output_block,
        jnp.zeros(heads_shape, jnp.float32),
        (
            lax.all_gather(keys, "ctx", axis=0, tiled=True),
            lax.all_gather(values, "ctx", axis=0, tiled=True),
        ),
        rows,
    )
    attended_low = mixed.reshape(rows, width).astype(jnp.bfloat16)
    middle = tokens + jnp.dot(attended_low, merge_matrix, preferred_element_type=jnp.float32)
    second_gain, second_shift, expand_matrix, expand_vector, reduce_matrix, reduce_vector = (
        lax.all_gather(feed_gain, ("batch", "ctx"), axis=0, tiled=True),
        lax.all_gather(feed_shift, ("batch", "ctx"), axis=0, tiled=True),
        lax.all_gather(expand_weight, ("batch", "ctx"), axis=0, tiled=True),
        lax.all_gather(expand_bias, ("batch", "ctx"), axis=0, tiled=True),
        lax.all_gather(reduce_weight, ("batch", "ctx"), axis=0, tiled=True),
        lax.all_gather(reduce_bias, ("batch", "ctx"), axis=0, tiled=True),
    )
    gain_two = second_gain.astype(jnp.float32)
    shift_two = second_shift.astype(jnp.float32)
    second_low = layer_norm(middle, gain_two, shift_two).astype(jnp.bfloat16)
    hidden = jnp.dot(
        second_low, expand_matrix, preferred_element_type=jnp.float32
    ) + expand_vector.astype(jnp.float32)
    active_low = jax.nn.gelu(hidden, approximate=True).astype(jnp.bfloat16)
    output = (
        middle
        + jnp.dot(active_low, reduce_matrix, preferred_element_type=jnp.float32)
        + reduce_vector.astype(jnp.float32)
    )
    result = output.astype(jnp.bfloat16)[None]
    grad_out = cotangent[0]
    grad_outf = grad_out.astype(jnp.float32)
    grad_reduce_bias = jnp.sum(grad_outf, axis=0)
    grad_reduce = contract_rows(active_low, grad_out)
    grad_active = contract_cols(grad_out, reduce_matrix)
    _, gelu_back = jax.vjp(lambda value: jax.nn.gelu(value, approximate=True), hidden)
    grad_hidden = gelu_back(grad_active)[0].astype(jnp.bfloat16)
    grad_expand_bias = jnp.sum(grad_hidden.astype(jnp.float32), axis=0)
    grad_expand = contract_rows(second_low, grad_hidden)
    grad_second = contract_cols(grad_hidden, expand_matrix)
    _, second_back = jax.vjp(layer_norm, middle, gain_two, shift_two)
    grad_mid, grad_gain_two, grad_shift_two = second_back(grad_second)
    grad_middle = grad_outf + grad_mid
    feed_sums = (
        lax.psum_scatter(grad_gain_two, ("batch", "ctx"), scatter_dimension=0, tiled=True),
        lax.psum_scatter(grad_shift_two, ("batch", "ctx"), scatter_dimension=0, tiled=True),
        lax.psum_scatter(grad_expand, ("batch", "ctx"), scatter_dimension=0, tiled=True),
        lax.psum_scatter(grad_expand_bias, ("batch", "ctx"), scatter_dimension=0, tiled=True),
        lax.psum_scatter(grad_reduce, ("batch", "ctx"), scatter_dimension=0, tiled=True),
        lax.psum_scatter(grad_reduce_bias, ("batch", "ctx"), scatter_dimension=0, tiled=True),
    )
    middle_low = grad_middle.astype(jnp.bfloat16)
    grad_merge = contract_rows(attended_low, middle_low)
    grad_attended = (
        contract_cols(middle_low, merge_matrix).astype(jnp.bfloat16).reshape(heads_shape)
    )
    spread = jnp.einsum("ahd,ahd->ha", grad_attended.astype(jnp.float32), mixed)
    zero_heads = jnp.zeros(heads_shape, jnp.float32)
    zero_rows = jnp.zeros((2 * length, width), jnp.float32)

    def cycle_step(turn, carry):
        visiting, carried, grad_content, grad_offset, grad_rows = carry
        owner = (place - turn) % cycle
        terms = pair_grads(
            query_content_term,
            query_position_term,
            visiting[0],
            visiting[1],
            block_first,
            owner * rows,
            seg_row,
            offsets_pad,
            logsum,
            spread,
            grad_attended,
        )
        carried = carried + jnp.stack([terms[2], terms[3]])
        grad_rows = add_window(grad_rows, terms[4], terms[5])
        visiting = shifted(visiting, "ctx", 1)
        carried = shifted_2(carried.astype(jnp.bfloat16), "ctx", 1).astype(carried.dtype)
        return (visiting, carried, grad_content + terms[0], grad_offset + terms[1], grad_rows)

    start_state = (
        jnp.stack([keys, values]),
        jnp.zeros((2,) + heads_shape, jnp.float32),
        zero_heads,
        zero_heads,
        zero_rows,
    )
    _, carried, grad_content, grad_offset, grad_rows = lax.fori_loop(
        0, cycle, cycle_step, start_state
    )
    grad_keys = carried[0]
    grad_values = carried[1]
    grad_content_bias = jnp.sum(grad_content, axis=0).reshape(width)
    gradient_position_bias = jnp.sum(grad_offset, axis=0).reshape(width)
    grad_joint = jnp.concatenate(
        [
            (grad_content + grad_offset).reshape(rows, width),
            grad_keys.reshape(rows, width),
            grad_values.reshape(rows, width),
        ],
        axis=1,
    ).astype(jnp.bfloat16)
    grad_joint_matrix = contract_rows(normed_low, grad_joint)
    grad_normed = contract_cols(grad_joint, joint_matrix)
    _, first_back = jax.vjp(layer_norm, tokens, gain_one, shift_one)
    grad_tokens, grad_gain_one, grad_shift_one = first_back(grad_normed)
    gradient = (grad_middle + grad_tokens)[None]
    full_table = sinusoid(0, length, width).astype(jnp.bfloat16)
    grad_offset_matrix = split_contract(full_table, grad_rows[length:])
    mixer_sums = (
        lax.psum_scatter(grad_gain_one, ("batch", "ctx"), scatter_dimension=0, tiled=True),
        lax.psum_scatter(grad_shift_one, ("batch", "ctx"), scatter_dimension=0, tiled=True),
        lax.psum_scatter(grad_joint_matrix, ("batch", "ctx"), scatter_dimension=0, tiled=True),
        lax.psum_scatter(grad_offset_matrix, ("batch", "ctx"), scatter_dimension=0, tiled=True),
        lax.psum_scatter(grad_content_bias, ("batch", "ctx"), scatter_dimension=0, tiled=True),
        lax.psum_scatter(gradient_position_bias, ("batch", "ctx"), scatter_dimension=0, tiled=True),
        lax.psum_scatter(grad_merge, ("batch", "ctx"), scatter_dimension=0, tiled=True),
    )
    return (
        result,
        gradient,
        mixer_sums[0],
        mixer_sums[1],
        mixer_sums[2],
        mixer_sums[3],
        mixer_sums[4],
        mixer_sums[5],
        mixer_sums[6],
        feed_sums[0],
        feed_sums[1],
        feed_sums[2],
        feed_sums[3],
        feed_sums[4],
        feed_sums[5],
    )


F32, BF16 = jnp.float32, jnp.bfloat16
MESH = pl.DeviceIdType.MESH
NEG = -1e30
ZS, YS, SS = 4, 2, 2


def dot(a, b, dims=((1,), (0,)), precision=None):
    return lax.dot_general(a, b, (dims, ((), ())), preferred_element_type=F32, precision=precision)


def dot_nt(a, b):
    return dot(a, b, ((1,), (1,)))


def dot_tn(a, b):
    return dot(a, b, ((0,), (0,)))


def iota(shape, axis):
    return lax.broadcasted_iota(jnp.int32, shape, axis)


def wide(tiles):
    return jnp.concatenate(tiles, axis=1)


def tall(tiles):
    return jnp.concatenate(tiles, axis=0)


def fold(x):
    half = x.shape[0] // 2
    return wide([x[:half], x[half:]])


def unfold(x):
    return tall([x[:, :HEAD], x[:, HEAD:]])


def normalize(x):
    center = x - jnp.mean(x, axis=-1, keepdims=True)
    inverse = lax.rsqrt(jnp.mean(center * center, axis=-1, keepdims=True) + 1e-05)
    return center * inverse, inverse


def norm_back(e, n, inverse):
    return inverse * (e - jnp.mean(e, axis=-1, keepdims=True) - n * jnp.mean(e * n, axis=-1, keepdims=True))


def colsum(x):
    return jnp.sum(x, axis=0, keepdims=True)


class Wires:
    def __init__(self, sends, recvs):
        self.sends, self.recvs, self.received, self.pending = sends, recvs, 0, []
        self.free = list(range(SENDS))
        self.peak = 0

    def slots(self, count):
        first = self.received
        self.received += count
        return first

    def copy(self, src, dst, slot, to, when=None):
        index = self.free.pop(0)
        self.peak = max(self.peak, SENDS - len(self.free))
        made = pltpu.make_async_remote_copy(
            src_ref=src,
            dst_ref=dst,
            send_sem=self.sends.at[index],
            recv_sem=self.recvs.at[slot],
            device_id=to,
            device_id_type=MESH,
        )
        self.pending.append((made, when, index))
        if when is None:
            made.start()
        else:
            pl.when(when)(made.start)

    def arrived(self, dst, slot, to):
        pltpu.make_async_remote_copy(
            src_ref=dst,
            dst_ref=dst,
            send_sem=self.sends.at[0],
            recv_sem=self.recvs.at[slot],
            device_id=to,
            device_id_type=MESH,
        ).wait_recv()

    def reap(self, keep=0):
        count = len(self.pending) - keep
        for made, when, index in self.pending[:count]:
            if when is None:
                made.wait_send()
            else:
                pl.when(when)(made.wait_send)
            self.free.append(index)
        self.pending = self.pending[count:]


SENDS, RECVS = 70, 74
def layer_kernel(
    n,
    small,
    ins,
    outs,
    *scratch,
):
    (
        TAB,
        TOK,
        NRM,
        W1S,
        W1,
        JW,
        MW,
        EW,
        RW,
        ES,
        PX,
        PG,
        KV,
        QC,
        QO,
        QCT,
        QOT,
        OFF,
        SCR,
        PST,
        ATF,
        LIN,
        ATS,
        ATR,
        ACT,
        GH,
        GSS,
        GSR,
        OUS,
        OUR,
        GAS,
        GAR,
        DKVT,
        DROWT,
        DKVS,
        DKVR,
        DKVF,
        DQF,
        RKV,
        RDQ,
        MG,
        EG,
        RG,
        CM,
        CE,
        CR,
        AM,
        BM,
        BE,
        BR,
        ZM,
        ZE,
        ZR,
        YM,
        YE,
        YR,
        EO,
        EX,
        EY,
        JGA,
        JGM,
        VGM,
        JR1,
        VR1,
        JF,
        VF,
        JR2,
        VR2,
        x_ref,
        jw_ref,
        ow_ref,
        g_ref,
        ew_ref,
        mw_ref,
        rw_ref,
        result_ref,
        rg_ref,
        eg_ref,
        mg_ref,
        gradient_ref,
        jg_ref,
        og_ref,
        vg_ref,
        local,
        sends,
        recvs,
        seg_ref,
        *vec_refs,
    ) = scratch
    T = x_ref.shape[1]
    D = x_ref.shape[2]
    FF = ew_ref.shape[1]
    r = jw_ref.shape[0]
    b = lax.axis_index("batch")
    c = lax.axis_index("ctx")
    h, s = c // SS, c % SS
    z, y = h // YS, h % YS
    shard = b * n + c

    def dev(b_, h_, s_):
        return {"batch": b_, "ctx": h_ * SS + s_}

    core = dev(1 - b, h, s)
    side = dev(b, h, 1 - s)
    flip_y = dev(b, h ^ 1, s)
    heads = [(q, h ^ q) for q in range(1, HEADS)]
    group = [(1 - b, s), (b, 1 - s), (1 - b, 1 - s)]
    wires = Wires(sends, recvs)

    barrier = pltpu.get_barrier_semaphore()
    for _, peer in heads:
        pl.semaphore_signal(barrier, inc=1, device_id=dev(b, peer, s), device_id_type=MESH)
    for b_, s_ in group:
        pl.semaphore_signal(barrier, inc=1, device_id=dev(b_, h, s_), device_id_type=MESH)

    here = (x_ref, jw_ref, ow_ref, g_ref, ew_ref, mw_ref, rw_ref, TAB)
    loads = [pltpu.make_async_copy(src, dst, local.at[i]) for i, (src, dst) in enumerate(zip(ins, here))]
    few = [pltpu.make_async_copy(src, dst, local.at[8]) for src, dst in zip(small, (seg_ref, *vec_refs))]
    for load in few + loads:
        load.start()
    made = (result_ref, rg_ref, eg_ref, mg_ref, gradient_ref, jg_ref, og_ref, vg_ref)
    stores = [
        pltpu.make_async_copy(src, dst, local.at[i]) for i, (src, dst) in enumerate(zip(made, outs))
    ]

    for load in few:
        load.wait()
    lines = []
    for ref in vec_refs:
        line = ref[...].astype(F32).reshape(1, ref.shape[0])
        lines.append(wide([line, jnp.zeros((1, 128 - ref.shape[0]), F32)]))
    vec = tall(lines + [jnp.zeros((r - len(lines), 128), F32)])
    by_16 = pltpu.roll(vec, (shard % 8) * 16, 1)
    by_64 = pltpu.roll(vec, (shard // 2 % 2) * 64, 1)
    vec = jnp.where(iota(vec.shape, 0) == 7, by_64, by_16).astype(BF16)
    for load in loads[:3]:
        load.wait()
    jw, ow = jw_ref[...], ow_ref[...]
    for k in range(HEADS):
        at = k * HEAD
        W1S[k] = wide(
            [
                jw[:, D + at : D + at + HEAD],
                jw[:, 2 * D + at : 2 * D + at + HEAD],
                jw[:, at : at + HEAD],
                ow[:, at : at + HEAD],
                vec,
            ]
        )
    TOK[h] = x_ref[0]
    W1[b, h, s] = W1S[h]
    for load in loads[3:7]:
        load.wait()
    pl.semaphore_wait(barrier, len(heads) + len(group))
    inner = (z == 1) | (z == 2)
    edge = (z == 0) | (z == 3)
    low_lane = iota((1, 128), 1) < HEAD

    w1_slot, w1_group = wires.slots(1), wires.slots(2)

    def w1_send():
        for _, peer in heads:
            wires.copy(W1S.at[peer], W1.at[b, h, s], w1_slot, dev(b, peer, s))

    def w1_pass():
        wires.arrived(W1.at[b, 0 : HEADS - 1, s], w1_slot, side)
        wires.copy(W1.at[b, :, s], W1.at[b, :, s], w1_group, side)
        wires.copy(W1.at[b, :, s], W1.at[b, :, s], w1_group + 1, core)

    def w1_core():
        wires.arrived(W1.at[b, :, 1 - s], w1_group, side)
        wires.copy(W1.at[b, :, 1 - s], W1.at[b, :, 1 - s], w1_group + 1, core)

    def w1_wait():
        wires.arrived(W1.at[1 - b], w1_group + 1, core)

    tok_slot, far_slot = wires.slots(6), wires.slots(ZS)

    def tok_at(z_):
        return TOK.at[z_ * YS + y]

    def half_at(z_, half):
        return TOK.at[z_ * YS + y, half * (T // 2) : (half + 1) * (T // 2)]

    def x_send():
        for half in range(2):
            src = x_ref.at[0, half * (T // 2) : (half + 1) * (T // 2)]
            for dz, when in ((2, edge), (1, None), (2, inner), (3, inner)):
                slot = tok_slot + 3 * half + dz - 1
                wires.copy(src, half_at(z, half), slot, dev(b, h ^ (2 * dz), s), when=when)
        wires.copy(x_ref.at[0], tok_at(z), far_slot + z, flip_y)

    def take(dz, half, when=None):
        block = half_at(z ^ dz, half)

        def wait():
            wires.arrived(block, tok_slot + 3 * half + dz - 1, side)

        if when is None:
            wait()
        else:
            pl.when(when)(wait)
        if dz == 2:
            wires.copy(block, block, tok_slot + 3 * half + 2, dev(b, h ^ 2, s), when=inner)
        wires.copy(block, block, far_slot + (z ^ dz), flip_y, when=when)

    def x_near(half):
        take(1, half, edge)
        take(2, half)
        take(1, half, inner)

    def x_far(half):
        take(3, half)

    def along_z(at, slot, relay=True):
        for dz in (1, 2, 3):
            far = dz == 3 and relay
            wires.copy(at(z), at(z), slot + dz - 1, dev(b, h ^ (2 * dz), s), when=inner if far else None)

    def from_z(at, slot, dz, relay=True):
        block = at(z ^ dz)
        wires.arrived(block, slot + dz - 1, side)
        if dz == 2 and relay:
            wires.copy(block, block, slot + 2, dev(b, h ^ 2, s), when=inner)

    def gather(W, ref):
        z_slot, y_slot, s_slot, slot, core_slot = (wires.slots(k) for k in (3, 1, 1, 1, 1))

        def at(z_):
            return W.at[b, z_, y, s]

        def own(z_):
            wires.copy(at(z_), at(z_), y_slot, flip_y)
            wires.copy(at(z_), at(z_), s_slot, side)

        def across(y_, s_):
            wires.copy(W.at[b, :, y_, s_], W.at[b, :, y_, s_], core_slot, core)

        def own_():
            W[b, z, y, s] = ref[...]
            own(z)

        def start():
            along_z(at, z_slot)

        def near():
            for dz in (2, 1):
                from_z(at, z_slot, dz)
                own(z ^ dz)

        def far_():
            from_z(at, z_slot, 3)
            own(z ^ 3)
            across(y, s)

        def diag():
            wires.arrived(W.at[b, :, 1 - y, s], y_slot, flip_y)
            wires.copy(W.at[b, :, 1 - y, s], W.at[b, :, 1 - y, s], slot, side)
            wires.arrived(W.at[b, :, y, 1 - s], s_slot, side)
            across(1 - y, s)
            across(y, 1 - s)

        def over():
            wires.arrived(W.at[b, :, 1 - y, 1 - s], slot, side)
            across(1 - y, 1 - s)

        def wait():
            wires.arrived(W.at[1 - b], core_slot, core)

        return SimpleNamespace(own=own_, start=start, near=near, far=far_, diag=diag, over=over, wait=wait)

    m, j = gather(MW, mw_ref), gather(JW, jw_ref)

    def gather_half(W, relay=True):
        z_slot, y_slot, core_slot = wires.slots(3), wires.slots(1), wires.slots(1)

        def at(z_):
            return W.at[b, z_, y]

        def across(y_):
            wires.copy(W.at[b, :, y_], W.at[b, :, y_], core_slot, core)

        def to_y(z_):
            wires.copy(at(z_), at(z_), y_slot, flip_y)

        def start():
            along_z(at, z_slot, relay)
            to_y(z)

        def near():
            for dz in (2, 1):
                from_z(at, z_slot, dz, relay)
                to_y(z ^ dz)

        def far_():
            from_z(at, z_slot, 3)
            to_y(z ^ 3)
            across(y)

        def over():
            wires.arrived(W.at[b, :, 1 - y], y_slot, flip_y)
            across(1 - y)

        def wait():
            wires.arrived(W.at[1 - b], core_slot, core)

        return SimpleNamespace(start=start, near=near, far=far_, over=over, wait=wait)

    es_slot, pair_slot = wires.slots(1), wires.slots(4)

    def r_own():
        RW[b, z, y] = rw_ref[...]

    def e_own():
        evens, odds = [], []
        for t in range(FF // 256):
            first = ew_ref[:, 256 * t : 256 * t + 128].astype(F32)
            second = ew_ref[:, 256 * t + 128 : 256 * t + 256].astype(F32)
            evens.append(jnp.where(low_lane, first, pltpu.roll(second, 64, 1)))
            odds.append(jnp.where(low_lane, pltpu.roll(first, 64, 1), second))
        evens, odds = wide(evens).astype(BF16), wide(odds).astype(BF16)
        EW[b, z, y, s] = jnp.where(s == 0, evens, odds)
        ES[...] = jnp.where(s == 0, odds, evens)
        wires.copy(ES, EW.at[b, z, y, s], es_slot, side)

    def e_pair():
        wires.arrived(EW.at[b, z, y, 1 - s], es_slot, side)

    e, r_ = gather_half(EW), gather_half(RW, relay=False)

    def pair_send():
        wires.copy(x_ref.at[0], PX, pair_slot, side)
        wires.copy(g_ref.at[0], PG, pair_slot + 1, side)

    def pair_wait():
        wires.arrived(PX, pair_slot, side)
        wires.arrived(PG, pair_slot + 1, side)

    kept = {}

    def vecs_step():
        vecs = W1[:, :, :, :, 256:384].reshape(2 * n, r, 128).astype(F32)
        rows = wide([jnp.sum(vecs[8 * t : 8 * t + 8], axis=0) for t in range(D // 128)])
        gain_one, shift_one, bias_c, bias_o = rows[0:1], rows[1:2], rows[2:3], rows[3:4]
        gain_two, shift_two, reduce_bias = rows[4:5], rows[5:6], rows[6:7]
        even = wide([vecs[4 * t] + vecs[4 * t + 2] for t in range(FF // 256)])[7:8]
        odd = wide([vecs[4 * t + 1] + vecs[4 * t + 3] for t in range(FF // 256)])[7:8]
        expand_bias = jnp.where(s == 0, even, odd)

        def own_head(row):
            pairs = jnp.zeros((1, 128), F32)
            for t in range(HEADS // 2):
                pairs = pairs + jnp.where(h // 2 == t, row[:, 128 * t : 128 * t + 128], 0.0)
            turned = pltpu.roll(pairs, HEAD, 1)
            return jnp.where(h % 2 == 0, pairs, turned)

        bias_c, bias_o = own_head(bias_c), own_head(bias_o)
        own_w = W1[:, :, :, :, 0:256].reshape(D, 256)
        kept.update(
            gain_one=gain_one,
            shift_one=shift_one,
            bias_c=bias_c,
            bias_o=bias_o,
            gain_two=gain_two,
            shift_two=shift_two,
            reduce_bias=reduce_bias,
            expand_bias=expand_bias,
            own_w=own_w,
        )

    kv_slot = wires.slots(HEADS // 2)

    def project(*blocks):
        normed, _ = normalize(tall([TOK[k] for k in blocks]).astype(F32))
        normed = (normed * kept["gain_one"] + kept["shift_one"]).astype(BF16)
        out = dot(normed, kept["own_w"])
        query = out[:, 128:]
        first = jnp.where(low_lane, (query + kept["bias_c"]).astype(BF16).astype(F32) * 0.125, 0.0).astype(BF16)
        second = (query + kept["bias_o"]).astype(BF16).astype(F32) * 0.125
        second = pltpu.roll(jnp.where(low_lane, second, 0.0), HEAD, 1).astype(BF16)
        for i, k in enumerate(blocks):
            rows = slice(i * T, i * T + T)
            NRM[k] = normed[rows]
            KV[k * SS + s] = out[rows, :128].astype(BF16)
            wires.copy(KV.at[k * SS + s], KV.at[k * SS + s], kv_slot + k // 2, side)
            QC[k] = first[rows]
            QO[k] = second[rows]

    def far_block(dz):
        far = h ^ (2 * dz + 1)
        wires.arrived(TOK.at[far], far_slot + (z ^ dz), side)
        return far

    def project_steps(near, far):
        project(*[h ^ (2 * dz) for dz in near], *[far_block(dz) for dz in far])

    first_blocks = [functools.partial(project_steps, *blocks) for blocks in (((0,), (0,)), ((1, 2), ()), ((), (1, 2)), ((3,), (3,)))]

    tiles = TAB.shape[0] // T

    parts = 4
    per = tiles // parts

    def offset_part(part):
        if part == 0:
            loads[7].wait()
            for t in range(4):
                OFF[tiles + t] = jnp.zeros((T, 128), BF16)
        rows = slice(part * per * T, (part + 1) * per * T)
        out = dot(TAB[rows, :], kept["own_w"][:, 128:])
        OFF[part * per : (part + 1) * per] = out.astype(BF16).reshape(per, T, 128)

    offs = [functools.partial(offset_part, part) for part in range(parts)]

    tril = iota((T, T), 1) <= iota((T, T), 0)
    diff = iota((T, T), 1) - iota((T, T), 0)
    eye = iota((T, T), 1) == iota((T, T), 0)
    flip = jnp.where(iota((T, T), 0) + iota((T, T), 1) == T - 1, 1.0, 0.0).astype(BF16)
    att_slot = wires.slots(2)

    def forward(pair):
        ks = (2 * pair, 2 * pair + 1)
        blocks = [k * SS + s for k in ks]
        q_both = tall([QC[k] for k in ks])
        qo = [QO[k] for k in ks]
        seg_q = []
        for block in blocks:
            seg_row = seg_ref[0:1, pl.ds(pl.multiple_of(block * T, T), T)].astype(F32)
            seg_q.append(jnp.sum(jnp.where(eye, seg_row, 0.0), axis=1, keepdims=True))
        peaks = [jnp.full((T, T), NEG, F32)] * 2
        for ch in range(pair + 1):
            first = ch * 4
            content = dot_nt(q_both, KV[first : first + 4].reshape(4 * T, 128))
            for i, block in enumerate(blocks):
                window = OFF[pl.ds(n - 1 - block + first, 5)].reshape(5 * T, 128)
                rel = dot_nt(qo[i], window)
                turned = [pltpu.roll(rel[:, t * T : (t + 1) * T], 1, 1, stride=1, stride_axis=0) for t in range(5)]
                for t in range(4):
                    seg_k = seg_ref[0:1, (first + t) * T : (first + t + 1) * T].astype(F32)
                    ok = (diff <= (block - first - t) * T) & (seg_k == seg_q[i])
                    score = content[i * T : (i + 1) * T, t * T : (t + 1) * T]
                    score = jnp.where(ok, score + jnp.where(tril, turned[t], turned[t + 1]), NEG)
                    SCR[i, first + t] = score
                    peaks[i] = jnp.maximum(peaks[i], score)
        peaks = [jnp.max(peak, axis=1, keepdims=True) for peak in peaks]
        totals, out = [jnp.zeros((T, T), F32)] * 2, jnp.zeros((2 * T, 128), F32)
        for ch in range(pair + 1):
            first = ch * 4
            lows = []
            for i, k in enumerate(ks):
                low = []
                for t in range(4):
                    p = jnp.exp(SCR[i, first + t] - peaks[i])
                    totals[i] = totals[i] + p
                    low.append(p.astype(BF16))
                lows.append(wide(low))
                turned = dot(flip, lows[i]).astype(BF16)
                for t in range(4):
                    PST[k, first + t] = turned[:, t * T : (t + 1) * T]
            out = out + dot(tall(lows), KV[first : first + 4].reshape(4 * T, 128))
        for i, k in enumerate(ks):
            inverse = 1.0 / jnp.sum(totals[i], axis=1, keepdims=True)
            att = out[i * T : (i + 1) * T, HEAD:] * inverse
            ATF[k] = wide([att, att])
            LIN[k] = jnp.broadcast_to(inverse, (T, T))
            ATS[k] = fold(att).astype(BF16)
        for k in ks:
            wires.copy(ATS.at[k], ATR.at[s, h], att_slot, dev(b, k, s), when=h != k)
            wires.copy(ATS.at[k], ATR.at[s, h], att_slot + 1, dev(b, k, 1 - s))

    def keys_wait(pair):
        wires.arrived(KV.at[pair * 2 : pair * 2 + 2], kv_slot + pair, side)

    kv = [functools.partial(keys_wait, pair) for pair in range(HEADS // 2)]
    fwd = [functools.partial(forward, pair) for pair in range(HEADS // 2)]

    def att_wait():
        ATR[s, h] = ATS[h]
        wires.arrived(ATR.at[s, 0 : HEADS - 1], att_slot, side)
        wires.arrived(ATR.at[1 - s], att_slot + 1, side)

    def by_heads(R):
        return wide([unfold(R[k].astype(F32)) for k in range(HEADS)]).astype(BF16)

    ga_slot = wires.slots(1)
    step = min(512, FF)

    def feed(first, heads_out, tokens, g_low):
        middle = tokens + dot(by_heads(heads_out), MW[...].reshape(D, D))
        normed, inverse = normalize(middle)
        second_low = (normed * kept["gain_two"] + kept["shift_two"]).astype(BF16)
        grad_second = jnp.zeros((T, D), F32)
        root, cube = math.sqrt(2.0 / math.pi), 0.044715
        rows = slice(first, first + T)
        for f in range(FF // 2 // step):
            cols = slice(f * step, f * step + step)
            e_w = EW[:, :, :, :, :, cols].reshape(D, step)
            r_w = RW[...].reshape(FF // 2, D)[cols]
            v = dot(second_low, e_w) + kept["expand_bias"][:, cols]
            tanh = jnp.tanh(root * (v + cube * v * v * v))
            ACT[rows, cols] = (0.5 * v * (1.0 + tanh)).astype(BF16)
            slope = 0.5 * (1.0 + tanh) + 0.5 * v * (1.0 - tanh * tanh) * (root * (1.0 + 3.0 * cube * v * v))
            grad_hidden = (dot_nt(g_low, r_w) * slope).astype(BF16)
            GH[rows, cols] = grad_hidden
            grad_second = grad_second + dot_nt(grad_hidden, e_w)
        return middle, normed, inverse, second_low, grad_second

    def ffn_other():
        _, _, _, second_low, grad_second = feed(T, ATR.at[1 - s], PX[...].astype(F32), PG[...])
        GSS[...] = grad_second.astype(BF16)
        wires.copy(GSS, GSR, pair_slot + 2, side)
        kept["second_other"] = second_low

    def ffn_own():
        middle, normed, inverse, second_low, grad_second = feed(0, ATR.at[s], x_ref[0].astype(F32), g_ref[0])
        kept.update(
            att_low=by_heads(ATR.at[s]),
            second_low=tall([second_low, kept["second_other"]]),
            g_low=tall([g_ref[0], PG[...]]),
            grad_second=grad_second,
            middle=middle,
            n_two=normed,
            inverse_two=inverse,
        )

    def ffn_out():
        output = dot(ACT[...], RW[...].reshape(FF // 2, D))
        OUS[...] = output[T:].astype(BF16)
        kept["output"] = kept["middle"] + kept["reduce_bias"] + output[:T]
        kept["bias_expand"] = colsum(GH[...].astype(F32))

    def ffn_send():
        wires.copy(OUS, OUR, pair_slot + 3, side)

    def ffn_back():
        n_two = kept["n_two"]
        wires.arrived(GSR, pair_slot + 2, side)
        grad_second = kept["grad_second"] + GSR[...].astype(F32)
        g = g_ref[0].astype(F32)
        grad_middle = g + norm_back(grad_second * kept["gain_two"], n_two, kept["inverse_two"])
        middle_low = grad_middle.astype(BF16)
        gradient_ref[0] = grad_middle
        grad_att = dot_nt(middle_low, MW[...].reshape(D, D))
        for k in range(HEADS):
            GAS[k] = fold(grad_att[:, k * HEAD : (k + 1) * HEAD]).astype(BF16)
        for _, peer in heads:
            wires.copy(GAS.at[peer], GAR.at[h], ga_slot, dev(b, peer, s))
        GAR[h] = GAS[h]
        kept.update(
            middle_low=middle_low,
            vec_feed=[colsum(grad_second * n_two), colsum(grad_second), colsum(g)],
        )

    def result_step():
        wires.arrived(OUR, pair_slot + 3, side)
        result_ref[0] = (kept["output"] + OUR[...].astype(F32)).astype(BF16)
        stores[0].start()

    def ga_wait():
        wires.arrived(GAR.at[0 : HEADS - 1], ga_slot, side)

    def add_into(W, index, other):
        W[index] = (W[index].astype(F32) + other.astype(F32)).astype(BF16)

    def scatter(W, C, A, B, Z, Z2, finish):
        slot = wires.slots(5)
        lead = (s,) if A is not None else ()

        def core_():
            wires.copy(W.at[1 - b], C, slot, core)

        def merge():
            wires.arrived(C, slot, core)

            def add(i, carry):
                for j in range(YS):
                    add_into(W, (b, i, j), C[i, j])
                return carry

            lax.fori_loop(0, ZS, add, 0)
            if A is not None:
                wires.copy(W.at[b, :, :, 1 - s], A, slot + 1, side)
            else:
                wires.copy(W.at[b, :, 1 - y], B, slot + 2, flip_y)

        def side_():
            wires.arrived(A, slot + 1, side)

            def add(i, carry):
                for j in range(YS):
                    add_into(W, (b, i, j, s), A[i, j])
                return carry

            lax.fori_loop(0, ZS, add, 0)
            wires.copy(W.at[b, :, 1 - y, s], B, slot + 2, flip_y)

        def plane():
            wires.arrived(B, slot + 2, flip_y)
            for i in range(ZS):
                add_into(W, (b, i, y) + lead, B[i])
            for dz in (1, 3):
                wires.copy(W.at[(b, z ^ dz, y) + lead], Z.at[dz // 2], slot + 3, dev(b, h ^ 2, s))

        def pair():
            wires.arrived(Z, slot + 3, side)
            for i in range(2):
                add_into(W, (b, z ^ (2 * i), y) + lead, Z[i])
            wires.copy(W.at[(b, z ^ 2, y) + lead], Z2, slot + 4, dev(b, h ^ 4, s))

        def total_():
            wires.arrived(Z2, slot + 4, side)
            finish(W[(b, z, y) + lead].astype(F32) + Z2[...].astype(F32))

        return SimpleNamespace(core=core_, merge=merge, side=side_, plane=plane, pair=pair, total=total_)

    def scatter_z(W, C, Z, Z2, B, finish):
        slot = wires.slots(4)

        def core_():
            wires.copy(W.at[1 - b], C, slot, core)

        def merge():
            wires.arrived(C, slot, core)

            def add(i, carry):
                for j in range(YS):
                    add_into(W, (b, i, j), C[i, j])
                return carry

            lax.fori_loop(0, ZS, add, 0)
            for dz in (1, 3):
                wires.copy(W.at[b, z ^ dz], Z.at[dz // 2], slot + 1, dev(b, h ^ 2, s))

        def pair():
            wires.arrived(Z, slot + 1, side)
            for i in range(2):
                for j in range(YS):
                    add_into(W, (b, z ^ (2 * i), j), Z[i, j])
            wires.copy(W.at[b, z ^ 2], Z2, slot + 2, dev(b, h ^ 4, s))

        def plane():
            wires.arrived(Z2, slot + 2, side)
            for j in range(YS):
                add_into(W, (b, z, j), Z2[j])
            wires.copy(W.at[b, z, 1 - y], B, slot + 3, flip_y)

        def total_():
            wires.arrived(B, slot + 3, flip_y)
            finish(W[b, z, y].astype(F32) + B[...].astype(F32))

        return SimpleNamespace(core=core_, merge=merge, pair=pair, plane=plane, total=total_)

    def keep_rows(ref, store):
        def put(total):
            ref[...] = total
            store.start()

        return put

    eg_slot = wires.slots(1)

    def swap_columns(total):
        EO[...] = jnp.where(s == 0, total[0], total[1])
        EX[...] = jnp.where(s == 0, total[1], total[0]).astype(BF16)
        wires.copy(EX, EY, eg_slot, side)

    def E_columns():
        wires.arrived(EY, eg_slot, side)
        own, other = EO[...], EY[...].astype(F32)
        even, odd = jnp.where(s == 0, own, other), jnp.where(s == 0, other, own)
        for t in range(FF // 256):
            a_, b_ = even[:, 128 * t : 128 * t + 128], odd[:, 128 * t : 128 * t + 128]
            eg_ref[:, 256 * t : 256 * t + 128] = jnp.where(low_lane, a_, pltpu.roll(b_, 64, 1))
            eg_ref[:, 256 * t + 128 : 256 * t + 256] = jnp.where(low_lane, pltpu.roll(a_, 64, 1), b_)
        stores[2].start()

    def R_make():
        RG[...] = dot_tn(ACT[...], kept["g_low"]).astype(BF16).reshape(RG.shape)

    def E_make():
        for f in range(FF // 2 // step):
            cols = slice(f * step, f * step + step)
            out = dot_tn(kept["second_low"], GH[:, cols])
            EG[:, :, :, :, :, cols] = out.astype(BF16).reshape(2, ZS, YS, SS, r, step)

    def M_make():
        MG[...] = dot_tn(kept["att_low"], kept["middle_low"]).astype(BF16).reshape(MG.shape)

    R = scatter_z(RG, CR, ZR, YR, BR, keep_rows(rg_ref, stores[1]))
    E = scatter(EG, CE, None, BE, ZE, YE, swap_columns)
    M = scatter(MG, CM, AM, BM, ZM, YM, keep_rows(mg_ref, stores[3]))

    cut = iota((T, T), 1) >= iota((T, T), 0)
    dkv_slot = wires.slots(HEADS // 2)
    rkv_slot, rdq_slot = wires.slots(1), wires.slots(1)
    zero_row = jnp.zeros((1, 128), F32)
    sums = {"c": zero_row, "o": zero_row, "kv": zero_row, "q": zero_row}

    def reverse():
        for t in range(n + 4):
            DROWT[t] = jnp.zeros((HEAD, T), F32)
        for k in range(HEADS):
            att, inverse = ATF[k], LIN[k]
            high = att.astype(BF16)
            rest = (att - high.astype(F32)).astype(BF16)
            inv_1 = inverse.astype(BF16).astype(F32)
            inv_2 = (inverse - inv_1).astype(BF16).astype(F32)
            inv_3 = inverse - inv_1 - inv_2
            place = iota((T, T), 1)
            parts_ = jnp.where(place == 0, inv_1, jnp.where(place == 1, inv_2, jnp.where(place == 2, inv_3, 0.0)))
            turned = dot(flip, wide([QC[k], QO[k], high, rest, parts_.astype(BF16)]))
            QCT[k] = turned[:, :128].T[:HEAD].astype(BF16)
            QOT[k] = turned[:, 128:256].T[HEAD:].astype(BF16)
            ATF[k] = turned[:, 256:384] + turned[:, 384:512]
            LIN[k] = jnp.broadcast_to(jnp.sum(turned[:, 512:], axis=1, keepdims=True), (T, T))

    def backward(pair):
        ks = (2 * pair, 2 * pair + 1)
        bases = [n - 1 - (k * SS + s) for k in ks]
        twice = []
        for k in ks:
            ga = GAR[k].astype(F32)
            other = pltpu.roll(ga, HEAD, 1)
            twice.append(tall([jnp.where(low_lane, ga, other), jnp.where(low_lane, other, ga)]).astype(BF16))
        twice = dot(flip, wide(twice))
        spreads, pads, lefts = [], [], []
        none = jnp.zeros((HEAD, T), BF16)
        for i, k in enumerate(ks):
            ga = twice[:, i * 128 : (i + 1) * 128]
            spreads.append(jnp.sum(ga * ATF[k], axis=1, keepdims=True) * 0.5 * LIN[k])
            scaled = ga * LIN[k]
            pads.append(jnp.where(low_lane, 0.0, scaled).astype(BF16))
            lefts.append(tall([QCT[k], none]))
            lefts.append(tall([none, scaled.T[HEAD:].astype(BF16)]))
        pads, lefts = tall(pads), wide(lefts)
        dq, dqo = jnp.zeros((2 * T, 128), F32), [jnp.zeros((T, 128), F32)] * 2
        for ch in range(pair + 1):
            first = ch * 4
            keys = KV[first : first + 4].reshape(4 * T, 128)
            gp = dot_nt(pads, keys)
            lows, stack = [], []
            for i, k in enumerate(ks):
                low, turned, probs = [], [], []
                for t in range(4):
                    p = PST[k, first + t]
                    ds = p.astype(F32) * (gp[i * T : (i + 1) * T, t * T : (t + 1) * T] - spreads[i])
                    probs.append(p)
                    low.append(ds.astype(BF16))
                    turned.append(pltpu.roll(ds, 0, 1, stride=1, stride_axis=0))
                lows.append(wide(low))
                stack += [lows[i], wide(probs)]
                dr = [jnp.where(cut, turned[0], 0.0)]
                for t in range(1, 4):
                    dr.append(jnp.where(cut, turned[t], turned[t - 1]))
                dr.append(jnp.where(cut, 0.0, turned[3]))
                dr = wide(dr).astype(BF16)
                window = OFF[pl.ds(bases[i] + first, 5)].reshape(5 * T, 128)
                dqo[i] = dqo[i] + dot(dr, window)
                back = dot(QOT[k], dr)
                for t in range(5):
                    DROWT[bases[i] + first + t] += back[:, t * T : (t + 1) * T]
            dq = dq + dot(tall(lows), keys)
            add = dot(lefts, tall(stack))
            for t in range(4):
                part = add[:, t * T : (t + 1) * T]
                DKVT[first + t] = part if pair == HEADS // 2 - 1 else DKVT[first + t] + part
        dqo = pltpu.roll(tall(dqo), HEAD, 1)
        sums["c"] = sums["c"] + colsum(dq) * 0.125
        sums["o"] = sums["o"] + colsum(dqo) * 0.125
        dq = ((dq + dqo) * 0.125).astype(BF16)
        dq = dot(flip, wide([dq[:T], dq[T:]]))
        for i, k in enumerate(ks):
            DQF[k] = fold(dq[:, i * 128 : i * 128 + HEAD]).astype(BF16)
            DKVS[k] = DKVT[k * SS + 1 - s].T.astype(BF16)
        for k in ks:
            wires.copy(DKVS.at[k], DKVR.at[k], dkv_slot + pair, side)
        for k in ks:
            wires.copy(DQF.at[k], RDQ.at[h], rdq_slot, dev(b, k, s), when=h != k)
        return dq

    def settle(pair, dq):
        ks = (2 * pair, 2 * pair + 1)
        wires.arrived(DKVR.at[ks[0] : ks[1] + 1], dkv_slot + pair, side)
        lows = []
        for i, k in enumerate(ks):
            dkv = (DKVT[k * SS + s].T + DKVR[k].astype(F32)).astype(BF16)
            DKVF[k] = dkv
            mine = jnp.where(low_lane, dq[:, i * 128 : (i + 1) * 128], 0.0)
            sums["kv"] = sums["kv"] + colsum(dkv.astype(F32))
            sums["q"] = sums["q"] + colsum(mine)
            lows.append(wide([dkv, mine.astype(BF16)]))
        for k in ks:
            wires.copy(DKVF.at[k], RKV.at[h], rkv_slot, dev(b, k, s), when=h != k)
        add = dot_tn(tall([NRM[k] for k in ks]), tall(lows))
        JGA[...] = add if pair == HEADS // 2 - 1 else JGA[...] + add

    kept_dq = {}

    def backward_step(pair):
        kept_dq[pair] = backward(pair)

    def settle_step(pair):
        settle(pair, kept_dq[pair])

    bwd = [functools.partial(backward_step, pair) for pair in range(HEADS // 2)]
    put = [functools.partial(settle_step, pair) for pair in range(HEADS // 2)]

    def offset_grad():
        rows_t = wide([DROWT[t] for t in range(tiles)])
        upper = rows_t.astype(BF16)
        lower = (rows_t - upper.astype(F32)).astype(BF16)
        og_t = dot(tall([upper, lower]), TAB[...])
        og = (og_t[:HEAD] + og_t[HEAD:]).T
        kept["og"] = og

    def jg_make():
        og, own_w, gain_one, shift_one = kept["og"], kept["own_w"], kept["gain_one"], kept["shift_one"]
        vec_feed, bias_expand = kept["vec_feed"], kept["bias_expand"]
        RKV[h] = DKVF[h]
        RDQ[h] = DQF[h]
        og = pltpu.roll(wide([og, jnp.zeros((D, HEAD), F32)]), HEAD, 1)
        grads = JGA[...]
        col_w = jnp.where(iota((D, 256), 1) < 192, own_w, jnp.zeros_like(own_w))
        totals = wide([sums["kv"], sums["q"]])
        high = totals.astype(BF16).astype(F32)
        parts_ = tall([high, totals - high, jnp.zeros((6, 256), F32)]).astype(BF16)
        shift_mixer = colsum(dot_nt(parts_, col_w))
        product = col_w.astype(F32) * grads
        high = product.astype(BF16)
        rest = (product - high.astype(F32)).astype(BF16)
        gain_mixer = dot_nt(jnp.ones((8, 512), BF16), wide([high, rest]))[0:1]
        gain_mixer = (gain_mixer - shift_one * shift_mixer) / gain_one

        def place_head(row):
            row = jnp.where(low_lane, row, 0.0)
            row = row + pltpu.roll(row, HEAD, 1)
            row = wide([row] * (D // 128))
            return jnp.where(iota((1, D), 1) // HEAD == h, row, 0.0)

        partial = tall(
            [gain_mixer, shift_mixer, place_head(sums["c"]), place_head(sums["o"])]
            + vec_feed
            + [jnp.zeros((9, D), F32)]
        )
        JGM[...] = wide([grads[:, :128], grads[:, 128:] + og]).astype(BF16).reshape(JGM.shape)
        low = partial.astype(BF16)
        source, lane = iota((D // 2, 128), 0), iota((D // 2, 128), 1)
        for s_ in range(SS):
            pick = jnp.where(source == lane // each * (SS * each) + s_ * each + lane % each, 1.0, 0.0).astype(BF16)
            for b_ in range(2):
                at = b_ * (FF // 4)
                bias = [bias_expand[:, at + 128 * q : at + 128 * q + 128] for q in range(FF // 512)]
                bias = tall([jnp.zeros((8, 128), F32)] + bias + [jnp.zeros((r - 8 - len(bias), 128), F32)])
                tile = dot(low[:, b_ * (D // 2) : (b_ + 1) * (D // 2)], pick) + jnp.where(s == s_, bias, 0.0)
                VGM[b_, s_] = tile.astype(BF16)
        for i, (b_, s_) in enumerate(group):
            wires.copy(JGM.at[b_, :, s_], JR1.at[i], jr_slot, dev(b_, h, s_))
            wires.copy(VGM.at[b_, s_], VR1.at[i], jr_slot + 1, dev(b_, h, s_))

    each = D // (2 * HEADS * SS)
    jr_slot, jf_slot = wires.slots(2), wires.slots(2)

    def jg_side():
        wires.arrived(JR1, jr_slot, side)
        wires.arrived(VR1, jr_slot + 1, side)
        total, vectors = JGM[b, :, s].astype(F32), VGM[b, s].astype(F32)
        for i in range(len(group)):
            total = total + JR1[i].astype(F32)
            vectors = vectors + VR1[i].astype(F32)
        JF[...] = total.astype(BF16)
        VF[...] = vectors.astype(BF16)
        for _, peer in heads:
            wires.copy(JF.at[peer], JR2.at[h], jf_slot, dev(b, peer, s))
            wires.copy(VF, VR2.at[h], jf_slot + 1, dev(b, peer, s))
        JR2[h] = JF[h]
        VR2[h] = VF[...]

    def rkv_wait():
        wires.arrived(RKV.at[0 : HEADS - 1], rkv_slot, side)
        wires.arrived(RDQ.at[0 : HEADS - 1], rdq_slot, side)

    def grad_step():
        gain_one = kept["gain_one"]
        x = x_ref[0].astype(F32)
        pieces_k, pieces_v = [], []
        for k in range(0, HEADS, 2):
            a_, b_ = RKV[k].astype(F32), RKV[k + 1].astype(F32)
            pieces_k.append(jnp.where(low_lane, a_, pltpu.roll(b_, HEAD, 1)))
            pieces_v.append(jnp.where(low_lane, pltpu.roll(a_, HEAD, 1), b_))
        grad_joint = wide([by_heads(RDQ), wide(pieces_k).astype(BF16), wide(pieces_v).astype(BF16)])
        joint_w = JW[...].reshape(D, 3 * D)
        grad_normed = dot_nt(grad_joint, joint_w)
        n_one, inverse_one = normalize(x)
        gradient_ref[0] += norm_back(grad_normed * gain_one, n_one, inverse_one)
        stores[4].start()

    def jg_wait():
        wires.arrived(JR2.at[0 : HEADS - 1], jf_slot, side)
        wires.arrived(VR2.at[0 : HEADS - 1], jf_slot + 1, side)

    def outs_step():
        got = [JR2[k].astype(F32) for k in range(HEADS)]
        jg_ref[...] = wide([a[:, 128:192] for a in got] + [a[:, 0:64] for a in got] + [a[:, 64:128] for a in got])
        og_ref[...] = wide([a[:, 192:256] for a in got])
        vectors = VR2[0].astype(F32)
        for k in range(1, HEADS):
            vectors = vectors + VR2[k].astype(F32)
        bias = jnp.zeros((1, 128), F32)
        for q in range(HEADS // 2):
            bias = bias + jnp.where(h // 2 == q, vectors[8 + q : 9 + q], 0.0)
        bias = jnp.where(h % 2 == 0, bias, pltpu.roll(bias, 64, 1))
        vectors = pltpu.roll(vectors, (128 - h * each) % 128, 1)
        vg_ref[...] = jnp.where(iota((r, 128), 0) == 7, bias, vectors)
        for store in stores[5:]:
            store.start()

    def reap(keep=12):
        wires.reap(keep)

    order = (
        w1_send,
        x_send,
        m.own,
        e_own,
        r_own,
        w1_pass,
        pair_send,
        functools.partial(x_near, 0),
        functools.partial(x_near, 1),
        e_pair,
        m.start,
        e.start,
        w1_core,
        functools.partial(x_far, 0),
        functools.partial(x_far, 1),
        r_.start,
        functools.partial(reap, 30),
        w1_wait,
        vecs_step,
        first_blocks[0],
        first_blocks[1],
        offs[0],
        offs[1],
        m.near,
        offs[2],
        offs[3],
        first_blocks[2],
        first_blocks[3],
        e.near,
        m.far,
        kv[0],
        fwd[0],
        e.far,
        kv[1],
        kv[2],
        fwd[2],
        r_.near,
        functools.partial(reap, 30),
        kv[3],
        fwd[3],
        r_.far,
        m.diag,
        fwd[1],
        e.over,
        m.over,
        r_.over,
        reap,
        m.wait,
        e.wait,
        r_.wait,
        pair_wait,
        att_wait,
        j.own,
        j.start,
        ffn_other,
        ffn_own,
        R_make,
        R.core,
        E_make,
        E.core,
        reap,
        ffn_back,
        R.merge,
        E.merge,
        ffn_out,
        ffn_send,
        M_make,
        M.core,
        M.merge,
        j.near,
        reverse,
        functools.partial(reap, 20),
        ga_wait,
        bwd[3],
        R.pair,
        E.plane,
        M.side,
        bwd[2],
        bwd[1],
        j.far,
        bwd[0],
        put[3],
        E.pair,
        M.plane,
        put[2],
        R.plane,
        functools.partial(reap, 20),
        offset_grad,
        put[1],
        j.diag,
        put[0],
        jg_make,
        M.pair,
        R.total,
        jg_side,
        j.over,
        rkv_wait,
        E.total,
        j.wait,
        grad_step,
        M.total,
        result_step,
        E_columns,
        reap,
        jg_wait,
        outs_step,
    )
    for step_ in order:
        step_()
    wires.reap()
    for store in stores:
        store.wait()


def spread_refs(n, *refs):
    layer_kernel(n, refs[:9], refs[9:17], refs[17:25], *refs[25:])


def hand_over(*refs):
    count = (len(refs) - 9) // 2
    ins, vectors, outs, smalls = refs[:count], refs[count], refs[count + 1 : 2 * count + 1], refs[2 * count + 1 :]
    for a, o in zip(ins, outs):
        o[...] = a[...]
    for i, o in enumerate(smalls):
        o[...] = vectors[i, 0 : o.shape[0]]


def table_reversed(length, width):
    half = width // 2
    freq = 10000.0 ** (-2.0 * np.arange(half) / width)
    angle = np.arange(length - 1, -1, -1)[:, None] * freq[None, :]
    return np.concatenate([np.sin(angle), np.cos(angle)], axis=1).astype(np.float32).astype(ml_dtypes.bfloat16)


def fast(
    n,
    inputs,
    segments,
    mixer_gain,
    mixer_shift,
    joint_weight,
    offset_weight,
    content_bias,
    offset_bias,
    merge_weight,
    feed_gain,
    feed_shift,
    expand_weight,
    expand_bias,
    reduce_weight,
    reduce_bias,
    cotangent,
):
    T, D = inputs.shape[1:]
    r = joint_weight.shape[0]
    FF = expand_weight.shape[1]
    rr = reduce_weight.shape[0]
    length = segments.shape[1]
    vecs = [mixer_gain, mixer_shift, content_bias, offset_bias, feed_gain, feed_shift, reduce_bias, expand_bias]
    table = jnp.asarray(table_reversed(length, D))
    V = pltpu.VMEM
    half = FF // 2
    blocks, folded = (HEADS, T, 128), (HEADS, T // 2, 128)
    scratch = [
        V((length, D), BF16),
        V((HEADS, T, D), BF16),
        V((HEADS, T, D), BF16),
        V((HEADS, r, 384), BF16),
        V((2, HEADS, SS, r, 384), BF16),
        V((2, ZS, YS, SS, r, 3 * D), BF16),
        V((2, ZS, YS, SS, r, D), BF16),
        V((2, ZS, YS, SS, r, half), BF16),
        V((2, ZS, YS, rr, D), BF16),
        V((r, half), BF16),
        V((T, D), BF16),
        V((T, D), BF16),
        V((n, T, 128), BF16),
        V(blocks, BF16),
        V(blocks, BF16),
        V((HEADS, HEAD, T), BF16),
        V((HEADS, HEAD, T), BF16),
        V((n + 4, T, 128), BF16),
        V((2, n, T, T), F32),
        V((HEADS, n, T, T), BF16),
        V((HEADS, T, T), F32),
        V((HEADS, T, T), F32),
        V(folded, BF16),
        V((SS,) + folded, BF16),
        V((2 * T, half), BF16),
        V((2 * T, half), BF16),
        V((T, D), BF16),
        V((T, D), BF16),
        V((T, D), BF16),
        V((T, D), BF16),
        V(folded, BF16),
        V(folded, BF16),
        V((n, 128, T), F32),
        V((n + 4, HEAD, T), F32),
        V(blocks, BF16),
        V(blocks, BF16),
        V(blocks, BF16),
        V(folded, BF16),
        V(blocks, BF16),
        V(folded, BF16),
        V((2, ZS, YS, SS, r, D), BF16),
        V((2, ZS, YS, SS, r, half), BF16),
        V((2, ZS, YS, rr, D), BF16),
        V((ZS, YS, SS, r, D), BF16),
        V((ZS, YS, SS, r, half), BF16),
        V((ZS, YS, rr, D), BF16),
        V((ZS, YS, r, D), BF16),
        V((ZS, r, D), BF16),
        V((ZS, SS, r, half), BF16),
        V((rr, D), BF16),
        V((2, r, D), BF16),
        V((2, SS, r, half), BF16),
        V((2, YS, rr, D), BF16),
        V((r, D), BF16),
        V((SS, r, half), BF16),
        V((YS, rr, D), BF16),
        V((r, half), F32),
        V((r, half), BF16),
        V((r, half), BF16),
        V((D, 256), F32),
        V((2, HEADS, SS, r, 256), BF16),
        V((2, SS, r, 128), BF16),
        V((3, HEADS, r, 256), BF16),
        V((3, r, 128), BF16),
        V((HEADS, r, 256), BF16),
        V((r, 128), BF16),
        V((HEADS, r, 256), BF16),
        V((HEADS, r, 128), BF16),
        V((1, T, D), BF16),
        V((r, 3 * D), BF16),
        V((r, D), BF16),
        V((1, T, D), BF16),
        V((r, FF), BF16),
        V((r, D), BF16),
        V((rr, D), BF16),
    ]
    out_shape = [
        jax.ShapeDtypeStruct((1, T, D), BF16),
        jax.ShapeDtypeStruct((rr, D), F32),
        jax.ShapeDtypeStruct((r, FF), F32),
        jax.ShapeDtypeStruct((r, D), F32),
        jax.ShapeDtypeStruct((1, T, D), F32),
        jax.ShapeDtypeStruct((r, 3 * D), F32),
        jax.ShapeDtypeStruct((r, D), F32),
        jax.ShapeDtypeStruct((r, 128), F32),
    ]
    scratch += [V(a.shape, a.dtype) for a in out_shape]
    scratch += [pltpu.SemaphoreType.DMA((count,)) for count in (9, SENDS, RECVS)]
    scratch += [V(a.shape, a.dtype) for a in (segments, *vecs)]
    vmem, hbm = pl.BlockSpec(memory_space=V), pl.BlockSpec(memory_space=pl.ANY)
    outs = pl.pallas_call(
        functools.partial(spread_refs, n),
        out_shape=out_shape,
        in_specs=[hbm] * 17,
        out_specs=[hbm] * 8,
        scratch_shapes=scratch,
        compiler_params=pltpu.CompilerParams(
            collective_id=0, has_side_effects=True, vmem_limit_bytes=60 * 2**20
        ),
    )(
        segments,
        *vecs,
        inputs,
        joint_weight,
        offset_weight,
        cotangent,
        expand_weight,
        merge_weight,
        reduce_weight,
        table,
    )
    big, vg = outs[:-1], outs[-1]
    final = pl.pallas_call(
        hand_over,
        out_shape=[jax.ShapeDtypeStruct(a.shape, a.dtype) for a in big]
        + [jax.ShapeDtypeStruct(v.shape, F32) for v in vecs],
        in_specs=[vmem] * (len(big) + 1),
        out_specs=[vmem] * (len(big) + len(vecs)),
    )(*big, vg)
    result, rg, eg, mg, gradient, jg, og = final[: len(big)]
    gain_m, shift_m, bias_c, bias_o, gain_f, shift_f, bias_r, bias_e = final[len(big) :]
    return (
        result,
        gradient,
        gain_m,
        shift_m,
        jg,
        og,
        bias_c,
        bias_o,
        mg,
        gain_f,
        shift_f,
        eg,
        bias_e,
        rg,
        bias_r,
    )


def solution(mesh):
    in_specs = (
        P("batch", "ctx", None),
        P("batch", None),
        P(("batch", "ctx")),
        P(("batch", "ctx")),
        P(("batch", "ctx"), None),
        P(("batch", "ctx"), None),
        P(("batch", "ctx")),
        P(("batch", "ctx")),
        P(("batch", "ctx"), None),
        P(("batch", "ctx")),
        P(("batch", "ctx")),
        P(("batch", "ctx"), None),
        P(("batch", "ctx")),
        P(("batch", "ctx"), None),
        P(("batch", "ctx")),
        P("batch", "ctx", None),
    )
    out_specs = (
        P("batch", "ctx", None),
        P("batch", "ctx", None),
        P(("batch", "ctx")),
        P(("batch", "ctx")),
        P(("batch", "ctx"), None),
        P(("batch", "ctx"), None),
        P(("batch", "ctx")),
        P(("batch", "ctx")),
        P(("batch", "ctx"), None),
        P(("batch", "ctx")),
        P(("batch", "ctx")),
        P(("batch", "ctx"), None),
        P(("batch", "ctx")),
        P(("batch", "ctx"), None),
        P(("batch", "ctx")),
    )
    n, cores = mesh.shape["ctx"], mesh.shape["batch"]

    def layer(*args):
        suits = n == HEADS * SS and cores == 2 and args[0].shape[1] == 128 and args[4].shape[0] == 16
        return fast(n, *args) if suits else local(*args)

    return jax.shard_map(layer, mesh=mesh, in_specs=in_specs, out_specs=out_specs, check_vma=False)
```
